32 devices in a mesh: dp: 16 (over z, y, x), tensor: 2 (over core).
Axes of the slice: x: 2, y: 2, z: 4, core: 2. Of those that a mesh axis runs over, the one named last changes fastest.
Arguments:
- latents: float32 [96, 16, 1024], P('dp'), may hold values from -6 to 6
- noise_field: float32 [96, 16, 1024], P('dp'), may hold values from -6 to 6
- image_tokens: int32 [96, 16], P('dp'), may hold values from 0 to 256, as said below
- timesteps: int32 [96, 16], P('dp'), may hold values from 0 to 999
- w_patch: float32 [2, 16, 384], replicated, may hold values from -0.3125 to 0.3125
- m_patch: float32 [2, 16, 384], replicated, may hold values from -3.5762787e-07 to 3.5762787e-07
- v_patch: float32 [2, 16, 384], replicated, may hold values from 1.3700372e-14 to 5.4801487e-14
- w_time: float32 [640, 384], replicated, may hold values from -0.375 to 0.375
- m_time: float32 [640, 384], replicated, may hold values from -3.5762787e-07 to 3.5762787e-07
- v_time: float32 [640, 384], replicated, may hold values from 1.3700372e-14 to 5.4801487e-14
- w_mod: float32 [384, 3072], P(None, 'tensor'), may hold values from -0.875 to 0.875
- m_mod: float32 [384, 3072], P(None, 'tensor'), may hold values from -3.5762787e-07 to 3.5762787e-07
- v_mod: float32 [384, 3072], P(None, 'tensor'), may hold values from 1.3700372e-14 to 5.4801487e-14
- w_qkv: float32 [2, 384, 1152], P(None, None, 'tensor'), may hold values from -0.3125 to 0.3125
- m_qkv: float32 [2, 384, 1152], P(None, None, 'tensor'), may hold values from -3.5762787e-07 to 3.5762787e-07
- v_qkv: float32 [2, 384, 1152], P(None, None, 'tensor'), may hold values from 1.3700372e-14 to 5.4801487e-14
- w_out: float32 [384, 384], P('tensor'), may hold values from -0.875 to 0.875
- m_out: float32 [384, 384], P('tensor'), may hold values from -3.5762787e-07 to 3.5762787e-07
- v_out: float32 [384, 384], P('tensor'), may hold values from 1.3700372e-14 to 5.4801487e-14
- w_up: float32 [384, 1536], P(None, 'tensor'), may hold values from -1.2247449 to 1.2247449, as said below
- m_up: float32 [384, 1536], P(None, 'tensor'), may hold values from -3.5762787e-07 to 3.5762787e-07
- v_up: float32 [384, 1536], P(None, 'tensor'), may hold values from 1.3700372e-14 to 5.4801487e-14
- w_down: float32 [1536, 384], P('tensor'), may hold values from -0.61237244 to 0.61237244, as said below
- m_down: float32 [1536, 384], P('tensor'), may hold values from -3.5762787e-07 to 3.5762787e-07
- v_down: float32 [1536, 384], P('tensor'), may hold values from 1.3700372e-14 to 5.4801487e-14
Outputs:
- loss_sum: float32 [], replicated
- count: float32 [], replicated
- grad_norm: float32 [], replicated
- first_patch: float32 [2, 16, 384], replicated
- second_patch: float32 [2, 16, 384], replicated
- weight_patch: float32 [2, 16, 384], replicated
- first_time: float32 [640, 384], replicated
- second_time: float32 [640, 384], replicated
- weight_time: float32 [640, 384], replicated
- first_mod: float32 [384, 3072], P(None, 'tensor')
- second_mod: float32 [384, 3072], P(None, 'tensor')
- weight_mod: float32 [384, 3072], P(None, 'tensor')
- first_qkv: float32 [2, 384, 1152], P(None, None, 'tensor')
- second_qkv: float32 [2, 384, 1152], P(None, None, 'tensor')
- weight_qkv: float32 [2, 384, 1152], P(None, None, 'tensor')
- first_out: float32 [384, 384], P('tensor')
- second_out: float32 [384, 384], P('tensor')
- weight_out: float32 [384, 384], P('tensor')
- first_up: float32 [384, 1536], P(None, 'tensor')
- second_up: float32 [384, 1536], P(None, 'tensor')
- weight_up: float32 [384, 1536], P(None, 'tensor')
- first_down: float32 [1536, 384], P('tensor')
- second_down: float32 [1536, 384], P('tensor')
- weight_down: float32 [1536, 384], P('tensor')
The draws below stay inside these ranges and needn't reach their ends.
Inputs may be any that keep to these rules, and one draw needn't show every extreme that they name: `image_tokens`: each entry is 0, 64, 144 or 256; the nonzero entries of a row come first and add up to at most 1024. `w_up`: real-valued entries of mean zero. `w_down`: real-valued entries of mean zero.
All inputs are finite; a program needn't handle non-finite values.
Results may differ from the reference program's by a relative error of at most 0.0063.
Values may be sent and summed in bfloat16 or wider, within the bound.
No kernel may reach another device: no remote copies, remote signals or barrier semaphores. Data moves between devices by JAX's collectives and lax.ppermute only.
A program may use at most 448 MiB of HBM per device.

```python
import math
import jax
import jax.numpy as jnp
from jax import lax

D = 384
HEADS = 6
HEAD_DIM = 64
FF = 1536
FREQ = 256
CHANNELS = 16
LEN = 1024
STEP = 10
SLOTS = 16
ROWS = 96
PARAMS = 3649536
N_TENSOR = 2


def draw_image_tokens(key, part):
    row_ids = jnp.arange(ROWS, dtype=jnp.int32)
    capacity = 256 + (LEN - 256) * row_ids // max(ROWS - 1, 1)
    picks = jax.random.randint(key, (ROWS, SLOTS), 0, 3)
    options = jnp.array([64, 144, 256], dtype=jnp.int32)
    wanted = options[picks]
    wanted = wanted.at[0, 0].set(256)

    def place_one(remaining, wanted_size):
        fitted = jnp.where(wanted_size <= remaining, wanted_size, jnp.where(remaining >= 64, 64, 0))
        return (remaining - fitted, fitted)
    _, chosen = lax.scan(place_one, capacity, wanted.T)
    return chosen.T.astype(jnp.int32)


def rising(count_units, top):
    steps_up = jnp.arange(count_units, dtype=jnp.float32) / max(count_units - 1, 1)
    return 1.0 + (top - 1.0) * steps_up


def draw_w_up(key, part):
    key = jax.random.fold_in(key, 11)
    ramp = rising(FF, 3.0)
    values = jax.random.truncated_normal(key, -6.0, 6.0, (D, FF), jnp.float32)
    return values * D ** (-0.5) * ramp[None, :]


def draw_w_down(key, part):
    key = jax.random.fold_in(key, 13)
    ramp = rising(FF, 3.0)
    values = jax.random.truncated_normal(key, -6.0, 6.0, (FF, D), jnp.float32)
    return values * FF ** (-0.5) * ramp[:, None]


def with_ends(values, stream_key, smallest, high):
    longest = values.shape.index(max(values.shape))
    spots = []
    for shift in (0, 1):
        where = [jax.random.randint(jax.random.fold_in(stream_key, axis), (), 0, length) for axis, length in enumerate(values.shape)]
        where[longest] = (where[longest] + shift) % values.shape[longest]
        spots.append(tuple(where))
    return values.at[spots[0]].set(smallest).at[spots[1]].set(high)


def block_levels(stream_key, shape, pieces, least, high):
    level, own = 1.0, jax.random.fold_in(stream_key, 6)
    for dim, blocks in pieces:
        heights = jnp.exp(jax.random.uniform(jax.random.fold_in(own, dim), (blocks,), jnp.float32, least / len(pieces), high / len(pieces)))
        level = level * jnp.repeat(heights, shape[dim] // blocks).reshape([-1 if axis == dim else 1 for axis in range(len(shape))])
    return level


def scatter_about(stream_key, extent, deviation, limit, shards=(), kind=jnp.bfloat16):
    level = block_levels(stream_key, extent, shards, -0.22, 0.18) if shards else 1.0
    values = jax.random.normal(stream_key, extent, jnp.float32) * deviation * level
    return jnp.minimum(jnp.maximum(values, -limit), limit).astype(kind)


def setup_inputs(seed: int = 0) -> dict:
    key_of = jax.random.split(jax.random.key(seed), 26)
    latents = scatter_about(key_of[0], (ROWS, CHANNELS, LEN), 1.0, 6.0, ((0, 16),), jnp.float32)
    noise_field = scatter_about(key_of[1], (ROWS, CHANNELS, LEN), 1.0, 6.0, ((0, 16),), jnp.float32)
    image_tokens = draw_image_tokens(jax.random.fold_in(key_of[25], 71), 0)
    timesteps = with_ends(jax.random.randint(key_of[3], (ROWS, SLOTS), 0, 1000), jax.random.fold_in(key_of[3], 1), 0, 999).astype(jnp.int32)
    w_patch = scatter_about(key_of[4], (2, CHANNELS, D), D ** -0.5, 0.3125, (), jnp.float32)
    m_patch = scatter_about(key_of[5], (2, CHANNELS, D), (0.00011 * PARAMS ** -0.5), 3.5762786865234375e-07, (), jnp.float32)
    v_patch = jnp.clip(jnp.exp(jax.random.uniform(key_of[6], (2, CHANNELS, D), jnp.float32, math.log(1.370037167481436e-14), math.log(5.480148669925744e-14))), 1.370037167481436e-14, 5.480148669925744e-14)
    w_time = scatter_about(key_of[7], (FREQ + D, D), FREQ ** -0.5, 0.375, (), jnp.float32)
    m_time = scatter_about(key_of[8], (FREQ + D, D), (0.00011 * PARAMS ** -0.5), 3.5762786865234375e-07, (), jnp.float32)
    v_time = jnp.clip(jnp.exp(jax.random.uniform(key_of[9], (FREQ + D, D), jnp.float32, math.log(1.370037167481436e-14), math.log(5.480148669925744e-14))), 1.370037167481436e-14, 5.480148669925744e-14)
    w_mod = scatter_about(key_of[10], (D, 8 * D), (D // 8) ** -0.5, 0.875, ((1, 2),), jnp.float32)
    m_mod = scatter_about(key_of[11], (D, 8 * D), (0.00011 * PARAMS ** -0.5), 3.5762786865234375e-07, ((1, 2),), jnp.float32)
    v_mod = jnp.clip(jnp.exp(math.log(5.480148669925744e-14) - 1.3862944 * jax.random.uniform(key_of[12], (D, 8 * D), jnp.float32) ** block_levels(key_of[12], (D, 8 * D), ((1, 2),), -0.2, 0.2)), 1.370037167481436e-14, 5.480148669925744e-14)
    w_qkv = scatter_about(key_of[13], (2, D, 3 * D), D ** -0.5, 0.3125, ((2, 2),), jnp.float32)
    m_qkv = scatter_about(key_of[14], (2, D, 3 * D), (0.00011 * PARAMS ** -0.5), 3.5762786865234375e-07, ((2, 2),), jnp.float32)
    v_qkv = jnp.clip(jnp.exp(math.log(5.480148669925744e-14) - 1.3862944 * jax.random.uniform(key_of[15], (2, D, 3 * D), jnp.float32) ** block_levels(key_of[15], (2, D, 3 * D), ((2, 2),), -0.2, 0.2)), 1.370037167481436e-14, 5.480148669925744e-14)
    w_out = scatter_about(key_of[16], (D, D), (D // 8) ** -0.5, 0.875, ((0, 2),), jnp.float32)
    m_out = scatter_about(key_of[17], (D, D), (0.00011 * PARAMS ** -0.5), 3.5762786865234375e-07, ((0, 2),), jnp.float32)
    v_out = jnp.clip(jnp.exp(math.log(5.480148669925744e-14) - 1.3862944 * jax.random.uniform(key_of[18], (D, D), jnp.float32) ** block_levels(key_of[18], (D, D), ((0, 2),), -0.2, 0.2)), 1.370037167481436e-14, 5.480148669925744e-14)
    w_up = draw_w_up(jax.random.fold_in(key_of[25], 71), 0)
    m_up = scatter_about(key_of[20], (D, FF), (0.00011 * PARAMS ** -0.5), 3.5762786865234375e-07, ((1, 2),), jnp.float32)
    v_up = jnp.clip(jnp.exp(math.log(5.480148669925744e-14) - 1.3862944 * jax.random.uniform(key_of[21], (D, FF), jnp.float32) ** block_levels(key_of[21], (D, FF), ((1, 2),), -0.2, 0.2)), 1.370037167481436e-14, 5.480148669925744e-14)
    w_down = draw_w_down(jax.random.fold_in(key_of[25], 71), 0)
    m_down = scatter_about(key_of[23], (FF, D), (0.00011 * PARAMS ** -0.5), 3.5762786865234375e-07, ((0, 2),), jnp.float32)
    v_down = jnp.clip(jnp.exp(math.log(5.480148669925744e-14) - 1.3862944 * jax.random.uniform(key_of[24], (FF, D), jnp.float32) ** block_levels(key_of[24], (FF, D), ((0, 2),), -0.2, 0.2)), 1.370037167481436e-14, 5.480148669925744e-14)
    return {"latents": latents, "noise_field": noise_field, "image_tokens": image_tokens, "timesteps": timesteps, "w_patch": w_patch, "m_patch": m_patch, "v_patch": v_patch, "w_time": w_time, "m_time": m_time, "v_time": v_time, "w_mod": w_mod, "m_mod": m_mod, "v_mod": v_mod, "w_qkv": w_qkv, "m_qkv": m_qkv, "v_qkv": v_qkv, "w_out": w_out, "m_out": m_out, "v_out": v_out, "w_up": w_up, "m_up": m_up, "v_up": v_up, "w_down": w_down, "m_down": m_down, "v_down": v_down}


@jax.custom_vjp
def low(v):
    return lax.optimization_barrier(v.astype(jnp.bfloat16)).astype(jnp.float32)

@jax.custom_vjp
def low_back(v):
    return v

def low_keep(v):
    return (low(v), None)

def low_pass(kept, grad):
    return (grad,)

def back_keep(v):
    return (v, None)

def back_low(kept, grad):
    return (low(grad),)
low.defvjp(low_keep, low_pass)
low_back.defvjp(back_keep, back_low)
PRECISE_MODE = lax.Precision.HIGHEST
NORM_EPS = 1e-06
CLIP_LIMIT = 0.001
LEARN_RATE = 0.03
BETA_FIRST = 0.9
BETA_SECOND = 0.95
ADAM_EPS = 1e-08
WEIGHT_DECAY = 0.1
MASKED = -1e+30

def precise(left, right):
    return jnp.dot(left, right, precision=PRECISE_MODE)

def normalize(values):
    centre = values - lax.optimization_barrier(jnp.mean(values, -1, keepdims=True))
    return centre * lax.rsqrt(lax.optimization_barrier(jnp.mean(centre * centre, -1, keepdims=True)) + NORM_EPS)

def packing(token_counts):
    ends = jnp.cumsum(token_counts, axis=1).astype(jnp.int32)
    starts = ends - token_counts
    position = jnp.arange(LEN, dtype=jnp.int32)
    segment = lax.optimization_barrier(jnp.sum((position[None, :, None] >= ends[:, None, :]).astype(jnp.int32), axis=2))
    validity = position[None, :] < ends[:, -1:]
    member = (segment[:, :, None] == jnp.arange(SLOTS, dtype=jnp.int32)[None, None, :]).astype(jnp.int32)
    image_side = (token_counts == 64).astype(jnp.int32) * 8 + (token_counts == 144).astype(jnp.int32) * 12 + (token_counts == 256).astype(jnp.int32) * 16
    offset = position[None, :] - lax.optimization_barrier(jnp.sum(member * starts[:, None, :], axis=2))
    side_safe = jnp.maximum(lax.optimization_barrier(jnp.sum(member * image_side[:, None, :], axis=2)), 1)
    return (segment, validity, member, offset // side_safe, offset % side_safe)

def position_table(row_pos, col_pos, width):
    quarter = width // 4
    omega = jnp.exp(-math.log(10000.0) * jnp.arange(quarter, dtype=jnp.float32) / quarter)
    row_angle = row_pos.astype(jnp.float32)[..., None] * omega
    col_angle = col_pos.astype(jnp.float32)[..., None] * omega
    return jnp.concatenate([jnp.sin(row_angle), jnp.cos(row_angle), jnp.sin(col_angle), jnp.cos(col_angle)], -1)

def signal_levels(steps):
    index = jnp.arange(1000, dtype=jnp.int32)
    betas = 0.0001 + 0.0199 * index.astype(jnp.float32) / 999.0
    logs = jnp.log(1.0 - betas)
    return jnp.exp(lax.optimization_barrier(jnp.sum(jnp.where(index <= steps[..., None], logs, 0.0), -1)))

def time_features(steps):
    half = FREQ // 2
    rates = jnp.exp(-math.log(10000.0) * jnp.arange(half, dtype=jnp.float32) / half)
    angle = steps.astype(jnp.float32)[..., None] * rates
    return jnp.concatenate([jnp.cos(angle), jnp.sin(angle)], -1)

def row_term(lowered, inputs):
    patch_low, qkv_low, out_low, up_low, down_low = lowered
    slot_mod, slot_shift, latent_row, noise_row, member_row, segment_row, valid_row, row_pos, col_pos, keep_slot, fade_slot = inputs
    member_f = member_row.astype(jnp.float32)
    valid_f = valid_row.astype(jnp.float32)
    token_mod = precise(member_f, slot_mod)
    shift1, scale1, gate1, shift2, scale2, gate2, shift3, scale3 = [token_mod[:, i * D:(i + 1) * D] for i in range(8)]
    token_shift = precise(member_f, slot_shift)
    noisy = precise(member_f, keep_slot)[:, None] * latent_row.T + precise(member_f, fade_slot)[:, None] * noise_row.T
    stream_in = low_back(precise(low(noisy), patch_low[0])) + position_table(row_pos, col_pos, D) * valid_f[:, None]
    attn_src = normalize(stream_in) * (1.0 + scale1) + shift1
    same = segment_row[:, None] == segment_row[None, :]
    group_heads = HEADS // N_TENSOR
    group_cols = 3 * D // N_TENSOR
    group_rows = D // N_TENSOR
    attended = jnp.zeros((LEN, D), jnp.float32)
    for group in range(N_TENSOR):
        attn_in = low(low_back(attn_src))
        cols = slice(group * group_cols, (group + 1) * group_cols)
        projected = low(low_back(precise(attn_in, qkv_low[:, cols]) + token_shift[:, cols]))
        projected = projected.reshape(LEN, group_heads, 3, HEAD_DIM)
        query, key_part, value = (projected[:, :, 0], projected[:, :, 1], projected[:, :, 2])
        scores = low_back(jnp.einsum('qhd,khd->hqk', query, key_part, precision=PRECISE_MODE) * HEAD_DIM ** (-0.5))
        scores = jnp.where(same[None], scores, MASKED)
        probs = jax.nn.softmax(scores, axis=-1)
        mixed = jnp.einsum('hqk,khd->qhd', low(probs), value, precision=PRECISE_MODE)
        mixed = low(low_back(mixed)).reshape(LEN, group_heads * HEAD_DIM)
        attended = attended + low(precise(mixed, out_low[group * group_rows:(group + 1) * group_rows]))
    attended = low_back(attended)
    stream_mid = stream_in + gate1 * attended
    mlp_src = normalize(stream_mid) * (1.0 + scale2) + shift2
    group_ff = FF // N_TENSOR
    mlp_out = jnp.zeros((LEN, D), jnp.float32)
    for group in range(N_TENSOR):
        mlp_in = low(low_back(mlp_src))
        up_proj = low_back(precise(mlp_in, up_low[:, group * group_ff:(group + 1) * group_ff]))
        activated = low(jax.nn.gelu(up_proj, approximate=True))
        mlp_out = mlp_out + low(precise(activated, down_low[group * group_ff:(group + 1) * group_ff]))
    mlp_out = low_back(mlp_out)
    stream_out = stream_mid + gate2 * mlp_out
    final_in = normalize(stream_out) * (1.0 + scale3) + shift3
    predicted = low_back(precise(low(final_in), patch_low[1].T))
    error = predicted - noise_row.T
    return jnp.sum(valid_f[:, None] * error * error)

def adam(weight, first, second, grad, factor):
    clipped = grad * factor
    first = BETA_FIRST * first + (1.0 - BETA_FIRST) * clipped
    second = BETA_SECOND * second + (1.0 - BETA_SECOND) * clipped * clipped
    fixed_first = first / (1.0 - BETA_FIRST ** STEP)
    fixed_second = second / (1.0 - BETA_SECOND ** STEP)
    weight = weight - LEARN_RATE * (fixed_first / (jnp.sqrt(fixed_second) + ADAM_EPS) + WEIGHT_DECAY * weight)
    return (first, second, weight)

def reference(latents, noise_field, image_tokens, timesteps, w_patch, m_patch, v_patch, w_time, m_time, v_time, w_mod, m_mod, v_mod, w_qkv, m_qkv, v_qkv, w_out, m_out, v_out, w_up, m_up, v_up, w_down, m_down, v_down):
    segment, validity, member, row_pos, col_pos = packing(image_tokens)
    level = signal_levels(timesteps)
    count = CHANNELS * jnp.sum(validity.astype(jnp.float32))
    features = time_features(timesteps).reshape(ROWS * SLOTS, FREQ)
    row_inputs = (latents, noise_field, member, segment, validity, row_pos, col_pos, jnp.sqrt(level), jnp.sqrt(1.0 - level))

    def total(params):
        p_patch, p_time, p_mod, p_qkv, p_out, p_up, p_down = params
        time_hidden = jax.nn.silu(precise(features, p_time[:FREQ]))
        cond = precise(time_hidden, p_time[FREQ:])
        modulation = precise(jax.nn.silu(cond), p_mod).reshape(ROWS, SLOTS, 8 * D)
        shift_slot = precise(cond, p_qkv[1]).reshape(ROWS, SLOTS, 3 * D)
        lowered = (low(p_patch), low(p_qkv[0]), low(p_out), low(p_up), low(p_down))

        def row_fn(inputs):
            return row_term(lowered, inputs)
        terms = lax.map(jax.checkpoint(row_fn), (modulation, shift_slot) + row_inputs)
        summed = jnp.sum(terms)
        return (summed / count, summed)
    weights = (w_patch, w_time, w_mod, w_qkv, w_out, w_up, w_down)
    _, back, loss_sum = jax.vjp(total, weights, has_aux=True)
    grads = back(jnp.ones((), jnp.float32))[0]
    grad_norm = jnp.sqrt(sum((jnp.sum(grad * grad) for grad in grads)))
    factor = jnp.minimum(1.0, CLIP_LIMIT / grad_norm)
    firsts = (m_patch, m_time, m_mod, m_qkv, m_out, m_up, m_down)
    seconds = (v_patch, v_time, v_mod, v_qkv, v_out, v_up, v_down)
    result = [loss_sum, count, grad_norm]
    for weight, first, second, grad in zip(weights, firsts, seconds, grads):
        result.extend(adam(weight, first, second, grad, factor))
    return tuple(result)
```

```python
from functools import partial
import math

import jax
import jax.numpy as jnp
import numpy as np
from jax import lax
from jax.experimental import pallas as pl
from jax.experimental.pallas import tpu as pltpu
from jax.sharding import PartitionSpec as P

HEAD_DIM = 64
STEP = 10
PRECISE_MODE = lax.Precision.HIGHEST
NORM_EPS = 1e-06
CLIP_LIMIT = 0.001
LEARN_RATE = 0.03
BETA_FIRST = 0.9
BETA_SECOND = 0.95
ADAM_EPS = 1e-08
WEIGHT_DECAY = 0.1
SIZES = (64, 144, 256)
TILE = 256
SLOT_LANES = 128
GELU_A = math.sqrt(2.0 / math.pi)
GELU_B = 0.044715
VMEM_LIMIT = 60 * 1024 * 1024
F32 = jnp.float32
BF16 = jnp.bfloat16


def precise(left, right):
    return jnp.dot(left, right, precision=PRECISE_MODE)


def dot(left, right):
    return lax.dot_general(left, right, (((1,), (0,)), ((), ())), preferred_element_type=F32)


def dot_nt(left, right):
    return lax.dot_general(left, right, (((1,), (1,)), ((), ())), preferred_element_type=F32)


def normalize(values):
    centre = values - jnp.mean(values, -1, keepdims=True)
    inverse = lax.rsqrt(jnp.mean(centre * centre, -1, keepdims=True) + NORM_EPS)
    return (centre * inverse, inverse)


def norm_back(grad, normed, inverse):
    return inverse * (
        grad
        - jnp.mean(grad, -1, keepdims=True)
        - normed * jnp.mean(grad * normed, -1, keepdims=True)
    )


def position_rows(width):
    quarter = width // 4
    omega = np.exp(-math.log(10000.0) * np.arange(quarter) / quarter)
    parts = []
    for size in SIZES:
        side = math.isqrt(size)
        offset = np.arange(size)
        row_angle = (offset // side)[:, None] * omega
        col_angle = (offset % side)[:, None] * omega
        parts.append(
            np.concatenate(
                [np.sin(row_angle), np.cos(row_angle), np.sin(col_angle), np.cos(col_angle)], -1
            )
        )
    return np.concatenate(parts, 0).astype(np.float32)


def for_sizes(count, body):
    offset = 0
    for size in SIZES:
        pl.when(count == size)(partial(body, size, offset))
        offset += size


def rows_at(start, size, step):
    return pl.ds(pl.multiple_of(start, step), size)


def fill_member(member, dst, size, index):
    lane = lax.broadcasted_iota(jnp.int32, (size, 2 * SLOT_LANES), 1)
    hot = (lane == index) | (lane == index + SLOT_LANES)
    member[rows_at(dst, size, 16), :] = hot.astype(F32).astype(BF16)


def head_mask(size, half):
    lane = lax.broadcasted_iota(jnp.int32, (size, 2 * HEAD_DIM), 1)
    return (lane >= HEAD_DIM) if half else (lane < HEAD_DIM)


def forward_kernel(
    tab, xin, places, modcat, shiftcat, w_in, w_fin, wqkv, wout, wup, wdn,
    proj, mixed, gmixed, gmid, stream, xtok, lse, gup, gdn, gout, gfin, sg, loss,
    xrow, member, deriv, active,
):
    width = stream.shape[1]
    low, high, tokens, tiles = (tab[3, j] for j in range(4))
    heads = width // HEAD_DIM
    hidden = wup.shape[1]
    for r in range(xin.shape[0]):
        turned = xin[r].astype(F32).T
        xrow[r * turned.shape[0] : (r + 1) * turned.shape[0], :] = turned.astype(BF16)

    def place_image(i, carry):
        src, dst = tab[1, i], tab[2, i]

        def body(size, offset):
            xtok[rows_at(dst, size, 16), :] = xrow[rows_at(src, size, 16), :]
            stream[rows_at(dst, size, 16), :] = places[offset : offset + size, :]
            fill_member(member, dst, size, i)

        for_sizes(tab[0, i], body)
        return carry

    lax.fori_loop(low, high, place_image, 0)
    tail = rows_at(tokens, TILE, 16)
    for ref in (xtok, stream, member, mixed):
        ref[tail, :] = jnp.zeros((TILE, ref.shape[1]), ref.dtype)
    for ref in (gup, gdn, gout, gfin, sg, loss):
        ref[...] = jnp.zeros(ref.shape, ref.dtype)

    def spread(hot, block):
        return dot(hot, modcat[block // 4, :, block % 4 * width : (block % 4 + 1) * width])

    def project_tile(t, carry):
        r = rows_at(t * TILE, TILE, TILE)
        entering = dot(xtok[r, :], w_in[...]) + stream[r, :]
        stream[r, :] = entering
        hot = member[r, :]
        normed, _ = normalize(entering)
        attn_in = (normed * (1.0 + spread(hot, 1)) + spread(hot, 0)).astype(BF16)
        proj[r, :] = (dot(attn_in, wqkv[...]) + dot(hot, shiftcat[...])).astype(BF16)
        return carry

    lax.fori_loop(0, tiles, project_tile, 0)

    def attend_image(i, carry):
        dst = tab[2, i]

        def body(size, offset):
            r = rows_at(dst, size, 16)
            value_t = proj[r, 2 * width : 3 * width].T
            pieces = []
            for h in range(heads):
                pair = slice(h // 2 * 128, h // 2 * 128 + 128)
                query = proj[r, pair]
                query = jnp.where(head_mask(size, h % 2), query, jnp.zeros_like(query))
                key = proj[r, width + pair.start : width + pair.stop]
                scores = dot_nt(key, query)
                top = jnp.max(scores, 0, keepdims=True)
                weights = jnp.exp((scores - top) * HEAD_DIM ** (-0.5))
                total = jnp.sum(weights, 0, keepdims=True)
                out = dot(value_t[h * HEAD_DIM : (h + 1) * HEAD_DIM, :], weights.astype(BF16))
                pieces.append(out / total)
                lse[i, h : h + 1, :size] = top * HEAD_DIM ** (-0.5) + jnp.log(total)
            mixed[r, :] = jnp.concatenate(pieces, 0).T.astype(BF16)

        for_sizes(tab[0, i], body)
        return carry

    lax.fori_loop(low, high, attend_image, 0)

    def token_tile(t, carry):
        r = rows_at(t * TILE, TILE, TILE)
        hot = member[r, :]
        hot_t = member[r, :SLOT_LANES].astype(F32).T.astype(BF16)

        def collect(block, value):
            sg[block * SLOT_LANES : (block + 1) * SLOT_LANES, :] += dot(hot_t, value.astype(BF16))

        mixed_tile = mixed[r, :]
        attended = dot(mixed_tile, wout[...])
        gate1 = spread(hot, 2)
        mid = stream[r, :] + gate1 * attended
        normed2, inverse2 = normalize(mid)
        scale2 = spread(hot, 4)
        mlp_in = (normed2 * (1.0 + scale2) + spread(hot, 3)).astype(BF16)
        mlp_out = jnp.zeros((TILE, width), F32)
        for j in range(0, hidden, width):
            up = dot(mlp_in, wup[:, j : j + width])
            square = up * up
            bent = jnp.tanh(up * (GELU_A + (GELU_A * GELU_B) * square))
            share = 0.5 + 0.5 * bent
            act = (up * share).astype(BF16)
            active[:, j : j + width] = act
            deriv[:, j : j + width] = share + up * (share * (1.0 - share)) * (
                2.0 * GELU_A + (6.0 * GELU_A * GELU_B) * square
            )
            mlp_out = mlp_out + dot(act, wdn[j : j + width, :])
        gate2 = spread(hot, 5)
        leaving = mid + gate2 * mlp_out
        normed3, inverse3 = normalize(leaving)
        scale3 = spread(hot, 7)
        final_in = (normed3 * (1.0 + scale3) + spread(hot, 6)).astype(BF16)
        predicted = dot_nt(final_in, w_fin[...])
        channels = w_fin.shape[0] // 2
        lane = lax.broadcasted_iota(jnp.int32, predicted.shape, 1)
        row = lax.broadcasted_iota(jnp.int32, predicted.shape, 0) + t * TILE
        keep = (lane >= channels) & (row < tokens)
        error = jnp.where(keep, predicted - xtok[r, :].astype(F32), 0.0)
        loss[...] += jnp.sum(error * error, 0, keepdims=True)
        grad_pred = (2.0 * error).astype(BF16)
        gfin[...] += dot(grad_pred.T, final_in)
        grad_final = dot(grad_pred, w_fin[...])
        collect(6, grad_final)
        collect(7, grad_final * normed3)
        grad_out = norm_back(grad_final * (1.0 + scale3), normed3, inverse3)
        collect(5, grad_out * mlp_out)
        grad_mlp = (grad_out * gate2).astype(BF16)
        grad_mlp_t = grad_mlp.T
        mlp_in_t = mlp_in.T
        grad_mlp_in = jnp.zeros((TILE, width), F32)
        for j in range(0, hidden, width):
            gdn[:, j : j + width] += dot(grad_mlp_t, active[:, j : j + width])
            grad_act = dot_nt(grad_mlp, wdn[j : j + width, :])
            grad_up = (grad_act * deriv[:, j : j + width]).astype(BF16)
            gup[:, j : j + width] += dot(mlp_in_t, grad_up)
            grad_mlp_in = grad_mlp_in + dot_nt(grad_up, wup[:, j : j + width])
        collect(3, grad_mlp_in)
        collect(4, grad_mlp_in * normed2)
        grad_mid = grad_out + norm_back(grad_mlp_in * (1.0 + scale2), normed2, inverse2)
        gmid[r, :] = grad_mid
        collect(2, grad_mid * attended)
        grad_attended = (grad_mid * gate1).astype(BF16)
        gout[...] += dot(mixed_tile.T, grad_attended)
        gmixed[r, :] = dot_nt(grad_attended, wout[...]).astype(BF16)
        return carry

    lax.fori_loop(0, tiles, token_tile, 0)


def backward_kernel(
    tab, modcat, wqkv, proj, mixed, gmixed, gmid, stream, xtok, lse, sg_in,
    gqkv, gshift, gemb, sg,
    gproj, member,
):
    width = stream.shape[1]
    low, high, tokens, tiles = (tab[3, j] for j in range(4))
    heads = width // HEAD_DIM
    sg[...] = sg_in[...]
    for ref in (gqkv, gshift, gemb):
        ref[...] = jnp.zeros(ref.shape, ref.dtype)
    tail = rows_at(tokens, TILE, 16)
    for ref in (gproj, member):
        ref[tail, :] = jnp.zeros((TILE, ref.shape[1]), ref.dtype)
    head_of = lax.broadcasted_iota(jnp.int32, (8, width), 1) // HEAD_DIM
    head_rows = (head_of == lax.broadcasted_iota(jnp.int32, (8, width), 0)).astype(F32).astype(BF16)

    def attend_image(i, carry):
        dst = tab[2, i]

        def body(size, offset):
            r = rows_at(dst, size, 16)
            fill_member(member, dst, size, i)
            product = gmixed[r, :].astype(F32) * mixed[r, :].astype(F32)
            coarse = product.astype(BF16)
            fine = (product - coarse.astype(F32)).astype(BF16)
            inner = dot_nt(head_rows, coarse) + dot_nt(head_rows, fine)
            key_t = proj[r, width : 2 * width].T
            query_pieces = []
            for p in range(heads // 2):
                pair = slice(p * 128, p * 128 + 128)
                query = proj[r, pair]
                key = proj[r, width + pair.start : width + pair.stop]
                value = proj[r, 2 * width + pair.start : 2 * width + pair.stop]
                grad = gmixed[r, pair]
                grad_key = jnp.zeros((size, 128), F32)
                grad_value = jnp.zeros((size, 128), F32)
                for half in range(2):
                    h = 2 * p + half
                    mask = head_mask(size, half)
                    query_h = jnp.where(mask, query, jnp.zeros_like(query))
                    grad_h = jnp.where(mask, grad, jnp.zeros_like(grad))
                    scores = dot_nt(key, query_h)
                    probs = jnp.exp(scores * HEAD_DIM ** (-0.5) - lse[i, h : h + 1, :size])
                    grad_probs = dot_nt(value, grad_h)
                    grad_scores = (probs * (grad_probs - inner[h : h + 1, :])).astype(BF16)
                    grad_value = grad_value + dot(probs.astype(BF16), grad_h)
                    grad_key = grad_key + dot(grad_scores, query_h)
                    query_pieces.append(dot(key_t[h * HEAD_DIM : (h + 1) * HEAD_DIM, :], grad_scores))
                gproj[r, width + pair.start : width + pair.stop] = (
                    grad_key * HEAD_DIM ** (-0.5)
                ).astype(BF16)
                gproj[r, 2 * width + pair.start : 2 * width + pair.stop] = grad_value.astype(BF16)
            grad_query = jnp.concatenate(query_pieces, 0) * HEAD_DIM ** (-0.5)
            gproj[r, :width] = grad_query.T.astype(BF16)

        for_sizes(tab[0, i], body)
        return carry

    lax.fori_loop(low, high, attend_image, 0)

    def token_tile(t, carry):
        r = rows_at(t * TILE, TILE, TILE)
        hot = member[r, :]
        hot_t = member[r, :SLOT_LANES].astype(F32).T.astype(BF16)

        def spread(block):
            return dot(hot, modcat[block // 4, :, block % 4 * width : (block % 4 + 1) * width])

        def collect(block, value):
            sg[block * SLOT_LANES : (block + 1) * SLOT_LANES, :] += dot(hot_t, value.astype(BF16))

        normed, inverse = normalize(stream[r, :])
        scale1 = spread(1)
        attn_in = (normed * (1.0 + scale1) + spread(0)).astype(BF16)
        grad_proj = gproj[r, :]
        gqkv[...] += dot(attn_in.T, grad_proj)
        gshift[...] += dot(hot_t, grad_proj)
        grad_attn_in = dot_nt(grad_proj, wqkv[...])
        collect(0, grad_attn_in)
        collect(1, grad_attn_in * normed)
        grad_in = gmid[r, :] + norm_back(grad_attn_in * (1.0 + scale1), normed, inverse)
        gemb[...] += dot(xtok[r, :].T, grad_in.astype(BF16))
        return carry

    lax.fori_loop(0, tiles, token_tile, 0)


def call_forward(tab, xin, modcat, shiftcat, w_in, w_fin, wqkv, wout, wup, wdn, room):
    width, hidden = wup.shape
    here, channels2, length = xin.shape
    slots = SLOT_LANES
    vmem = pl.BlockSpec(memory_space=pltpu.VMEM)
    shape = jax.ShapeDtypeStruct
    outs = (
        shape((room, 3 * width), BF16),
        shape((room, width), BF16),
        shape((room, width), BF16),
        shape((room, width), F32),
        shape((room, width), F32),
        shape((room, channels2), BF16),
        shape((slots, 8, max(SIZES)), F32),
        shape((width, hidden), F32),
        shape((width, hidden), F32),
        shape((width, width), F32),
        shape((channels2, width), F32),
        shape((8 * slots, width), F32),
        shape((1, channels2), F32),
    )
    return pl.pallas_call(
        forward_kernel,
        out_shape=outs,
        in_specs=[pl.BlockSpec(memory_space=pltpu.SMEM)] + [vmem] * 10,
        out_specs=[vmem] * len(outs),
        scratch_shapes=[
            pltpu.VMEM((here * length, channels2), BF16),
            pltpu.VMEM((room, 2 * slots), BF16),
            pltpu.VMEM((TILE, hidden), F32),
            pltpu.VMEM((TILE, hidden), BF16),
        ],
        compiler_params=pltpu.CompilerParams(vmem_limit_bytes=VMEM_LIMIT),
        name="forward",
    )(tab, xin, jnp.asarray(position_rows(width)), modcat, shiftcat, w_in, w_fin, wqkv, wout, wup, wdn)


def call_backward(tab, modcat, wqkv, saved, sg):
    proj, mixed, gmixed, gmid, stream, xtok, lse = saved
    room, width = stream.shape
    slots = SLOT_LANES
    vmem = pl.BlockSpec(memory_space=pltpu.VMEM)
    shape = jax.ShapeDtypeStruct
    outs = (
        shape((width, 3 * width), F32),
        shape((slots, 3 * width), F32),
        shape((xtok.shape[1], width), F32),
        shape(sg.shape, F32),
    )
    return pl.pallas_call(
        backward_kernel,
        out_shape=outs,
        in_specs=[pl.BlockSpec(memory_space=pltpu.SMEM)] + [vmem] * 10,
        out_specs=[vmem] * len(outs),
        scratch_shapes=[
            pltpu.VMEM((room, 3 * width), BF16),
            pltpu.VMEM((room, 2 * slots), BF16),
        ],
        compiler_params=pltpu.CompilerParams(vmem_limit_bytes=VMEM_LIMIT),
        name="backward",
    )(tab, modcat, wqkv, proj, mixed, gmixed, gmid, stream, xtok, lse, sg)


def signal_levels(steps):
    index = jnp.arange(1000, dtype=jnp.int32)
    betas = 0.0001 + 0.0199 * index.astype(F32) / 999.0
    logs = jnp.log(1.0 - betas)
    return jnp.exp(jnp.sum(jnp.where(index <= steps[..., None], logs, 0.0), -1))


def time_features(steps, freqs):
    half = freqs // 2
    rates = jnp.exp(-math.log(10000.0) * jnp.arange(half, dtype=F32) / half)
    angle = steps.astype(F32)[..., None] * rates
    return jnp.concatenate([jnp.cos(angle), jnp.sin(angle)], -1)


def running_sum(values):
    size = values.shape[-1]
    before = np.arange(size)[:, None] > np.arange(size)[None, :]
    return jnp.sum(jnp.where(before, values[..., None, :], 0), -1)


def image_table(counts, core, length):
    rows_here, slots = counts.shape
    row_start = running_sum(counts) + length * jnp.arange(rows_here, dtype=jnp.int32)[:, None]
    flat = counts.reshape(-1)
    start = running_sum(flat)
    total = jnp.sum(flat)
    index = jnp.arange(flat.shape[0], dtype=jnp.int32)
    first_half = jnp.sum((2 * start + flat <= total).astype(jnp.int32))
    low = jnp.where(core == 0, 0, first_half)
    high = jnp.where(core == 0, first_half, flat.shape[0])
    base = jnp.sum(jnp.where(index < low, flat, 0))
    tokens = jnp.sum(jnp.where((index >= low) & (index < high), flat, 0))
    tiles = (tokens + TILE - 1) // TILE
    facts = jnp.stack([low, high, tokens, tiles]).astype(jnp.int32)
    pad = lambda v: jnp.pad(v.astype(jnp.int32), (0, 128 - v.shape[0]))
    return jnp.stack([pad(flat), pad(row_start.reshape(-1)), pad(start - base), pad(facts)])


def split_bits(values):
    coarse = values.astype(BF16)
    return coarse, (values - coarse.astype(F32)).astype(BF16)


def stacked_bits(values):
    coarse, fine = split_bits(values)
    room = ((0, SLOT_LANES - values.shape[0]), (0, 0))
    return jnp.concatenate([jnp.pad(coarse, room), jnp.pad(fine, room)], 0)


def swap(value):
    return lax.ppermute(value, "tensor", [(0, 1), (1, 0)])


def stage(size, bit):
    return [(i, i ^ (1 << bit)) for i in range(size)]


def reduce_scatter(values, narrow):
    size = values.shape[0]
    place = lax.axis_index("dp")
    bit = 0
    shape = values.shape[1:]
    while size >> bit > 1:
        mine = (place >> bit) & 1
        paired = values.reshape(values.shape[0] // 2, 2, *shape)
        keep = lax.dynamic_index_in_dim(paired, mine, 1, keepdims=False)
        give = lax.dynamic_index_in_dim(paired, 1 - mine, 1, keepdims=False)
        if narrow:
            give = give.astype(BF16)
        got = lax.ppermute(give, "dp", stage(size, bit))
        values = keep + got.astype(F32)
        bit += 1
    return values[0]


def all_gather(values, size):
    place = lax.axis_index("dp")
    bits = size.bit_length() - 1
    values = values[None]
    for bit in reversed(range(bits)):
        got = lax.ppermute(values, "dp", stage(size, bit))
        mine = ((place >> bit) & 1) == 0
        values = jnp.stack([jnp.where(mine, values, got), jnp.where(mine, got, values)], 1)
        values = values.reshape(-1, *values.shape[2:])
    return values


def adam(weight, first, second, grad, factor):
    clipped = grad * factor
    first = BETA_FIRST * first + (1.0 - BETA_FIRST) * clipped
    second = BETA_SECOND * second + (1.0 - BETA_SECOND) * clipped * clipped
    fixed_first = first / (1.0 - BETA_FIRST**STEP)
    fixed_second = second / (1.0 - BETA_SECOND**STEP)
    weight = weight - LEARN_RATE * (
        fixed_first / (jnp.sqrt(fixed_second) + ADAM_EPS) + WEIGHT_DECAY * weight
    )
    return (first, second, weight)


def pack(arrays, multiple):
    parts = []
    for a in arrays:
        rows, cols = a.shape
        if cols % 128:
            parts.append(a.reshape(-1, 128))
        else:
            parts.append(jnp.swapaxes(a.reshape(rows, cols // 128, 128), 0, 1).reshape(-1, 128))
    total = sum(p.shape[0] for p in parts)
    rest = -total % multiple
    if rest:
        parts.append(jnp.zeros((rest, 128), arrays[0].dtype))
    return jnp.concatenate(parts, 0)


def unpack(packed, shapes):
    out, at = [], 0
    for rows, cols in shapes:
        count = rows * cols // 128
        part = packed[at : at + count]
        at += count
        if cols % 128:
            out.append(part.reshape(rows, cols))
        else:
            out.append(jnp.swapaxes(part.reshape(cols // 128, rows, 128), 0, 1).reshape(rows, cols))
    return out


def shards(
    latents, noise_field, image_tokens, timesteps,
    w_patch, m_patch, v_patch, w_time, m_time, v_time, w_mod, m_mod, v_mod,
    w_qkv, m_qkv, v_qkv, w_out, m_out, v_out, w_up, m_up, v_up, w_down, m_down, v_down,
):
    rows_here, channels, length = latents.shape
    slots = image_tokens.shape[1]
    width = w_patch.shape[2]
    freqs = w_time.shape[0] - width
    core = lax.axis_index("tensor")
    n_dp = lax.axis_size("dp")
    chip_slots = rows_here * slots
    group = w_out.shape[0]
    group_heads = group // HEAD_DIM
    half_hidden = w_up.shape[1]
    kept = rows_here // 2
    mirror = [(i, n_dp - 1 - i) for i in range(n_dp)]

    numbers = jnp.concatenate([image_tokens, timesteps], 1)
    numbers = jnp.concatenate([numbers[:kept], lax.ppermute(numbers[kept:], "dp", mirror)], 0)
    level = signal_levels(timesteps)
    starts = running_sum(image_tokens)
    position = jnp.arange(length, dtype=jnp.int32)[None, :, None]
    member = (position >= starts[:, None, :]) & (position < (starts + image_tokens)[:, None, :])
    keep_tok = jnp.sum(jnp.where(member, jnp.sqrt(level)[:, None, :], 0.0), -1)
    fade_tok = jnp.sum(jnp.where(member, jnp.sqrt(1.0 - level)[:, None, :], 0.0), -1)
    noisy = keep_tok[:, None, :] * latents + fade_tok[:, None, :] * noise_field
    payload = jnp.concatenate([noisy.astype(BF16), noise_field.astype(BF16)], 1)
    xin = jnp.concatenate([payload[:kept], lax.ppermute(payload[kept:], "dp", mirror)], 0)
    counts, steps = numbers[:, :slots], numbers[:, slots:].reshape(-1)
    tab = image_table(counts, core, length)

    qkv_own = (
        w_qkv[0].astype(BF16).reshape(width, group_heads, 3, HEAD_DIM).swapaxes(1, 2).reshape(width, 3, group)
    )
    out_own, up_own, down_own = (w.astype(BF16) for w in (w_out, w_up, w_down))
    wqkv = jnp.stack([qkv_own, swap(qkv_own)], 2).reshape(width, 6 * group)
    wout = jnp.concatenate([out_own, swap(out_own)], 0)
    wup = jnp.concatenate([up_own, swap(up_own)], 1)
    wdn = jnp.concatenate([down_own, swap(down_own)], 0)
    patch_b = w_patch.astype(BF16)
    nothing = jnp.zeros_like(patch_b[0])
    w_in = jnp.concatenate([patch_b[0], nothing], 0)
    w_fin = jnp.concatenate([nothing, patch_b[1]], 0)

    features = time_features(steps, freqs)
    time_hidden, silu_time_back = jax.vjp(jax.nn.silu, precise(features, w_time[:freqs]))
    cond = precise(time_hidden, w_time[freqs:])
    cond_act, silu_cond_back = jax.vjp(jax.nn.silu, cond)
    mod_own = precise(cond_act, w_mod)
    shift_own = (
        precise(cond, w_qkv[1]).reshape(chip_slots, group_heads, 3, HEAD_DIM).swapaxes(1, 2).reshape(chip_slots, 3, group)
    )
    mod_other = swap(mod_own)
    modcat = jnp.stack(
        [
            stacked_bits(jnp.where(core == 0, mod_own, mod_other)),
            stacked_bits(jnp.where(core == 0, mod_other, mod_own)),
        ]
    )
    shiftcat = stacked_bits(jnp.stack([shift_own, swap(shift_own)], 2).reshape(chip_slots, 6 * group))

    longest = rows_here * length // 2 + max(SIZES) // 2
    room = (longest + TILE - 1) // TILE * TILE + TILE
    *saved, gup, gdn, gout, gfin, sg, loss = call_forward(
        tab, xin, modcat, shiftcat, w_in, w_fin, wqkv, wout, wup, wdn, room
    )
    gqkv, gshift, gemb, sg = call_backward(tab, modcat, wqkv, saved, sg)

    def meet(own, other, narrow=True):
        return own + swap(other.astype(BF16) if narrow else other).astype(F32)

    g_up = meet(gup[:, :half_hidden], gup[:, half_hidden:])
    g_down_t = meet(gdn[:, :half_hidden], gdn[:, half_hidden:])
    g_out = meet(gout[:group], gout[group:])

    def head_order(v):
        return v.reshape(-1, 3, group_heads, HEAD_DIM).swapaxes(1, 2).reshape(-1, 3 * group)

    gqkv = gqkv.reshape(width, 3, 2, group)
    g_qkv_main = meet(head_order(gqkv[:, :, 0]), head_order(gqkv[:, :, 1]))
    gshift = gshift[:chip_slots].reshape(chip_slots, 3, 2, group)
    shift_grad = meet(head_order(gshift[:, :, 0]), head_order(gshift[:, :, 1]), False)
    sg = sg.reshape(2, 4, SLOT_LANES, width)[:, :, :chip_slots]
    sg_own = lax.dynamic_index_in_dim(sg, core, 0, keepdims=False)
    sg_other = lax.dynamic_index_in_dim(sg, 1 - core, 0, keepdims=False)
    mod_grad = meet(sg_own, sg_other, False).swapaxes(0, 1).reshape(chip_slots, 4 * width)
    g_embed, g_final = gemb[:channels], gfin[channels:]
    g_patch = meet(
        jnp.where(core == 0, g_embed, g_final), jnp.where(core == 0, g_final, g_embed), False
    )
    loss_sum = jnp.sum(loss)
    loss_sum = meet(loss_sum, loss_sum, False)
    g_qkv_time = precise(cond.T, shift_grad)
    g_mod = precise(cond_act.T, mod_grad)
    term = silu_cond_back(precise(mod_grad, w_mod.T))[0] + precise(shift_grad, w_qkv[1].T)
    grad_cond = meet(term, term, False)
    g_time_second = precise(time_hidden.T, grad_cond)
    g_time_first = precise(features.T, silu_time_back(precise(grad_cond, w_time[freqs:].T))[0])
    g_time = jnp.concatenate([g_time_first, g_time_second], 0)
    time_half = g_time.shape[0] // 2
    g_time = lax.dynamic_slice_in_dim(g_time, core * time_half, time_half, 0)
    count_here = channels * jnp.sum(image_tokens).astype(F32)
    facts = jnp.zeros((8, 128), F32).at[0, 0].set(loss_sum).at[0, 1].set(count_here)

    wide = (g_up, g_down_t, g_out, g_qkv_main, g_qkv_time, g_mod)
    narrow_rows = pack(wide, 16 * n_dp)
    exact_rows = pack((g_time, g_patch, facts), 16 * n_dp)
    narrow_rows = reduce_scatter(narrow_rows.reshape(n_dp, -1, 128), True).astype(BF16)
    exact_rows = reduce_scatter(exact_rows.reshape(n_dp, -1, 128), False)
    narrow_rows = all_gather(narrow_rows, n_dp).reshape(-1, 128)
    exact_rows = all_gather(exact_rows, n_dp).reshape(-1, 128)
    g_up, g_down_t, g_out, g_qkv_main, g_qkv_time, g_mod = unpack(
        narrow_rows.astype(F32), [g.shape for g in wide]
    )
    g_time, g_patch, facts = unpack(exact_rows, [g_time.shape, g_patch.shape, facts.shape])
    loss_sum, count = facts[0, 0], facts[0, 1]
    wide = (g_up, g_down_t, g_out, g_qkv_main, g_qkv_time, g_mod)
    squares = sum(jnp.sum(g * g) for g in wide + (g_time, g_patch))
    grad_norm = jnp.sqrt(squares + swap(squares)) / count
    factor = jnp.minimum(1.0, CLIP_LIMIT / grad_norm) / count
    g_time_other, g_patch_other = swap(g_time), swap(g_patch)
    first = core == 0
    g_time = jnp.concatenate(
        [jnp.where(first, g_time, g_time_other), jnp.where(first, g_time_other, g_time)], 0
    )
    g_patch = jnp.stack(
        [jnp.where(first, g_patch, g_patch_other), jnp.where(first, g_patch_other, g_patch)]
    )
    g_qkv = jnp.stack([g_qkv_main, g_qkv_time])
    weights = (w_patch, w_time, w_mod, w_qkv, w_out, w_up, w_down)
    firsts = (m_patch, m_time, m_mod, m_qkv, m_out, m_up, m_down)
    seconds = (v_patch, v_time, v_mod, v_qkv, v_out, v_up, v_down)
    grads = (g_patch, g_time, g_mod, g_qkv, g_out, g_up, g_down_t.T)
    result = [loss_sum, count, grad_norm]
    for weight, first, second, grad in zip(weights, firsts, seconds, grads):
        result.extend(adam(weight, first, second, grad, factor))
    return tuple(result)


def solution(mesh):
    rows, flat, cols = P("dp", None, None), P("dp", None), P(None, "tensor")
    whole, deep, split = P(), P(None, None, "tensor"), P("tensor", None)
    weights = [p for p in (whole, whole, cols, deep, split, cols, split) for _ in range(3)]
    return jax.shard_map(
        shards,
        mesh=mesh,
        in_specs=(rows, rows, flat, flat, *weights),
        out_specs=(whole, whole, whole, *weights),
        check_vma=False,
    )
```

```python
from functools import partial
import math

import jax
import jax.numpy as jnp
import numpy as np
from jax import lax
from jax.experimental import pallas as pl
from jax.experimental.pallas import tpu as pltpu
from jax.sharding import PartitionSpec as P

HEAD_DIM = 64
STEP = 10
PRECISE_MODE = lax.Precision.HIGHEST
NORM_EPS = 1e-06
CLIP_LIMIT = 0.001
LEARN_RATE = 0.03
BETA_FIRST = 0.9
BETA_SECOND = 0.95
ADAM_EPS = 1e-08
WEIGHT_DECAY = 0.1
SIZES = (64, 144, 256)
TILE = 256
SLOT_LANES = 128
GELU_A = math.sqrt(2.0 / math.pi)
GELU_B = 0.044715
VMEM_LIMIT = 60 * 1024 * 1024
F32 = jnp.float32
BF16 = jnp.bfloat16


def precise(left, right):
    return jnp.dot(left, right, precision=PRECISE_MODE)


def dot(left, right):
    return lax.dot_general(left, right, (((1,), (0,)), ((), ())), preferred_element_type=F32)


def dot_nt(left, right):
    return lax.dot_general(left, right, (((1,), (1,)), ((), ())), preferred_element_type=F32)


def normalize(values):
    centre = values - jnp.mean(values, -1, keepdims=True)
    inverse = lax.rsqrt(jnp.mean(centre * centre, -1, keepdims=True) + NORM_EPS)
    return (centre * inverse, inverse)


def norm_back(grad, normed, inverse):
    return inverse * (
        grad
        - jnp.mean(grad, -1, keepdims=True)
        - normed * jnp.mean(grad * normed, -1, keepdims=True)
    )


def position_rows(width):
    quarter = width // 4
    omega = np.exp(-math.log(10000.0) * np.arange(quarter) / quarter)
    parts = []
    for size in SIZES:
        side = math.isqrt(size)
        offset = np.arange(size)
        row_angle = (offset // side)[:, None] * omega
        col_angle = (offset % side)[:, None] * omega
        parts.append(
            np.concatenate(
                [np.sin(row_angle), np.cos(row_angle), np.sin(col_angle), np.cos(col_angle)], -1
            )
        )
    return np.concatenate(parts, 0).astype(np.float32)


def for_sizes(count, body):
    offset = 0
    for size in SIZES:
        pl.when(count == size)(partial(body, size, offset))
        offset += size


def rows_at(start, size, step):
    return pl.ds(pl.multiple_of(start, step), size)


def fill_member(member, dst, size, index):
    lane = lax.broadcasted_iota(jnp.int32, (size, 2 * SLOT_LANES), 1)
    hot = (lane == index) | (lane == index + SLOT_LANES)
    member[rows_at(dst, size, 16), :] = hot.astype(F32).astype(BF16)


def head_mask(size, half):
    lane = lax.broadcasted_iota(jnp.int32, (size, 2 * HEAD_DIM), 1)
    return (lane >= HEAD_DIM) if half else (lane < HEAD_DIM)


def forward_kernel(
    tab, xin, places, modcat, shiftcat, w_in, w_fin, wqkv, wout, wup, wdn,
    proj, mixed, gmixed, gmid, stream, xtok, lse, own, other, gfin, sg, loss,
    xrow, member, deriv, active, gup, gdn, gout,
):
    width = stream.shape[1]
    low, high, tokens, tiles = (tab[3, j] for j in range(4))
    heads = width // HEAD_DIM
    hidden = wup.shape[1]
    for r in range(xin.shape[0]):
        turned = xin[r].astype(F32).T
        xrow[r * turned.shape[0] : (r + 1) * turned.shape[0], :] = turned.astype(BF16)

    def place_image(i, carry):
        src, dst = tab[1, i], tab[2, i]

        def body(size, offset):
            xtok[rows_at(dst, size, 16), :] = xrow[rows_at(src, size, 16), :]
            stream[rows_at(dst, size, 16), :] = places[offset : offset + size, :]
            fill_member(member, dst, size, i)

        for_sizes(tab[0, i], body)
        return carry

    lax.fori_loop(low, high, place_image, 0)
    tail = rows_at(tokens, TILE, 16)
    for ref in (xtok, stream, member, mixed):
        ref[tail, :] = jnp.zeros((TILE, ref.shape[1]), ref.dtype)
    for ref in (gup, gdn, gout, gfin, sg, loss):
        ref[...] = jnp.zeros(ref.shape, ref.dtype)

    def spread(hot, block):
        return dot(hot, modcat[block // 4, :, block % 4 * width : (block % 4 + 1) * width])

    def project_tile(t, carry):
        r = rows_at(t * TILE, TILE, TILE)
        entering = dot(xtok[r, :], w_in[...]) + stream[r, :]
        stream[r, :] = entering
        hot = member[r, :]
        normed, _ = normalize(entering)
        attn_in = (normed * (1.0 + spread(hot, 1)) + spread(hot, 0)).astype(BF16)
        proj[r, :] = (dot(attn_in, wqkv[...]) + dot(hot, shiftcat[...])).astype(BF16)
        return carry

    lax.fori_loop(0, tiles, project_tile, 0)

    def attend_image(i, carry):
        dst = tab[2, i]

        def body(size, offset):
            r = rows_at(dst, size, 16)
            value_t = proj[r, 2 * width : 3 * width].T
            pieces = []
            for h in range(heads):
                pair = slice(h // 2 * 128, h // 2 * 128 + 128)
                query = proj[r, pair]
                query = jnp.where(head_mask(size, h % 2), query, jnp.zeros_like(query))
                key = proj[r, width + pair.start : width + pair.stop]
                scores = dot_nt(key, query)
                top = jnp.max(scores, 0, keepdims=True)
                weights = jnp.exp((scores - top) * HEAD_DIM ** (-0.5))
                total = jnp.sum(weights, 0, keepdims=True)
                out = dot(value_t[h * HEAD_DIM : (h + 1) * HEAD_DIM, :], weights.astype(BF16))
                pieces.append(out / total)
                lse[i, h : h + 1, :size] = top * HEAD_DIM ** (-0.5) + jnp.log(total)
            mixed[r, :] = jnp.concatenate(pieces, 0).T.astype(BF16)

        for_sizes(tab[0, i], body)
        return carry

    lax.fori_loop(low, high, attend_image, 0)

    def token_tile(t, carry):
        r = rows_at(t * TILE, TILE, TILE)
        hot = member[r, :]
        hot_t = member[r, :SLOT_LANES].astype(F32).T.astype(BF16)

        def collect(block, value):
            sg[block * SLOT_LANES : (block + 1) * SLOT_LANES, :] += dot(hot_t, value.astype(BF16))

        mixed_tile = mixed[r, :]
        attended = dot(mixed_tile, wout[...])
        gate1 = spread(hot, 2)
        mid = stream[r, :] + gate1 * attended
        normed2, inverse2 = normalize(mid)
        scale2 = spread(hot, 4)
        mlp_in = (normed2 * (1.0 + scale2) + spread(hot, 3)).astype(BF16)
        mlp_out = jnp.zeros((TILE, width), F32)
        for j in range(0, hidden, width):
            up = dot(mlp_in, wup[:, j : j + width])
            square = up * up
            bent = jnp.tanh(up * (GELU_A + (GELU_A * GELU_B) * square))
            share = 0.5 + 0.5 * bent
            act = (up * share).astype(BF16)
            active[:, j : j + width] = act
            deriv[:, j : j + width] = share + up * (share * (1.0 - share)) * (
                2.0 * GELU_A + (6.0 * GELU_A * GELU_B) * square
            )
            mlp_out = mlp_out + dot(act, wdn[j : j + width, :])
        gate2 = spread(hot, 5)
        leaving = mid + gate2 * mlp_out
        normed3, inverse3 = normalize(leaving)
        scale3 = spread(hot, 7)
        final_in = (normed3 * (1.0 + scale3) + spread(hot, 6)).astype(BF16)
        predicted = dot_nt(final_in, w_fin[...])
        channels = w_fin.shape[0] // 2
        lane = lax.broadcasted_iota(jnp.int32, predicted.shape, 1)
        row = lax.broadcasted_iota(jnp.int32, predicted.shape, 0) + t * TILE
        keep = (lane >= channels) & (row < tokens)
        error = jnp.where(keep, predicted - xtok[r, :].astype(F32), 0.0)
        loss[...] += jnp.sum(error * error, 0, keepdims=True)
        grad_pred = (2.0 * error).astype(BF16)
        gfin[...] += dot(grad_pred.T, final_in)
        grad_final = dot(grad_pred, w_fin[...])
        collect(6, grad_final)
        collect(7, grad_final * normed3)
        grad_out = norm_back(grad_final * (1.0 + scale3), normed3, inverse3)
        collect(5, grad_out * mlp_out)
        grad_mlp = (grad_out * gate2).astype(BF16)
        grad_mlp_t = grad_mlp.T
        mlp_in_t = mlp_in.T
        grad_mlp_in = jnp.zeros((TILE, width), F32)
        for j in range(0, hidden, width):
            gdn[:, j : j + width] += dot(grad_mlp_t, active[:, j : j + width])
            grad_act = dot_nt(grad_mlp, wdn[j : j + width, :])
            grad_up = (grad_act * deriv[:, j : j + width]).astype(BF16)
            gup[:, j : j + width] += dot(mlp_in_t, grad_up)
            grad_mlp_in = grad_mlp_in + dot_nt(grad_up, wup[:, j : j + width])
        collect(3, grad_mlp_in)
        collect(4, grad_mlp_in * normed2)
        grad_mid = grad_out + norm_back(grad_mlp_in * (1.0 + scale2), normed2, inverse2)
        gmid[r, :] = grad_mid
        collect(2, grad_mid * attended)
        grad_attended = (grad_mid * gate1).astype(BF16)
        gout[...] += dot(mixed_tile.T, grad_attended)
        gmixed[r, :] = dot_nt(grad_attended, wout[...]).astype(BF16)
        return carry

    lax.fori_loop(0, tiles, token_tile, 0)
    at = 0
    half = hidden // 2
    for ref in (gup, gdn):
        for j in range(0, half, 128):
            own[at : at + width, :] = ref[:, j : j + 128]
            other[at : at + width, :] = ref[:, half + j : half + j + 128].astype(BF16)
            at += width
    half = width // 2
    for j in range(0, width, 128):
        own[at : at + half, :] = gout[:half, j : j + 128]
        other[at : at + half, :] = gout[half:, j : j + 128].astype(BF16)
        at += half


def backward_kernel(
    tab, modcat, wqkv, proj, mixed, gmixed, gmid, stream, xtok, lse, sg_in,
    main_own, main_other, shift_own, shift_other, gemb, sg,
    gproj, member, gqkv, gshift,
):
    width = stream.shape[1]
    low, high, tokens, tiles = (tab[3, j] for j in range(4))
    heads = width // HEAD_DIM
    sg[...] = sg_in[...]
    for ref in (gqkv, gshift, gemb):
        ref[...] = jnp.zeros(ref.shape, ref.dtype)
    tail = rows_at(tokens, TILE, 16)
    for ref in (gproj, member):
        ref[tail, :] = jnp.zeros((TILE, ref.shape[1]), ref.dtype)
    head_of = lax.broadcasted_iota(jnp.int32, (8, width), 1) // HEAD_DIM
    head_rows = (head_of == lax.broadcasted_iota(jnp.int32, (8, width), 0)).astype(F32).astype(BF16)

    def attend_image(i, carry):
        dst = tab[2, i]

        def body(size, offset):
            r = rows_at(dst, size, 16)
            fill_member(member, dst, size, i)
            product = gmixed[r, :].astype(F32) * mixed[r, :].astype(F32)
            coarse = product.astype(BF16)
            fine = (product - coarse.astype(F32)).astype(BF16)
            inner = dot_nt(head_rows, coarse) + dot_nt(head_rows, fine)
            key_t = proj[r, width : 2 * width].T
            query_pieces = []
            for p in range(heads // 2):
                pair = slice(p * 128, p * 128 + 128)
                query = proj[r, pair]
                key = proj[r, width + pair.start : width + pair.stop]
                value = proj[r, 2 * width + pair.start : 2 * width + pair.stop]
                grad = gmixed[r, pair]
                grad_key = jnp.zeros((size, 128), F32)
                grad_value = jnp.zeros((size, 128), F32)
                for half in range(2):
                    h = 2 * p + half
                    mask = head_mask(size, half)
                    query_h = jnp.where(mask, query, jnp.zeros_like(query))
                    grad_h = jnp.where(mask, grad, jnp.zeros_like(grad))
                    scores = dot_nt(key, query_h)
                    probs = jnp.exp(scores * HEAD_DIM ** (-0.5) - lse[i, h : h + 1, :size])
                    grad_probs = dot_nt(value, grad_h)
                    grad_scores = (probs * (grad_probs - inner[h : h + 1, :])).astype(BF16)
                    grad_value = grad_value + dot(probs.astype(BF16), grad_h)
                    grad_key = grad_key + dot(grad_scores, query_h)
                    query_pieces.append(dot(key_t[h * HEAD_DIM : (h + 1) * HEAD_DIM, :], grad_scores))
                gproj[r, width + pair.start : width + pair.stop] = (
                    grad_key * HEAD_DIM ** (-0.5)
                ).astype(BF16)
                gproj[r, 2 * width + pair.start : 2 * width + pair.stop] = grad_value.astype(BF16)
            grad_query = jnp.concatenate(query_pieces, 0) * HEAD_DIM ** (-0.5)
            gproj[r, :width] = grad_query.T.astype(BF16)

        for_sizes(tab[0, i], body)
        return carry

    lax.fori_loop(low, high, attend_image, 0)

    def token_tile(t, carry):
        r = rows_at(t * TILE, TILE, TILE)
        hot = member[r, :]
        hot_t = member[r, :SLOT_LANES].astype(F32).T.astype(BF16)

        def spread(block):
            return dot(hot, modcat[block // 4, :, block % 4 * width : (block % 4 + 1) * width])

        def collect(block, value):
            sg[block * SLOT_LANES : (block + 1) * SLOT_LANES, :] += dot(hot_t, value.astype(BF16))

        normed, inverse = normalize(stream[r, :])
        scale1 = spread(1)
        attn_in = (normed * (1.0 + scale1) + spread(0)).astype(BF16)
        grad_proj = gproj[r, :]
        gqkv[...] += dot(attn_in.T, grad_proj)
        gshift[...] += dot(hot_t, grad_proj)
        grad_attn_in = dot_nt(grad_proj, wqkv[...])
        collect(0, grad_attn_in)
        collect(1, grad_attn_in * normed)
        grad_in = gmid[r, :] + norm_back(grad_attn_in * (1.0 + scale1), normed, inverse)
        gemb[...] += dot(xtok[r, :].T, grad_in.astype(BF16))
        return carry

    lax.fori_loop(0, tiles, token_tile, 0)
    group = width // 2
    for source, own, other in ((gqkv, main_own, main_other), (gshift, shift_own, shift_other)):
        for g, target in ((0, own), (1, other)):
            pieces = [
                source[:, part * width + g * group + h * HEAD_DIM : part * width + g * group + (h + 1) * HEAD_DIM]
                for h in range(heads // 2)
                for part in range(3)
            ]
            target[...] = jnp.concatenate(pieces, 1).astype(target.dtype)


def call_forward(tab, xin, modcat, shiftcat, w_in, w_fin, wqkv, wout, wup, wdn, room):
    width, hidden = wup.shape
    here, channels2, length = xin.shape
    slots = SLOT_LANES
    mlp_rows = width * (hidden + width // 2) // 128
    vmem = pl.BlockSpec(memory_space=pltpu.VMEM)
    shape = jax.ShapeDtypeStruct
    outs = (
        shape((room, 3 * width), BF16),
        shape((room, width), BF16),
        shape((room, width), BF16),
        shape((room, width), F32),
        shape((room, width), F32),
        shape((room, channels2), BF16),
        shape((slots, 8, max(SIZES)), F32),
        shape((mlp_rows, 128), F32),
        shape((mlp_rows, 128), BF16),
        shape((channels2, width), F32),
        shape((8 * slots, width), F32),
        shape((1, channels2), F32),
    )
    return pl.pallas_call(
        forward_kernel,
        out_shape=outs,
        in_specs=[pl.BlockSpec(memory_space=pltpu.SMEM)] + [vmem] * 10,
        out_specs=[vmem] * len(outs),
        scratch_shapes=[
            pltpu.VMEM((here * length, channels2), BF16),
            pltpu.VMEM((room, 2 * slots), BF16),
            pltpu.VMEM((TILE, hidden), F32),
            pltpu.VMEM((TILE, hidden), BF16),
            pltpu.VMEM((width, hidden), F32),
            pltpu.VMEM((width, hidden), F32),
            pltpu.VMEM((width, width), F32),
        ],
        compiler_params=pltpu.CompilerParams(vmem_limit_bytes=VMEM_LIMIT),
        name="forward",
    )(tab, xin, jnp.asarray(position_rows(width)), modcat, shiftcat, w_in, w_fin, wqkv, wout, wup, wdn)


def call_backward(tab, modcat, wqkv, saved, sg):
    proj, mixed, gmixed, gmid, stream, xtok, lse = saved
    room, width = stream.shape
    slots = SLOT_LANES
    vmem = pl.BlockSpec(memory_space=pltpu.VMEM)
    shape = jax.ShapeDtypeStruct
    outs = (
        shape((width, 3 * width // 2), F32),
        shape((width, 3 * width // 2), BF16),
        shape((slots, 3 * width // 2), F32),
        shape((slots, 3 * width // 2), F32),
        shape((xtok.shape[1], width), F32),
        shape(sg.shape, F32),
    )
    return pl.pallas_call(
        backward_kernel,
        out_shape=outs,
        in_specs=[pl.BlockSpec(memory_space=pltpu.SMEM)] + [vmem] * 10,
        out_specs=[vmem] * len(outs),
        scratch_shapes=[
            pltpu.VMEM((room, 3 * width), BF16),
            pltpu.VMEM((room, 2 * slots), BF16),
            pltpu.VMEM((width, 3 * width), F32),
            pltpu.VMEM((slots, 3 * width), F32),
        ],
        compiler_params=pltpu.CompilerParams(vmem_limit_bytes=VMEM_LIMIT),
        name="backward",
    )(tab, modcat, wqkv, proj, mixed, gmixed, gmid, stream, xtok, lse, sg)


def signal_levels(steps):
    index = jnp.arange(1000, dtype=jnp.int32)
    betas = 0.0001 + 0.0199 * index.astype(F32) / 999.0
    logs = jnp.log(1.0 - betas)
    return jnp.exp(jnp.sum(jnp.where(index <= steps[..., None], logs, 0.0), -1))


def time_features(steps, freqs):
    half = freqs // 2
    rates = jnp.exp(-math.log(10000.0) * jnp.arange(half, dtype=F32) / half)
    angle = steps.astype(F32)[..., None] * rates
    return jnp.concatenate([jnp.cos(angle), jnp.sin(angle)], -1)


def running_sum(values):
    size = values.shape[-1]
    before = np.arange(size)[:, None] > np.arange(size)[None, :]
    return jnp.sum(jnp.where(before, values[..., None, :], 0), -1)


def image_table(counts, core, length):
    rows_here, slots = counts.shape
    row_start = running_sum(counts) + length * jnp.arange(rows_here, dtype=jnp.int32)[:, None]
    flat = counts.reshape(-1)
    start = running_sum(flat)
    total = jnp.sum(flat)
    index = jnp.arange(flat.shape[0], dtype=jnp.int32)
    first_half = jnp.sum((2 * start + flat <= total).astype(jnp.int32))
    low = jnp.where(core == 0, 0, first_half)
    high = jnp.where(core == 0, first_half, flat.shape[0])
    base = jnp.sum(jnp.where(index < low, flat, 0))
    tokens = jnp.sum(jnp.where((index >= low) & (index < high), flat, 0))
    tiles = (tokens + TILE - 1) // TILE
    facts = jnp.stack([low, high, tokens, tiles]).astype(jnp.int32)
    pad = lambda v: jnp.pad(v.astype(jnp.int32), (0, 128 - v.shape[0]))
    return jnp.stack([pad(flat), pad(row_start.reshape(-1)), pad(start - base), pad(facts)])


def split_bits(values):
    coarse = values.astype(BF16)
    return coarse, (values - coarse.astype(F32)).astype(BF16)


def stacked_bits(values):
    coarse, fine = split_bits(values)
    room = ((0, SLOT_LANES - values.shape[0]), (0, 0))
    return jnp.concatenate([jnp.pad(coarse, room), jnp.pad(fine, room)], 0)


def swap(value):
    return lax.ppermute(value, "tensor", [(0, 1), (1, 0)])


def exact(left, right, dims):
    return lax.dot_general(left, right, (dims, ((), ())), precision=PRECISE_MODE, preferred_element_type=F32)


def gather_kernel(
    own, got, main_own, main_got, shift_own, shift_got, sg_own, sg_got, cond, act_t, cond_t, w_mod, w_time,
    rows, term,
):
    width = w_mod.shape[0]
    slots = cond.shape[0]
    at = own.shape[0]
    rows[:at, :] = own[...] + got[...].astype(F32)
    shift = shift_own[...] + shift_got[...]
    main = main_own[...] + main_got[...].astype(F32)
    both = jnp.concatenate([main, exact(cond_t[...], shift, ((1,), (0,)))], 1)
    for j in range(0, both.shape[1], 128):
        rows[at : at + width, :] = both[:, j : j + 128]
        at += width
    total = jnp.zeros((slots, width), F32)
    for part in range(4):
        grad = sg_own[part] + sg_got[part]
        block = exact(act_t[...], grad, ((1,), (0,)))
        for j in range(0, width, 128):
            rows[at : at + width, :] = block[:, j : j + 128]
            at += width
        total = total + exact(grad, w_mod[:, part * width : (part + 1) * width], ((1,), (1,)))
    rows[at:, :] = jnp.zeros((rows.shape[0] - at, 128), F32)
    gate = 1.0 / (1.0 + jnp.exp(-cond[...]))
    total = total * (gate * (1.0 + cond[...] * (1.0 - gate)))
    term[...] = total + exact(shift, w_time[...], ((1,), (1,)))


def call_gather(rows, *args):
    vmem = pl.BlockSpec(memory_space=pltpu.VMEM)
    slots, width = args[8].shape
    return pl.pallas_call(
        gather_kernel,
        out_shape=(jax.ShapeDtypeStruct((rows, 128), F32), jax.ShapeDtypeStruct((slots, width), F32)),
        in_specs=[vmem] * len(args),
        out_specs=[vmem] * 2,
        compiler_params=pltpu.CompilerParams(vmem_limit_bytes=VMEM_LIMIT),
        name="collect_grads",
    )(*args)


def adam_values(weight, first, second, grad, factor):
    clipped = grad * factor
    first = BETA_FIRST * first + (1.0 - BETA_FIRST) * clipped
    second = BETA_SECOND * second + (1.0 - BETA_SECOND) * clipped * clipped
    root = jnp.sqrt(second * (1.0 / (1.0 - BETA_SECOND**STEP))) + ADAM_EPS
    step = first * (1.0 / (1.0 - BETA_FIRST**STEP)) / root
    return (first, second, weight - LEARN_RATE * (step + WEIGHT_DECAY * weight))


def adam_kernel(n_dp, lists, chunk, time_chunk, n_got, place, factor, patch, *refs):
    got, refs = refs[:n_got], refs[n_got:]
    ins, outs, bufs = refs[:21], refs[21:42], refs[42:63]
    rows, time_rows, sem_in, sem_out, sem_got = refs[63:]
    width = ins[3].shape[1]
    here = place[0]
    scale = factor[0]
    jobs = []
    for p in range(7):
        shape = ins[3 * p].shape
        if p == 0:
            jobs.append((p, None))
        elif p == 3:
            jobs.extend((p, (i,)) for i in range(2))
        else:
            step = shape[0] // 2 if p == 1 else min(width, shape[0])
            jobs.extend(
                (p, (pl.ds(r, step), pl.ds(j, width))) for r in range(0, shape[0], step) for j in range(0, shape[1], width)
            )

    def view(ref, where):
        return ref if where is None else ref.at[where]

    loads = []
    for i, (p, where) in enumerate(jobs):
        group = []
        for k in range(3):
            copy = pltpu.make_async_copy(
                view(ins[3 * p + k], where), view(bufs[3 * p + k], where), sem_in.at[3 * i + k]
            )
            copy.start()
            group.append(copy)
        loads.append(group)
    arrivals = []
    for stream, (pieces, order) in enumerate(lists):
        base = stream * n_dp * chunk
        for source, relatives in zip(pieces, order):
            for j, relative in enumerate(relatives):
                owner = here ^ relative
                parts = [(0, chunk, rows, base + owner * chunk)]
                if stream < 2:
                    parts.append((chunk, time_chunk, time_rows, stream * n_dp * time_chunk + owner * time_chunk))
                for start, size, target, at in parts:
                    copy = pltpu.make_async_copy(
                        got[source].at[j, pl.ds(start, size), :],
                        target.at[pl.ds(pl.multiple_of(at, 16), size), :],
                        sem_got.at[len(arrivals)],
                    )
                    copy.start()
                    arrivals.append(copy)
    for copy in arrivals:
        copy.wait()

    def tiles(at, size, count):
        return jnp.concatenate([rows[at + i * size : at + (i + 1) * size, :] for i in range(count)], 1).astype(F32)

    per_tile = width // 128
    half_time = ins[3].shape[0] // 2
    offsets = {5: 0}
    offsets[6] = ins[15].shape[0] * ins[15].shape[1] // 128
    offsets[4] = offsets[6] + ins[18].shape[0] * ins[18].shape[1] // 128
    offsets[3] = offsets[4] + ins[12].shape[0] * ins[12].shape[1] // 128
    offsets[2] = offsets[3] + 2 * ins[9].shape[1] * ins[9].shape[2] // 128
    stores = []
    for i, (p, where) in enumerate(jobs):
        for copy in loads[i]:
            copy.wait()
        if p == 0:
            grad = patch[...]
        elif p == 1:
            top = where[0].start // half_time * n_dp * time_chunk
            grad = jnp.concatenate(
                [time_rows[top + t * half_time : top + (t + 1) * half_time, :] for t in range(per_tile)], 1
            ).astype(F32)
        elif p == 3:
            cols = ins[9].shape[2]
            at, shift = divmod(where[0] * cols, 128)
            count = (shift + cols + 127) // 128
            grad = tiles(offsets[3] + at * width, width, count)[:, shift : shift + cols]
        elif p == 6:
            grad = tiles(offsets[6] + where[0].start // 128 * width, width, per_tile).T
        else:
            size = ins[3 * p].shape[0]
            grad = tiles(offsets[p] + where[1].start // 128 * size, size, per_tile)
        b = bufs[3 * p : 3 * p + 3]
        index = ... if where is None else where
        values = adam_values(b[0][index], b[1][index], b[2][index], grad, scale)
        for k, value in enumerate(values):
            b[k][index] = value
            copy = pltpu.make_async_copy(view(b[k], where), view(outs[3 * p + k], where), sem_out.at[3 * i + k])
            copy.start()
            stores.append(copy)
    for copy in stores:
        copy.wait()


def call_adam(n_dp, lists, chunk, time_chunk, place, factor, patch, got, params):
    smem = pl.BlockSpec(memory_space=pltpu.SMEM)
    vmem = pl.BlockSpec(memory_space=pltpu.VMEM)
    anywhere = pl.BlockSpec(memory_space=pl.ANY)
    n_jobs = 3 * 16
    return pl.pallas_call(
        partial(adam_kernel, n_dp, lists, chunk, time_chunk, len(got)),
        out_shape=[jax.ShapeDtypeStruct(w.shape, F32) for w in params],
        in_specs=[smem, smem, vmem] + [anywhere] * (len(got) + len(params)),
        out_specs=[anywhere] * len(params),
        scratch_shapes=[pltpu.VMEM(w.shape, F32) for w in params]
        + [
            pltpu.VMEM((3 * n_dp * chunk, 128), BF16),
            pltpu.VMEM((2 * n_dp * time_chunk, 128), BF16),
            pltpu.SemaphoreType.DMA((n_jobs,)),
            pltpu.SemaphoreType.DMA((n_jobs,)),
            pltpu.SemaphoreType.DMA((5 * n_dp,)),
        ],
        compiler_params=pltpu.CompilerParams(vmem_limit_bytes=VMEM_LIMIT),
        name="adam",
    )(place, factor, patch, *got, *params)


def stage(size, bit):
    return [(i, i ^ (1 << bit)) for i in range(size)]


def bit_order(size, turn):
    bits = list(range(size.bit_length() - 1))
    lead = bits[:3]
    turn %= max(len(lead), 1)
    return lead[turn:] + lead[:turn] + bits[3:]


def reduce_scatter(values, size, turn, narrow):
    place = lax.axis_index("dp")
    order = bit_order(size, turn)
    left = sorted(order, reverse=True)
    values = values.reshape(*(2 for _ in left), *values.shape[1:])
    for bit in order:
        mine = (place >> bit) & 1
        axis = left.index(bit)
        left.remove(bit)
        keep = lax.dynamic_index_in_dim(values, mine, axis, keepdims=False)
        give = lax.dynamic_index_in_dim(values, 1 - mine, axis, keepdims=False)
        if narrow:
            give = give.astype(BF16)
        values = keep + lax.ppermute(give, "dp", stage(size, bit)).astype(F32)
    return values


def all_gather(values, size, turn):
    held, relatives = values[None], [0]
    pieces = []
    order = bit_order(size, turn)[::-1]
    for n, bit in enumerate(order):
        got = lax.ppermute(held, "dp", stage(size, bit))
        moved = [r ^ (1 << bit) for r in relatives]
        if n == len(order) - 1:
            pieces = [(held, relatives), (got, moved)]
        held, relatives = jnp.concatenate([held, got], 0), relatives + moved
    return pieces


def sum_everywhere(value, size):
    value = value + swap(value)
    for bit in range(size.bit_length() - 1):
        value = value + lax.ppermute(value, "dp", stage(size, bit))
    return value


def shards(
    latents, noise_field, image_tokens, timesteps,
    w_patch, m_patch, v_patch, w_time, m_time, v_time, w_mod, m_mod, v_mod,
    w_qkv, m_qkv, v_qkv, w_out, m_out, v_out, w_up, m_up, v_up, w_down, m_down, v_down,
):
    rows_here, channels, length = latents.shape
    slots = image_tokens.shape[1]
    width = w_patch.shape[2]
    freqs = w_time.shape[0] - width
    core = lax.axis_index("tensor")
    n_dp = lax.axis_size("dp")
    chip_slots = rows_here * slots
    group = w_out.shape[0]
    group_heads = group // HEAD_DIM
    half_hidden = w_up.shape[1]
    kept = rows_here // 2
    mirror = [(i, n_dp - 1 - i) for i in range(n_dp)]

    numbers = jnp.concatenate([image_tokens, timesteps], 1)
    numbers = jnp.concatenate([numbers[:kept], lax.ppermute(numbers[kept:], "dp", mirror)], 0)
    level = signal_levels(timesteps)
    starts = running_sum(image_tokens)
    position = jnp.arange(length, dtype=jnp.int32)[None, :, None]
    member = (position >= starts[:, None, :]) & (position < (starts + image_tokens)[:, None, :])
    keep_tok = jnp.sum(jnp.where(member, jnp.sqrt(level)[:, None, :], 0.0), -1)
    fade_tok = jnp.sum(jnp.where(member, jnp.sqrt(1.0 - level)[:, None, :], 0.0), -1)
    noisy = keep_tok[:, None, :] * latents + fade_tok[:, None, :] * noise_field
    payload = jnp.concatenate([noisy.astype(BF16), noise_field.astype(BF16)], 1)
    xin = jnp.concatenate([payload[:kept], lax.ppermute(payload[kept:], "dp", mirror)], 0)
    counts, steps = numbers[:, :slots], numbers[:, slots:].reshape(-1)
    tab = image_table(counts, core, length)

    qkv_own = (
        w_qkv[0].astype(BF16).reshape(width, group_heads, 3, HEAD_DIM).swapaxes(1, 2).reshape(width, 3, group)
    )
    out_own, up_own, down_own = (w.astype(BF16) for w in (w_out, w_up, w_down))
    wqkv = jnp.stack([qkv_own, swap(qkv_own)], 2).reshape(width, 6 * group)
    wout = jnp.concatenate([out_own, swap(out_own)], 0)
    wup = jnp.concatenate([up_own, swap(up_own)], 1)
    wdn = jnp.concatenate([down_own, swap(down_own)], 0)
    patch_b = w_patch.astype(BF16)
    nothing = jnp.zeros_like(patch_b[0])
    w_in = jnp.concatenate([patch_b[0], nothing], 0)
    w_fin = jnp.concatenate([nothing, patch_b[1]], 0)

    features = time_features(steps, freqs)
    time_hidden, silu_time_back = jax.vjp(jax.nn.silu, precise(features, w_time[:freqs]))
    cond = precise(time_hidden, w_time[freqs:])
    cond_act = jax.nn.silu(cond)
    mod_own = precise(cond_act, w_mod)
    shift_own = (
        precise(cond, w_qkv[1]).reshape(chip_slots, group_heads, 3, HEAD_DIM).swapaxes(1, 2).reshape(chip_slots, 3, group)
    )
    mod_other = swap(mod_own)
    modcat = jnp.stack(
        [
            stacked_bits(jnp.where(core == 0, mod_own, mod_other)),
            stacked_bits(jnp.where(core == 0, mod_other, mod_own)),
        ]
    )
    shiftcat = stacked_bits(jnp.stack([shift_own, swap(shift_own)], 2).reshape(chip_slots, 6 * group))

    longest = rows_here * length // 2 + max(SIZES) // 2
    room = (longest + TILE - 1) // TILE * TILE + TILE
    *saved, own, other, gfin, sg, loss = call_forward(
        tab, xin, modcat, shiftcat, w_in, w_fin, wqkv, wout, wup, wdn, room
    )
    main_own, main_other, time_own, time_other, gemb, sg = call_backward(tab, modcat, wqkv, saved, sg)

    patch = jnp.concatenate([gemb[:channels], gfin[channels:]], 0)
    count_here = 0.5 * channels * jnp.sum(image_tokens).astype(F32)
    facts = jnp.stack([jnp.sum(loss), count_here])
    facts = jnp.pad(facts[None], ((0, 7), (0, width - 2)))
    patch = sum_everywhere(jnp.concatenate([patch, facts], 0), n_dp)
    loss_sum, count = patch[2 * channels, 0], patch[2 * channels, 1]
    patch = patch[: 2 * channels].reshape(2, channels, width)
    sg = sg.reshape(2, 4, SLOT_LANES, width)[:, :, :chip_slots]
    sg_own = lax.dynamic_index_in_dim(sg, core, 0, keepdims=False)
    sg_other = lax.dynamic_index_in_dim(sg, 1 - core, 0, keepdims=False)
    wide = own.shape[0] + (2 * 3 * group + 4 * width) * width // 128
    unit = 3 * n_dp * 16
    wide = (wide + unit - 1) // unit * unit
    chunk = wide // (3 * n_dp)
    rows, term = call_gather(
        wide, own, swap(other), main_own, swap(main_other),
        time_own[:chip_slots], swap(time_other[:chip_slots]), sg_own, swap(sg_other),
        cond, cond_act.T, cond.T, w_mod, w_qkv[1],
    )
    grad_cond = term + swap(term)
    g_time_second = precise(time_hidden.T, grad_cond)
    g_time_first = precise(features.T, silu_time_back(precise(grad_cond, w_time[freqs:].T))[0])
    g_time = jnp.concatenate([g_time_first, g_time_second], 0)
    time_half = g_time.shape[0] // 2
    g_time = lax.dynamic_slice_in_dim(g_time, core * time_half, time_half, 0)
    g_time = jnp.swapaxes(g_time.reshape(time_half, width // 128, 128), 0, 1).reshape(-1, 128)
    time_chunk = (g_time.shape[0] + 16 * n_dp - 1) // (16 * n_dp) * 16
    g_time = jnp.pad(g_time, ((0, time_chunk * n_dp - g_time.shape[0]), (0, 0)))

    rows = rows.reshape(3, n_dp, chunk, 128)
    parts = [reduce_scatter(rows[k], n_dp, k, True) for k in range(3)]
    time_part = reduce_scatter(g_time.reshape(n_dp, time_chunk, 128), n_dp, 1, False)
    squares = sum(jnp.sum(v * v) for v in (*parts, time_part))
    squares = sum_everywhere(squares, n_dp) + jnp.sum(patch * patch)
    time_part = time_part.astype(BF16)
    time_got = swap(time_part)
    first = core == 0
    sent = [v.astype(BF16) for v in parts]
    sent[0] = jnp.concatenate([sent[0], jnp.where(first, time_part, time_got)], 0)
    sent[1] = jnp.concatenate([sent[1], jnp.where(first, time_got, time_part)], 0)
    got, lists = [], []
    for k in range(3):
        pieces = all_gather(sent[k], n_dp, k)
        lists.append(([len(got) + i for i in range(len(pieces))], [r for _, r in pieces]))
        got.extend(v for v, _ in pieces)
    grad_norm = jnp.sqrt(squares) / count
    factor = jnp.minimum(1.0, CLIP_LIMIT / grad_norm) / count
    params = (
        w_patch, m_patch, v_patch, w_time, m_time, v_time, w_mod, m_mod, v_mod,
        w_qkv, m_qkv, v_qkv, w_out, m_out, v_out, w_up, m_up, v_up, w_down, m_down, v_down,
    )
    updated = call_adam(
        n_dp, lists, chunk, time_chunk, lax.axis_index("dp").reshape(1), factor.reshape(1), patch, got, params
    )
    return (loss_sum, count, grad_norm, *updated)


def solution(mesh):
    rows, flat, cols = P("dp", None, None), P("dp", None), P(None, "tensor")
    whole, deep, split = P(), P(None, None, "tensor"), P("tensor", None)
    weights = [p for p in (whole, whole, cols, deep, split, cols, split) for _ in range(3)]
    return jax.shard_map(
        shards,
        mesh=mesh,
        in_specs=(rows, rows, flat, flat, *weights),
        out_specs=(whole, whole, whole, *weights),
        check_vma=False,
    )
```

```python
from functools import partial
import math

import jax
import jax.numpy as jnp
import numpy as np
from jax import lax
from jax.experimental import pallas as pl
from jax.experimental.pallas import tpu as pltpu
from jax.sharding import PartitionSpec as P

HEAD_DIM = 64
STEP = 10
PRECISE_MODE = lax.Precision.HIGHEST
NORM_EPS = 1e-06
CLIP_LIMIT = 0.001
LEARN_RATE = 0.03
BETA_FIRST = 0.9
BETA_SECOND = 0.95
ADAM_EPS = 1e-08
WEIGHT_DECAY = 0.1
SIZES = (64, 144, 256)
TILE = 256
SLOT_LANES = 128
GELU_A = math.sqrt(2.0 / math.pi)
GELU_B = 0.044715
VMEM_LIMIT = 60 * 1024 * 1024
F32 = jnp.float32
BF16 = jnp.bfloat16


def precise(left, right):
    return jnp.dot(left, right, precision=PRECISE_MODE)


def dot(left, right):
    return lax.dot_general(left, right, (((1,), (0,)), ((), ())), preferred_element_type=F32)


def dot_nt(left, right):
    return lax.dot_general(left, right, (((1,), (1,)), ((), ())), preferred_element_type=F32)


def normalize(values):
    centre = values - jnp.mean(values, -1, keepdims=True)
    inverse = lax.rsqrt(jnp.mean(centre * centre, -1, keepdims=True) + NORM_EPS)
    return (centre * inverse, inverse)


def norm_back(grad, normed, inverse):
    return inverse * (
        grad
        - jnp.mean(grad, -1, keepdims=True)
        - normed * jnp.mean(grad * normed, -1, keepdims=True)
    )


def position_rows(width):
    quarter = width // 4
    omega = np.exp(-math.log(10000.0) * np.arange(quarter) / quarter)
    parts = []
    for size in SIZES:
        side = math.isqrt(size)
        offset = np.arange(size)
        row_angle = (offset // side)[:, None] * omega
        col_angle = (offset % side)[:, None] * omega
        parts.append(
            np.concatenate(
                [np.sin(row_angle), np.cos(row_angle), np.sin(col_angle), np.cos(col_angle)], -1
            )
        )
    return np.concatenate(parts, 0).astype(np.float32)


def for_sizes(count, body):
    offset = 0
    for size in SIZES:
        pl.when(count == size)(partial(body, size, offset))
        offset += size


def rows_at(start, size, step):
    return pl.ds(pl.multiple_of(start, step), size)


def fill_member(member, dst, size, index):
    lane = lax.broadcasted_iota(jnp.int32, (size, 2 * SLOT_LANES), 1)
    hot = (lane == index) | (lane == index + SLOT_LANES)
    member[rows_at(dst, size, 16), :] = hot.astype(F32).astype(BF16)


def head_mask(size, half):
    lane = lax.broadcasted_iota(jnp.int32, (size, 2 * HEAD_DIM), 1)
    return (lane >= HEAD_DIM) if half else (lane < HEAD_DIM)


def forward_kernel(
    tab, x_own, x_got, places, mod_own, mod_got, shift_own, shift_got, patch,
    qkv_own, qkv_got, out_own, out_got, up_own, up_got, dn_own, dn_got,
    proj, mixed, gmixed, gmid, stream, xtok, lse, own, other, gfin, sg, loss, modcat, wqkv,
    xrow, member, deriv, active, gup, gdn, gout, shiftcat, wout, w_in, w_fin,
):
    width = stream.shape[1]
    low, high, tokens, tiles, core = (tab[3, j] for j in range(5))
    heads = width // HEAD_DIM
    group_heads = heads // 2
    group = width // 2
    half_hidden = up_own.shape[1]
    hidden = 2 * half_hidden
    channels = patch.shape[1]
    chip_slots = mod_own.shape[0]
    at = 0
    for x in (x_own, x_got):
        for r in range(x.shape[0]):
            turned = x[r].astype(F32).T
            xrow[at : at + turned.shape[0], :] = turned.astype(BF16)
            at += turned.shape[0]
    for g, source in enumerate((qkv_own, qkv_got)):
        for h in range(group_heads):
            for part in range(3):
                to = part * width + g * group + h * HEAD_DIM
                start = (3 * h + part) * HEAD_DIM
                wqkv[to : to + HEAD_DIM, :] = source[start : start + HEAD_DIM, :]
    wout[:group, :] = out_own[...]
    wout[group:, :] = out_got[...]
    nothing = jnp.zeros((channels, width), BF16)
    w_in[:channels, :] = patch[0].astype(BF16)
    w_in[channels:, :] = nothing
    w_fin[:channels, :] = nothing
    w_fin[channels:, :] = patch[1].astype(BF16)

    def two_terms(target, values):
        coarse = values.astype(BF16)
        rest = jnp.zeros((SLOT_LANES - chip_slots, values.shape[1]), BF16)
        for base, term in ((0, coarse), (SLOT_LANES, (values - coarse.astype(F32)).astype(BF16))):
            target[base : base + chip_slots, :] = term
            target[base + chip_slots : base + SLOT_LANES, :] = rest

    for half in range(2):
        two_terms(modcat.at[half], jnp.where(core == half, mod_own[...], mod_got[...]))
    two_terms(
        shiftcat,
        jnp.concatenate(
            [
                source[:, (3 * h + part) * HEAD_DIM : (3 * h + part + 1) * HEAD_DIM]
                for part in range(3)
                for source in (shift_own, shift_got)
                for h in range(group_heads)
            ],
            1,
        ),
    )
    ups = [(ref, j) for ref in (up_own, up_got) for j in range(0, half_hidden, width)]
    downs = [(ref, j) for ref in (dn_own, dn_got) for j in range(0, half_hidden, width)]

    def place_image(i, carry):
        src, dst = tab[1, i], tab[2, i]

        def body(size, offset):
            xtok[rows_at(dst, size, 16), :] = xrow[rows_at(src, size, 16), :]
            stream[rows_at(dst, size, 16), :] = places[offset : offset + size, :]
            fill_member(member, dst, size, i)

        for_sizes(tab[0, i], body)
        return carry

    lax.fori_loop(low, high, place_image, 0)
    tail = rows_at(tokens, TILE, 16)
    for ref in (xtok, stream, member, mixed):
        ref[tail, :] = jnp.zeros((TILE, ref.shape[1]), ref.dtype)
    for ref in (gup, gdn, gout, gfin, sg, loss):
        ref[...] = jnp.zeros(ref.shape, ref.dtype)

    def spread(hot, block):
        return dot(hot, modcat[block // 4, :, block % 4 * width : (block % 4 + 1) * width])

    def project_tile(t, carry):
        r = rows_at(t * TILE, TILE, TILE)
        entering = dot(xtok[r, :], w_in[...]) + stream[r, :]
        stream[r, :] = entering
        hot = member[r, :]
        normed, _ = normalize(entering)
        attn_in = (normed * (1.0 + spread(hot, 1)) + spread(hot, 0)).astype(BF16)
        proj[r, :] = (dot_nt(attn_in, wqkv[...]) + dot(hot, shiftcat[...])).astype(BF16)
        return carry

    lax.fori_loop(0, tiles, project_tile, 0)

    def attend_image(i, carry):
        dst = tab[2, i]

        def body(size, offset):
            r = rows_at(dst, size, 16)
            value_t = proj[r, 2 * width : 3 * width].T
            pieces = []
            for h in range(heads):
                pair = slice(h // 2 * 128, h // 2 * 128 + 128)
                query = proj[r, pair]
                query = jnp.where(head_mask(size, h % 2), query, jnp.zeros_like(query))
                key = proj[r, width + pair.start : width + pair.stop]
                scores = dot_nt(key, query)
                top = jnp.max(scores, 0, keepdims=True)
                weights = jnp.exp((scores - top) * HEAD_DIM ** (-0.5))
                total = jnp.sum(weights, 0, keepdims=True)
                out = dot(value_t[h * HEAD_DIM : (h + 1) * HEAD_DIM, :], weights.astype(BF16))
                pieces.append(out / total)
                lse[i, h : h + 1, :size] = top * HEAD_DIM ** (-0.5) + jnp.log(total)
            mixed[r, :] = jnp.concatenate(pieces, 0).T.astype(BF16)

        for_sizes(tab[0, i], body)
        return carry

    lax.fori_loop(low, high, attend_image, 0)

    def token_tile(t, carry):
        r = rows_at(t * TILE, TILE, TILE)
        hot = member[r, :]
        hot_t = member[r, :SLOT_LANES].astype(F32).T.astype(BF16)

        def collect(block, value):
            sg[block * SLOT_LANES : (block + 1) * SLOT_LANES, :] += dot(hot_t, value.astype(BF16))

        mixed_tile = mixed[r, :]
        attended = dot(mixed_tile, wout[...])
        gate1 = spread(hot, 2)
        mid = stream[r, :] + gate1 * attended
        normed2, inverse2 = normalize(mid)
        scale2 = spread(hot, 4)
        mlp_in = (normed2 * (1.0 + scale2) + spread(hot, 3)).astype(BF16)
        mlp_out = jnp.zeros((TILE, width), F32)
        for j, (wup, u), (wdn, d) in zip(range(0, hidden, width), ups, downs):
            up = dot(mlp_in, wup[:, u : u + width])
            square = up * up
            bent = jnp.tanh(up * (GELU_A + (GELU_A * GELU_B) * square))
            share = 0.5 + 0.5 * bent
            act = (up * share).astype(BF16)
            active[:, j : j + width] = act
            deriv[:, j : j + width] = share + up * (share * (1.0 - share)) * (
                2.0 * GELU_A + (6.0 * GELU_A * GELU_B) * square
            )
            mlp_out = mlp_out + dot(act, wdn[d : d + width, :])
        gate2 = spread(hot, 5)
        leaving = mid + gate2 * mlp_out
        normed3, inverse3 = normalize(leaving)
        scale3 = spread(hot, 7)
        final_in = (normed3 * (1.0 + scale3) + spread(hot, 6)).astype(BF16)
        predicted = dot_nt(final_in, w_fin[...])
        lane = lax.broadcasted_iota(jnp.int32, predicted.shape, 1)
        row = lax.broadcasted_iota(jnp.int32, predicted.shape, 0) + t * TILE
        keep = (lane >= channels) & (row < tokens)
        error = jnp.where(keep, predicted - xtok[r, :].astype(F32), 0.0)
        loss[...] += jnp.sum(error * error, 0, keepdims=True)
        grad_pred = (2.0 * error).astype(BF16)
        gfin[...] += dot(grad_pred.T, final_in)
        grad_final = dot(grad_pred, w_fin[...])
        collect(6, grad_final)
        collect(7, grad_final * normed3)
        grad_out = norm_back(grad_final * (1.0 + scale3), normed3, inverse3)
        collect(5, grad_out * mlp_out)
        grad_mlp = (grad_out * gate2).astype(BF16)
        grad_mlp_t = grad_mlp.T
        mlp_in_t = mlp_in.T
        grad_mlp_in = jnp.zeros((TILE, width), F32)
        for j, (wup, u), (wdn, d) in zip(range(0, hidden, width), ups, downs):
            gdn[:, j : j + width] += dot(grad_mlp_t, active[:, j : j + width])
            grad_act = dot_nt(grad_mlp, wdn[d : d + width, :])
            grad_up = (grad_act * deriv[:, j : j + width]).astype(BF16)
            gup[:, j : j + width] += dot(mlp_in_t, grad_up)
            grad_mlp_in = grad_mlp_in + dot_nt(grad_up, wup[:, u : u + width])
        collect(3, grad_mlp_in)
        collect(4, grad_mlp_in * normed2)
        grad_mid = grad_out + norm_back(grad_mlp_in * (1.0 + scale2), normed2, inverse2)
        gmid[r, :] = grad_mid
        collect(2, grad_mid * attended)
        grad_attended = (grad_mid * gate1).astype(BF16)
        gout[...] += dot(mixed_tile.T, grad_attended)
        gmixed[r, :] = dot_nt(grad_attended, wout[...]).astype(BF16)
        return carry

    lax.fori_loop(0, tiles, token_tile, 0)
    at = 0
    half = hidden // 2
    for ref in (gup, gdn):
        for j in range(0, half, 128):
            own[at : at + width, :] = ref[:, j : j + 128]
            other[at : at + width, :] = ref[:, half + j : half + j + 128].astype(BF16)
            at += width
    half = width // 2
    for j in range(0, width, 128):
        own[at : at + half, :] = gout[:half, j : j + 128]
        other[at : at + half, :] = gout[half:, j : j + 128].astype(BF16)
        at += half


def backward_kernel(
    tab, modcat, wqkv, proj, mixed, gmixed, gmid, stream, xtok, lse, sg_in,
    main_own, main_other, shift_own, shift_other, gemb, sg_own, sg_other,
    gproj, member, gqkv, gshift, sg,
):
    width = stream.shape[1]
    low, high, tokens, tiles, core = (tab[3, j] for j in range(5))
    heads = width // HEAD_DIM
    sg[...] = sg_in[...]
    for ref in (gqkv, gshift, gemb):
        ref[...] = jnp.zeros(ref.shape, ref.dtype)
    tail = rows_at(tokens, TILE, 16)
    for ref in (gproj, member):
        ref[tail, :] = jnp.zeros((TILE, ref.shape[1]), ref.dtype)
    head_of = lax.broadcasted_iota(jnp.int32, (8, width), 1) // HEAD_DIM
    head_rows = (head_of == lax.broadcasted_iota(jnp.int32, (8, width), 0)).astype(F32).astype(BF16)

    def attend_image(i, carry):
        dst = tab[2, i]

        def body(size, offset):
            r = rows_at(dst, size, 16)
            fill_member(member, dst, size, i)
            product = gmixed[r, :].astype(F32) * mixed[r, :].astype(F32)
            coarse = product.astype(BF16)
            fine = (product - coarse.astype(F32)).astype(BF16)
            inner = dot_nt(head_rows, coarse) + dot_nt(head_rows, fine)
            key_t = proj[r, width : 2 * width].T
            query_pieces = []
            for p in range(heads // 2):
                pair = slice(p * 128, p * 128 + 128)
                query = proj[r, pair]
                key = proj[r, width + pair.start : width + pair.stop]
                value = proj[r, 2 * width + pair.start : 2 * width + pair.stop]
                grad = gmixed[r, pair]
                grad_key = jnp.zeros((size, 128), F32)
                grad_value = jnp.zeros((size, 128), F32)
                for half in range(2):
                    h = 2 * p + half
                    mask = head_mask(size, half)
                    query_h = jnp.where(mask, query, jnp.zeros_like(query))
                    grad_h = jnp.where(mask, grad, jnp.zeros_like(grad))
                    scores = dot_nt(key, query_h)
                    probs = jnp.exp(scores * HEAD_DIM ** (-0.5) - lse[i, h : h + 1, :size])
                    grad_probs = dot_nt(value, grad_h)
                    grad_scores = (probs * (grad_probs - inner[h : h + 1, :])).astype(BF16)
                    grad_value = grad_value + dot(probs.astype(BF16), grad_h)
                    grad_key = grad_key + dot(grad_scores, query_h)
                    query_pieces.append(dot(key_t[h * HEAD_DIM : (h + 1) * HEAD_DIM, :], grad_scores))
                gproj[r, width + pair.start : width + pair.stop] = (
                    grad_key * HEAD_DIM ** (-0.5)
                ).astype(BF16)
                gproj[r, 2 * width + pair.start : 2 * width + pair.stop] = grad_value.astype(BF16)
            grad_query = jnp.concatenate(query_pieces, 0) * HEAD_DIM ** (-0.5)
            gproj[r, :width] = grad_query.T.astype(BF16)

        for_sizes(tab[0, i], body)
        return carry

    lax.fori_loop(low, high, attend_image, 0)

    def token_tile(t, carry):
        r = rows_at(t * TILE, TILE, TILE)
        hot = member[r, :]
        hot_t = member[r, :SLOT_LANES].astype(F32).T.astype(BF16)

        def spread(block):
            return dot(hot, modcat[block // 4, :, block % 4 * width : (block % 4 + 1) * width])

        def collect(block, value):
            sg[block * SLOT_LANES : (block + 1) * SLOT_LANES, :] += dot(hot_t, value.astype(BF16))

        normed, inverse = normalize(stream[r, :])
        scale1 = spread(1)
        attn_in = (normed * (1.0 + scale1) + spread(0)).astype(BF16)
        grad_proj = gproj[r, :]
        gqkv[...] += dot(attn_in.T, grad_proj)
        gshift[...] += dot(hot_t, grad_proj)
        grad_attn_in = dot(grad_proj, wqkv[...])
        collect(0, grad_attn_in)
        collect(1, grad_attn_in * normed)
        grad_in = gmid[r, :] + norm_back(grad_attn_in * (1.0 + scale1), normed, inverse)
        gemb[...] += dot(xtok[r, :].T, grad_in.astype(BF16))
        return carry

    lax.fori_loop(0, tiles, token_tile, 0)
    group = width // 2
    turned = gqkv[...].T
    kept = shift_own.shape[0]
    for g, (main, shift) in enumerate(((main_own, shift_own), (main_other, shift_other))):
        pieces = []
        for h in range(heads // 2):
            for part in range(3):
                start = part * width + g * group + h * HEAD_DIM
                to = (3 * h + part) * HEAD_DIM
                main[to : to + HEAD_DIM, :] = turned[start : start + HEAD_DIM, :].astype(main.dtype)
                pieces.append(gshift[:kept, start : start + HEAD_DIM])
        shift[...] = jnp.concatenate(pieces, 1)
    for part in range(4):
        lower = sg[part * SLOT_LANES : part * SLOT_LANES + kept, :]
        upper = sg[(4 + part) * SLOT_LANES : (4 + part) * SLOT_LANES + kept, :]
        sg_own[part] = jnp.where(core == 0, lower, upper)
        sg_other[part] = jnp.where(core == 0, upper, lower)


def call_forward(tab, x_own, x_got, mods, shifts, patch, weights, room):
    kept, channels2, length = x_own.shape
    width, half_hidden = weights[4].shape
    hidden = 2 * half_hidden
    slots = SLOT_LANES
    mlp_rows = width * (hidden + width // 2) // 128
    vmem = pl.BlockSpec(memory_space=pltpu.VMEM)
    shape = jax.ShapeDtypeStruct
    outs = (
        shape((room, 3 * width), BF16),
        shape((room, width), BF16),
        shape((room, width), BF16),
        shape((room, width), F32),
        shape((room, width), F32),
        shape((room, channels2), BF16),
        shape((slots, 8, max(SIZES)), F32),
        shape((mlp_rows, 128), F32),
        shape((mlp_rows, 128), BF16),
        shape((channels2, width), F32),
        shape((8 * slots, width), F32),
        shape((1, channels2), F32),
        shape((2, 2 * slots, 4 * width), BF16),
        shape((3 * width, width), BF16),
    )
    return pl.pallas_call(
        forward_kernel,
        out_shape=outs,
        in_specs=[pl.BlockSpec(memory_space=pltpu.SMEM)] + [vmem] * 16,
        out_specs=[vmem] * len(outs),
        scratch_shapes=[
            pltpu.VMEM((2 * kept * length, channels2), BF16),
            pltpu.VMEM((room, 2 * slots), BF16),
            pltpu.VMEM((TILE, hidden), F32),
            pltpu.VMEM((TILE, hidden), BF16),
            pltpu.VMEM((width, hidden), F32),
            pltpu.VMEM((width, hidden), F32),
            pltpu.VMEM((width, width), F32),
            pltpu.VMEM((2 * slots, 3 * width), BF16),
            pltpu.VMEM((width, width), BF16),
            pltpu.VMEM((channels2, width), BF16),
            pltpu.VMEM((channels2, width), BF16),
        ],
        compiler_params=pltpu.CompilerParams(vmem_limit_bytes=VMEM_LIMIT),
        name="forward",
    )(tab, x_own, x_got, jnp.asarray(position_rows(width)), *mods, *shifts, patch, *weights)


def call_backward(tab, modcat, wqkv, saved, sg, kept):
    proj, mixed, gmixed, gmid, stream, xtok, lse = saved
    room, width = stream.shape
    slots = SLOT_LANES
    vmem = pl.BlockSpec(memory_space=pltpu.VMEM)
    shape = jax.ShapeDtypeStruct
    outs = (
        shape((3 * width // 2, width), F32),
        shape((3 * width // 2, width), BF16),
        shape((kept, 3 * width // 2), F32),
        shape((kept, 3 * width // 2), F32),
        shape((xtok.shape[1], width), F32),
        shape((4, kept, width), F32),
        shape((4, kept, width), F32),
    )
    return pl.pallas_call(
        backward_kernel,
        out_shape=outs,
        in_specs=[pl.BlockSpec(memory_space=pltpu.SMEM)] + [vmem] * 10,
        out_specs=[vmem] * len(outs),
        scratch_shapes=[
            pltpu.VMEM((room, 3 * width), BF16),
            pltpu.VMEM((room, 2 * slots), BF16),
            pltpu.VMEM((width, 3 * width), F32),
            pltpu.VMEM((slots, 3 * width), F32),
            pltpu.VMEM((8 * slots, width), F32),
        ],
        compiler_params=pltpu.CompilerParams(vmem_limit_bytes=VMEM_LIMIT),
        name="backward",
    )(tab, modcat, wqkv, proj, mixed, gmixed, gmid, stream, xtok, lse, sg)


def signal_levels(steps):
    index = jnp.arange(1000, dtype=jnp.int32)
    betas = 0.0001 + 0.0199 * index.astype(F32) / 999.0
    logs = jnp.log(1.0 - betas)
    return jnp.exp(jnp.sum(jnp.where(index <= steps[..., None], logs, 0.0), -1))


def time_features(steps, freqs):
    half = freqs // 2
    rates = jnp.exp(-math.log(10000.0) * jnp.arange(half, dtype=F32) / half)
    angle = steps.astype(F32)[..., None] * rates
    return jnp.concatenate([jnp.cos(angle), jnp.sin(angle)], -1)


def running_sum(values):
    size = values.shape[-1]
    before = np.arange(size)[:, None] > np.arange(size)[None, :]
    return jnp.sum(jnp.where(before, values[..., None, :], 0), -1)


def image_table(counts, core, length):
    rows_here, slots = counts.shape
    row_start = running_sum(counts) + length * jnp.arange(rows_here, dtype=jnp.int32)[:, None]
    flat = counts.reshape(-1)
    start = running_sum(flat)
    total = jnp.sum(flat)
    index = jnp.arange(flat.shape[0], dtype=jnp.int32)
    first_half = jnp.sum((2 * start + flat <= total).astype(jnp.int32))
    low = jnp.where(core == 0, 0, first_half)
    high = jnp.where(core == 0, first_half, flat.shape[0])
    base = jnp.sum(jnp.where(index < low, flat, 0))
    tokens = jnp.sum(jnp.where((index >= low) & (index < high), flat, 0))
    tiles = (tokens + TILE - 1) // TILE
    facts = jnp.stack([low, high, tokens, tiles, core]).astype(jnp.int32)
    pad = lambda v: jnp.pad(v.astype(jnp.int32), (0, 128 - v.shape[0]))
    return jnp.stack([pad(flat), pad(row_start.reshape(-1)), pad(start - base), pad(facts)])


def swap(value):
    return lax.ppermute(value, "tensor", [(0, 1), (1, 0)])


def fine_dot(left, right, dims):
    left_a, right_a = left.astype(BF16), right.astype(BF16)
    left_b = (left - left_a.astype(F32)).astype(BF16)
    right_b = (right - right_a.astype(F32)).astype(BF16)
    product = partial(lax.dot_general, dimension_numbers=(dims, ((), ())), preferred_element_type=F32)
    return product(left_a, right_a) + (product(left_a, right_b) + product(left_b, right_a))


PLAIN, TURNED = ((1,), (0,)), ((1,), (1,))


def silu_slope(value):
    gate = 1.0 / (1.0 + jnp.exp(-value))
    return gate * (1.0 + value * (1.0 - gate))


def term_kernel(shift_own, shift_got, sg_own, sg_got, cond, w_mod, w_time, term):
    width = w_mod.shape[0]
    total = jnp.zeros(cond.shape, F32)
    for part in range(4):
        grad = sg_own[part] + sg_got[part]
        total = total + fine_dot(grad, w_mod[:, part * width : (part + 1) * width], TURNED)
    term[...] = total * silu_slope(cond[...]) + fine_dot(shift_own[...] + shift_got[...], w_time[...], PLAIN)


def pack_kernel(own, got, main_own, main_got, shift_own, shift_got, sg_own, sg_got, cond, rows):
    width = cond.shape[1]
    at = own.shape[0]
    rows[:at, :] = own[...] + got[...].astype(F32)
    values = cond[...]
    act_t = (values / (1.0 + jnp.exp(-values))).T
    shift_t = (shift_own[...] + shift_got[...]).T

    def put(block):
        nonlocal at
        for j in range(0, width, 128):
            rows[at : at + block.shape[0], :] = block[:, j : j + 128]
            at += block.shape[0]

    put(main_own[...] + main_got[...].astype(F32))
    put(fine_dot(shift_t, values, PLAIN))
    for part in range(4):
        put(fine_dot(act_t, sg_own[part] + sg_got[part], PLAIN))
    rows[at:, :] = jnp.zeros((rows.shape[0] - at, 128), F32)


def time_kernel(time_chunk, extra, tab, term, got, before, features, w_time, patch, patch_got, rows, flat):
    width = w_time.shape[1]
    freqs = features.shape[1]
    grad_cond = term[...] + got[...]
    values = before[...]
    hidden = values / (1.0 + jnp.exp(-values))
    second = fine_dot(hidden.T, grad_cond, PLAIN)
    inner = fine_dot(grad_cond, w_time[freqs:, :], TURNED) * silu_slope(values)
    first = fine_dot(features[...].T, inner, PLAIN)
    half = w_time.shape[0] // 2
    both = jnp.concatenate([first, second], 0)
    mine = jnp.where(tab[3, 4] == 0, both[:half], both[half:])
    shared = patch[...] + patch_got[...]
    n_dp = rows.shape[0]
    flat[...] = jnp.zeros(flat.shape, F32)
    patch_at = n_dp * time_chunk
    for t in range(width // 128):
        flat[t * half : (t + 1) * half, :] = mine[:, t * 128 : (t + 1) * 128]
        to = patch_at + t * shared.shape[0]
        flat[to : to + shared.shape[0], :] = shared[:, t * 128 : (t + 1) * 128]
    for d in range(n_dp):
        rows[d, :time_chunk, :] = flat[d * time_chunk : (d + 1) * time_chunk, :]
        rows[d, time_chunk:, :] = flat[patch_at + d * extra : patch_at + (d + 1) * extra, :]


def call_time(n_dp, time_chunk, extra, table, *args):
    vmem = pl.BlockSpec(memory_space=pltpu.VMEM)
    return pl.pallas_call(
        partial(time_kernel, time_chunk, extra),
        out_shape=jax.ShapeDtypeStruct((n_dp, time_chunk + extra, 128), F32),
        in_specs=[pl.BlockSpec(memory_space=pltpu.SMEM)] + [vmem] * len(args),
        out_specs=vmem,
        scratch_shapes=[pltpu.VMEM((n_dp * (time_chunk + extra), 128), F32)],
        compiler_params=pltpu.CompilerParams(vmem_limit_bytes=VMEM_LIMIT),
        name="time_grads",
    )(table, *args)


def call_small(kernel, shape, name, *args):
    vmem = pl.BlockSpec(memory_space=pltpu.VMEM)
    return pl.pallas_call(
        kernel,
        out_shape=jax.ShapeDtypeStruct(shape, F32),
        in_specs=[vmem] * len(args),
        out_specs=vmem,
        compiler_params=pltpu.CompilerParams(vmem_limit_bytes=VMEM_LIMIT),
        name=name,
    )(*args)


def adam_values(weight, first, second, grad, factor):
    clipped = grad * factor
    first = BETA_FIRST * first + (1.0 - BETA_FIRST) * clipped
    second = BETA_SECOND * second + (1.0 - BETA_SECOND) * clipped * clipped
    root = jnp.sqrt(second * (1.0 / (1.0 - BETA_SECOND**STEP))) + ADAM_EPS
    step = first * (1.0 / (1.0 - BETA_FIRST**STEP)) / root
    return (first, second, weight - LEARN_RATE * (step + WEIGHT_DECAY * weight))


def adam_kernel(n_dp, lists, chunks, time_chunk, extra, place, *refs):
    n_got = sum(len(pieces) for pieces, _ in lists)
    got, refs = refs[:n_got], refs[n_got:]
    ins, outs, stats, bufs = refs[:21], refs[21:42], refs[42], refs[43:64]
    rows, time_rows, extra_rows, sem_in, sem_out, sem_got = refs[64:]
    width = ins[3].shape[1]
    here = place[0]
    jobs = []
    for p in range(7):
        shape = ins[3 * p].shape
        if p == 0:
            jobs.append((p, None))
        elif p == 3:
            jobs.extend((p, (i,)) for i in range(2))
        else:
            step = shape[0] // 2 if p == 1 else min(width, shape[0])
            jobs.extend(
                (p, (pl.ds(r, step), pl.ds(j, width))) for r in range(0, shape[0], step) for j in range(0, shape[1], width)
            )

    def view(ref, where):
        return ref if where is None else ref.at[where]

    loads = []
    for i, (p, where) in enumerate(jobs):
        group = []
        for k in range(3):
            copy = pltpu.make_async_copy(
                view(ins[3 * p + k], where), view(bufs[3 * p + k], where), sem_in.at[3 * i + k]
            )
            copy.start()
            group.append(copy)
        loads.append(group)
    arrivals = []
    base = 0
    for stream, ((pieces, order), chunk) in enumerate(zip(lists, chunks)):
        for source, relatives in zip(pieces, order):
            for j, relative in enumerate(relatives):
                owner = here ^ relative
                parts = [(0, chunk, rows, base + owner * chunk)]
                if stream == len(chunks) - 1:
                    parts.append((chunk, time_chunk, time_rows, owner * time_chunk))
                    parts.append((chunk + time_chunk, time_chunk, time_rows, (n_dp + owner) * time_chunk))
                    parts.append((chunk + 2 * time_chunk, 6 * extra, extra_rows, owner * 6 * extra))
                for start, size, target, at in parts:
                    copy = pltpu.make_async_copy(
                        got[source].at[j, pl.ds(start, size), :],
                        target.at[pl.ds(pl.multiple_of(at, 16), size), :],
                        sem_got.at[len(arrivals)],
                    )
                    copy.start()
                    arrivals.append(copy)
        base += n_dp * chunk
    for copy in arrivals:
        copy.wait()
    shards = []
    squares = jnp.zeros((1, 128), F32)
    for owner in range(n_dp):
        at = owner * 6 * extra
        terms = [extra_rows[at + k * 2 * extra : at + (k + 1) * 2 * extra, :].astype(F32) for k in range(3)]
        whole = terms[0] + terms[1] + terms[2]
        shards.append(whole[:extra])
        squares = squares + whole[extra : extra + 1]
    shared = jnp.concatenate(shards, 0)
    each = 2 * ins[0].shape[1] + 8
    patch = jnp.concatenate([shared[t * each : t * each + each - 8] for t in range(width // 128)], 1)
    facts = shared[each - 8 : each - 7]
    loss, count = facts[:, 0:1], facts[:, 1:2]
    squares = jnp.sum(squares, 1, keepdims=True)
    squares = squares + jnp.sum(jnp.sum(patch * patch, 1, keepdims=True), 0, keepdims=True)
    grad_norm = jnp.sqrt(squares) / count
    scale = jnp.minimum(1.0, CLIP_LIMIT / grad_norm) / count
    lane = lax.broadcasted_iota(jnp.int32, stats.shape, 1)
    stats[...] = jnp.where(lane == 0, loss, jnp.where(lane == 1, count, grad_norm))
    patch = patch.reshape(ins[0].shape)

    def tiles(at, size, count):
        return jnp.concatenate([rows[at + i * size : at + (i + 1) * size, :] for i in range(count)], 1).astype(F32)

    per_tile = width // 128
    half_time = ins[3].shape[0] // 2
    offsets = {5: 0}
    offsets[6] = ins[15].shape[0] * ins[15].shape[1] // 128
    offsets[4] = offsets[6] + ins[18].shape[0] * ins[18].shape[1] // 128
    offsets[3] = offsets[4] + ins[12].shape[0] * ins[12].shape[1] // 128
    offsets[2] = offsets[3] + 2 * ins[9].shape[1] * ins[9].shape[2] // 128
    stores = []
    for i, (p, where) in enumerate(jobs):
        for copy in loads[i]:
            copy.wait()
        if p == 0:
            grad = patch
        elif p == 1:
            top = where[0].start // half_time * n_dp * time_chunk
            grad = jnp.concatenate(
                [time_rows[top + t * half_time : top + (t + 1) * half_time, :] for t in range(per_tile)], 1
            ).astype(F32)
        elif p == 3:
            size = ins[9].shape[1]
            grad = tiles(offsets[3] + where[0] * size * per_tile, size, per_tile)
        elif p == 6:
            grad = tiles(offsets[6] + where[0].start // 128 * width, width, per_tile).T
        else:
            size = ins[3 * p].shape[0]
            grad = tiles(offsets[p] + where[1].start // 128 * size, size, per_tile)
        b = bufs[3 * p : 3 * p + 3]
        index = ... if where is None else where
        values = adam_values(b[0][index], b[1][index], b[2][index], grad, scale)
        for k, value in enumerate(values):
            b[k][index] = value
            copy = pltpu.make_async_copy(view(b[k], where), view(outs[3 * p + k], where), sem_out.at[3 * i + k])
            copy.start()
            stores.append(copy)
    for copy in stores:
        copy.wait()


def call_adam(n_dp, lists, chunks, time_chunk, extra, place, got, params):
    smem = pl.BlockSpec(memory_space=pltpu.SMEM)
    vmem = pl.BlockSpec(memory_space=pltpu.VMEM)
    anywhere = pl.BlockSpec(memory_space=pl.ANY)
    n_jobs = 3 * 16
    return pl.pallas_call(
        partial(adam_kernel, n_dp, lists, chunks, time_chunk, extra),
        out_shape=[jax.ShapeDtypeStruct(w.shape, F32) for w in params] + [jax.ShapeDtypeStruct((8, 128), F32)],
        in_specs=[smem] + [anywhere] * (len(got) + len(params)),
        out_specs=[anywhere] * len(params) + [vmem],
        scratch_shapes=[pltpu.VMEM(w.shape, F32) for w in params]
        + [
            pltpu.VMEM((n_dp * sum(chunks), 128), BF16),
            pltpu.VMEM((2 * n_dp * time_chunk, 128), BF16),
            pltpu.VMEM((n_dp * 6 * extra, 128), BF16),
            pltpu.SemaphoreType.DMA((n_jobs,)),
            pltpu.SemaphoreType.DMA((n_jobs,)),
            pltpu.SemaphoreType.DMA((6 * n_dp,)),
        ],
        compiler_params=pltpu.CompilerParams(vmem_limit_bytes=VMEM_LIMIT),
        name="adam",
    )(place, *got, *params)


def stage(size, bit):
    return [(i, i ^ (1 << bit)) for i in range(size)]


def bit_order(size, turn):
    bits = list(range(size.bit_length() - 1))
    lead = bits[:3]
    turn %= max(len(lead), 1)
    return lead[turn:] + lead[:turn] + bits[3:]


def halve(streams, exact, size):
    place = lax.axis_index("dp")
    orders = [bit_order(size, turn) for turn in range(len(streams))]
    lefts = [sorted(order, reverse=True) for order in orders]
    last = len(streams) - 1

    def shaped(v):
        return v.reshape(*(2,) * len(orders[0]), *v.shape[1:])

    values = [shaped(v) for v in streams]
    exact = shaped(exact)
    for n in range(len(orders[0])):
        for k in range(len(streams)):
            bit = orders[k][n]
            mine = (place >> bit) & 1
            axis = lefts[k].index(bit)
            lefts[k].remove(bit)

            def halves(v):
                return (
                    lax.dynamic_index_in_dim(v, mine, axis, keepdims=False),
                    lax.dynamic_index_in_dim(v, 1 - mine, axis, keepdims=False),
                )

            keep, give = halves(values[k])
            give = give.astype(BF16)
            if k == last:
                exact, sent = halves(exact)
                coarse = lax.reduce_precision(sent, 8, 7)
                give = jnp.concatenate([give, coarse.astype(BF16), (sent - coarse).astype(BF16)], -2)
            got = lax.ppermute(give, "dp", stage(size, bit)).astype(F32)
            if k == last:
                m, e = keep.shape[-2], exact.shape[-2]
                exact = exact + (got[..., m : m + e, :] + got[..., m + e :, :])
                got = got[..., :m, :]
            values[k] = keep + got
    return values, exact


def gather(values, size, turn):
    held, relatives = values[None], [0]
    pieces = []
    order = bit_order(size, turn)[::-1]
    for n, bit in enumerate(order):
        got = lax.ppermute(held, "dp", stage(size, bit))
        moved = [r ^ (1 << bit) for r in relatives]
        if n == len(order) - 1:
            pieces = [(held, relatives), (got, moved)]
        else:
            held, relatives = jnp.concatenate([held, got], 0), relatives + moved
    return pieces


def shards(
    latents, noise_field, image_tokens, timesteps,
    w_patch, m_patch, v_patch, w_time, m_time, v_time, w_mod, m_mod, v_mod,
    w_qkv, m_qkv, v_qkv, w_out, m_out, v_out, w_up, m_up, v_up, w_down, m_down, v_down,
):
    rows_here, channels, length = latents.shape
    slots = image_tokens.shape[1]
    width = w_patch.shape[2]
    freqs = w_time.shape[0] - width
    core = lax.axis_index("tensor")
    n_dp = lax.axis_size("dp")
    chip_slots = rows_here * slots
    group = w_out.shape[0]
    kept = rows_here // 2
    mirror = [(i, n_dp - 1 - i) for i in range(n_dp)]

    numbers = jnp.concatenate([image_tokens, timesteps], 1)
    numbers = jnp.concatenate([numbers[:kept], lax.ppermute(numbers[kept:], "dp", mirror)], 0)
    level = signal_levels(timesteps)
    starts = running_sum(image_tokens)
    position = jnp.arange(length, dtype=jnp.int32)[None, :, None]
    member = (position >= starts[:, None, :]) & (position < (starts + image_tokens)[:, None, :])
    keep_tok = jnp.sum(jnp.where(member, jnp.sqrt(level)[:, None, :], 0.0), -1)
    fade_tok = jnp.sum(jnp.where(member, jnp.sqrt(1.0 - level)[:, None, :], 0.0), -1)
    noisy = keep_tok[:, None, :] * latents + fade_tok[:, None, :] * noise_field
    payload = jnp.concatenate([noisy.astype(BF16), noise_field.astype(BF16)], 1)
    x_got = lax.ppermute(payload[kept:], "dp", mirror)
    counts, steps = numbers[:, :slots], numbers[:, slots:].reshape(-1)
    tab = image_table(counts, core, length)

    qkv_t, qkv_m, qkv_v = (v.swapaxes(1, 2) for v in (w_qkv, m_qkv, v_qkv))
    halves = []
    for w in (qkv_t[0], w_out, w_up, w_down):
        w = w.astype(BF16)
        halves.extend((w, swap(w)))

    features = time_features(steps, freqs)
    before = precise(features, w_time[:freqs])
    cond = precise(jax.nn.silu(before), w_time[freqs:])
    mod_own = precise(jax.nn.silu(cond), w_mod)
    shift_own = precise(cond, qkv_t[1].T)

    longest = rows_here * length // 2 + max(SIZES) // 2
    room = (longest + TILE - 1) // TILE * TILE + TILE
    *saved, own, other, gfin, sg, loss, modcat, wqkv = call_forward(
        tab, payload[:kept], x_got, (mod_own, swap(mod_own)), (shift_own, swap(shift_own)), w_patch, halves, room
    )
    main_own, main_other, time_own, time_other, gemb, sg_own, sg_other = call_backward(
        tab, modcat, wqkv, saved, sg, chip_slots
    )

    patch = jnp.concatenate([gemb[:channels], gfin[channels:]], 0)
    count_here = 0.5 * channels * jnp.sum(image_tokens).astype(F32)
    facts = jnp.stack([jnp.sum(loss), count_here])
    patch = jnp.concatenate([patch, jnp.pad(facts[None], ((0, 7), (0, width - 2)))], 0)
    slot_grads = (time_own, swap(time_other), sg_own, swap(sg_other))
    term = call_small(term_kernel, cond.shape, "cond_term", *slot_grads, cond, w_mod, qkv_t[1])

    def share(count, multiple):
        return (count + n_dp * multiple - 1) // (n_dp * multiple) * multiple

    time_chunk = share(w_time.shape[0] // 2 * width // 128, 16)
    extra = share(patch.size // 128, 8)
    wide = share(own.shape[0] + (2 * 3 * group + 4 * width) * width // 128, 1)
    most = (wide + 2 * (time_chunk + extra) + 47) // 48 * 16
    chunks = (most, most, max(wide - 2 * most + 15, 16) // 16 * 16)
    rows = call_small(
        pack_kernel, (n_dp * sum(chunks), 128), "pack_grads",
        own, swap(other), main_own, swap(main_other), *slot_grads, cond,
    )
    g_time = call_time(
        n_dp, time_chunk, extra, tab, term, swap(term), before, features, w_time, patch, swap(patch)
    )

    streams, at = [], 0
    for c in chunks:
        streams.append(rows[at : at + n_dp * c].reshape(n_dp, c, 128))
        at += n_dp * c
    parts, exact_part = halve(streams, g_time, n_dp)
    time_part, patch_part = exact_part[:time_chunk], exact_part[time_chunk:]
    squares = sum(jnp.sum(v * v) for v in (*parts, time_part))
    mine = jnp.concatenate([time_part, jnp.full((8, 128), squares, F32)], 0)
    theirs = swap(mine)
    first = core == 0
    both_time = [jnp.where(first, mine, theirs)[:time_chunk], jnp.where(first, theirs, mine)[:time_chunk]]
    lane = jnp.arange(128)[None]
    spot = (jnp.arange(extra)[:, None] == 0) & (lane == 0)
    total = jnp.where(spot, mine[time_chunk, 0] + theirs[time_chunk, 0], 0.0)
    terms, rest = [], jnp.concatenate([patch_part, total], 0)
    for _ in range(3):
        coarse = lax.reduce_precision(rest, 8, 7)
        terms.append(coarse.astype(BF16))
        rest = rest - coarse
    sent = [v.astype(BF16) for v in parts]
    sent[-1] = jnp.concatenate([sent[-1], *(v.astype(BF16) for v in both_time), *terms], 0)
    got, lists = [], []
    for k in range(3):
        pieces = gather(sent[k], n_dp, k)
        lists.append(([len(got) + i for i in range(len(pieces))], [r for _, r in pieces]))
        got.extend(v for v, _ in pieces)
    params = (
        w_patch, m_patch, v_patch, w_time, m_time, v_time, w_mod, m_mod, v_mod,
        qkv_t, qkv_m, qkv_v, w_out, m_out, v_out, w_up, m_up, v_up, w_down, m_down, v_down,
    )
    *updated, stats = call_adam(
        n_dp, lists, chunks, time_chunk, extra, lax.axis_index("dp").reshape(1), got, params
    )
    for k in range(9, 12):
        updated[k] = updated[k].swapaxes(1, 2)
    return (stats[0, 0], stats[0, 1], stats[0, 2], *updated)


def solution(mesh):
    rows, flat, cols = P("dp", None, None), P("dp", None), P(None, "tensor")
    whole, deep, split = P(), P(None, None, "tensor"), P("tensor", None)
    weights = [p for p in (whole, whole, cols, deep, split, cols, split) for _ in range(3)]
    return jax.shard_map(
        shards,
        mesh=mesh,
        in_specs=(rows, rows, flat, flat, *weights),
        out_specs=(whole, whole, whole, *weights),
        check_vma=False,
    )
```

```python
from functools import partial
import math

import jax
import jax.numpy as jnp
import numpy as np
from jax import lax
from jax.experimental import pallas as pl
from jax.experimental.pallas import tpu as pltpu
from jax.sharding import PartitionSpec as P

HEAD_DIM = 64
STEP = 10
PRECISE_MODE = lax.Precision.HIGHEST
NORM_EPS = 1e-06
CLIP_LIMIT = 0.001
LEARN_RATE = 0.03
BETA_FIRST = 0.9
BETA_SECOND = 0.95
ADAM_EPS = 1e-08
WEIGHT_DECAY = 0.1
SIZES = (64, 144, 256)
TILE = 256
SLOT_LANES = 128
GELU_A = math.sqrt(2.0 / math.pi)
GELU_B = 0.044715
VMEM_LIMIT = 60 * 1024 * 1024
F32 = jnp.float32
BF16 = jnp.bfloat16


def precise(left, right):
    return jnp.dot(left, right, precision=PRECISE_MODE)


def dot(left, right):
    return lax.dot_general(left, right, (((1,), (0,)), ((), ())), preferred_element_type=F32)


def dot_nt(left, right):
    return lax.dot_general(left, right, (((1,), (1,)), ((), ())), preferred_element_type=F32)


def normalize(values):
    centre = values - jnp.mean(values, -1, keepdims=True)
    inverse = lax.rsqrt(jnp.mean(centre * centre, -1, keepdims=True) + NORM_EPS)
    return (centre * inverse, inverse)


def norm_back(grad, normed, inverse):
    return inverse * (
        grad
        - jnp.mean(grad, -1, keepdims=True)
        - normed * jnp.mean(grad * normed, -1, keepdims=True)
    )


def position_rows(width):
    quarter = width // 4
    omega = np.exp(-math.log(10000.0) * np.arange(quarter) / quarter)
    parts = []
    for size in SIZES:
        side = math.isqrt(size)
        offset = np.arange(size)
        row_angle = (offset // side)[:, None] * omega
        col_angle = (offset % side)[:, None] * omega
        parts.append(
            np.concatenate(
                [np.sin(row_angle), np.cos(row_angle), np.sin(col_angle), np.cos(col_angle)], -1
            )
        )
    return np.concatenate(parts, 0).astype(np.float32)


def for_sizes(count, body):
    offset = 0
    for size in SIZES:
        pl.when(count == size)(partial(body, size, offset))
        offset += size


def rows_at(start, size, step):
    return pl.ds(pl.multiple_of(start, step), size)


def fill_member(member, dst, size, index):
    lane = lax.broadcasted_iota(jnp.int32, (size, 2 * SLOT_LANES), 1)
    hot = (lane == index) | (lane == index + SLOT_LANES)
    member[rows_at(dst, size, 16), :] = hot.astype(F32).astype(BF16)


def both_heads(pair):
    first = lax.broadcasted_iota(jnp.int32, pair.shape, 1) < HEAD_DIM
    nothing = jnp.zeros_like(pair)
    return jnp.concatenate([jnp.where(first, pair, nothing), jnp.where(first, nothing, pair)], 0)


def own_lanes(rows):
    size = rows.shape[0] // 2
    first = lax.broadcasted_iota(jnp.int32, (size, rows.shape[1]), 1) < HEAD_DIM
    return jnp.where(first, rows[:size], rows[size:])


def step_kernel(
    tab, x_own, x_got, places, mod_own, mod_got, shift_own, shift_got, patch,
    qkv_own, qkv_got, out_own, out_got, up_own, up_got, dn_own, dn_got,
    up_kept, down_kept, out_kept, other, gfin, loss, main_own, main_other, time_own, time_other, gemb, sg_own, sg_other,
    proj, mixed, gmixed, gmid, stream, xtok, lse, sg, modcat, wqkv,
    xrow, member, deriv, active, up_sent, down_sent, gout, shiftcat, wout, w_in, w_fin, gshift,
):
    width = stream.shape[1]
    gqkv = deriv.at[:, : 3 * width]
    low, high, tokens, tiles, core = (tab[3, j] for j in range(5))
    heads = width // HEAD_DIM
    group_heads = heads // 2
    group = width // 2
    half_hidden = up_own.shape[1]
    hidden = 2 * half_hidden
    channels = patch.shape[1]
    chip_slots = mod_own.shape[0]
    at = 0
    for x in (x_own, x_got):
        for r in range(x.shape[0]):
            turned = x[r].astype(F32).T
            xrow[at : at + turned.shape[0], :] = turned.astype(BF16)
            at += turned.shape[0]
    for g, source in enumerate((qkv_own, qkv_got)):
        for h in range(group_heads):
            for part in range(3):
                to = part * width + g * group + h * HEAD_DIM
                start = (3 * h + part) * HEAD_DIM
                wqkv[to : to + HEAD_DIM, :] = source[start : start + HEAD_DIM, :]
    wout[:group, :] = out_own[...]
    wout[group:, :] = out_got[...]
    nothing = jnp.zeros((channels, width), BF16)
    w_in[:channels, :] = patch[0].astype(BF16)
    w_in[channels:, :] = nothing
    w_fin[:channels, :] = nothing
    w_fin[channels:, :] = patch[1].astype(BF16)

    def two_terms(target, values):
        coarse = values.astype(BF16)
        rest = jnp.zeros((SLOT_LANES - chip_slots, values.shape[1]), BF16)
        for base, term in ((0, coarse), (SLOT_LANES, (values - coarse.astype(F32)).astype(BF16))):
            target[base : base + chip_slots, :] = term
            target[base + chip_slots : base + SLOT_LANES, :] = rest

    for half in range(2):
        two_terms(modcat.at[half], jnp.where(core == half, mod_own[...], mod_got[...]))
    two_terms(
        shiftcat,
        jnp.concatenate(
            [
                source[:, (3 * h + part) * HEAD_DIM : (3 * h + part + 1) * HEAD_DIM]
                for part in range(3)
                for source in (shift_own, shift_got)
                for h in range(group_heads)
            ],
            1,
        ),
    )
    parts = (
        (0, up_own, dn_own, up_kept, down_kept),
        (half_hidden, up_got, dn_got, up_sent, down_sent),
    )

    def place_image(i, carry):
        src, dst = tab[1, i], tab[2, i]

        def body(size, offset):
            xtok[rows_at(dst, size, 16), :] = xrow[rows_at(src, size, 16), :]
            stream[rows_at(dst, size, 16), :] = places[offset : offset + size, :]
            fill_member(member, dst, size, i)

        for_sizes(tab[0, i], body)
        return carry

    lax.fori_loop(low, high, place_image, 0)
    tail = rows_at(tokens, TILE, 16)
    for ref in (xtok, stream, member, mixed):
        ref[tail, :] = jnp.zeros((TILE, ref.shape[1]), ref.dtype)
    for ref in (up_kept, down_kept, up_sent, down_sent, gout, gfin, sg, loss, gshift, gemb):
        ref[...] = jnp.zeros(ref.shape, ref.dtype)

    def spread(hot, block):
        return dot(hot, modcat[block // 4, :, block % 4 * width : (block % 4 + 1) * width])

    def project_tile(t, carry):
        r = rows_at(t * TILE, TILE, TILE)
        entering = dot(xtok[r, :], w_in[...]) + stream[r, :]
        stream[r, :] = entering
        hot = member[r, :]
        normed, _ = normalize(entering)
        attn_in = (normed * (1.0 + spread(hot, 1)) + spread(hot, 0)).astype(BF16)
        proj[r, :] = (dot_nt(attn_in, wqkv[...]) + dot(hot, shiftcat[...])).astype(BF16)
        return carry

    lax.fori_loop(0, tiles, project_tile, 0)

    def attend_image(i, carry):
        dst = tab[2, i]

        def body(size, offset):
            r = rows_at(dst, size, 16)
            pairs = range(heads // 2)
            ones = jnp.ones((16, size), BF16)
            scores, weights = [], []
            for p in pairs:
                key = proj[r, width + 128 * p : width + 128 * p + 128]
                scores.append(dot_nt(key, both_heads(proj[r, 128 * p : 128 * p + 128])))
            tops = [jnp.max(v, 0, keepdims=True) for v in scores]
            weights = [jnp.exp((v - top) * HEAD_DIM ** (-0.5)) for v, top in zip(scores, tops)]
            for p in pairs:
                value_t = proj[r, 2 * width + 128 * p : 2 * width + 128 * p + 128].T
                out = dot(jnp.concatenate([value_t, ones], 0), weights[p].astype(BF16))
                total = out[128:129]
                lse[tab[4, i], p : p + 1, : 2 * size] = tops[p] * HEAD_DIM ** (-0.5) + jnp.log(total)
                mixed[r, 128 * p : 128 * p + 128] = own_lanes((out[:128] / total).T).astype(BF16)

        for_sizes(tab[0, i], body)
        return carry

    lax.fori_loop(low, high, attend_image, 0)

    def token_tile(t, carry):
        r = rows_at(t * TILE, TILE, TILE)
        hot = member[r, :]
        hot_t = member[r, :SLOT_LANES].astype(F32).T.astype(BF16)

        def collect(block, value):
            sg[block * SLOT_LANES : (block + 1) * SLOT_LANES, :] += dot(hot_t, value.astype(BF16))

        mixed_tile = mixed[r, :]
        attended = dot(mixed_tile, wout[...])
        gate1 = spread(hot, 2)
        mid = stream[r, :] + gate1 * attended
        normed2, inverse2 = normalize(mid)
        scale2 = spread(hot, 4)
        mlp_in = (normed2 * (1.0 + scale2) + spread(hot, 3)).astype(BF16)
        mlp_out = jnp.zeros((TILE, width), F32)
        for j, wup, wdn, _, _ in parts:
            up = dot(mlp_in, wup[...])
            square = up * up
            bent = jnp.tanh(up * (GELU_A + (GELU_A * GELU_B) * square))
            share = 0.5 + 0.5 * bent
            act = (up * share).astype(BF16)
            active[:, j : j + half_hidden] = act
            deriv[:TILE, j : j + half_hidden] = share + up * (share * (1.0 - share)) * (
                2.0 * GELU_A + (6.0 * GELU_A * GELU_B) * square
            )
            mlp_out = mlp_out + dot(act, wdn[...])
        gate2 = spread(hot, 5)
        leaving = mid + gate2 * mlp_out
        normed3, inverse3 = normalize(leaving)
        scale3 = spread(hot, 7)
        final_in = (normed3 * (1.0 + scale3) + spread(hot, 6)).astype(BF16)
        predicted = dot_nt(final_in, w_fin[...])
        lane = lax.broadcasted_iota(jnp.int32, predicted.shape, 1)
        row = lax.broadcasted_iota(jnp.int32, predicted.shape, 0) + t * TILE
        keep = (lane >= channels) & (row < tokens)
        error = jnp.where(keep, predicted - xtok[r, :].astype(F32), 0.0)
        loss[...] += jnp.sum(error * error, 0, keepdims=True)
        grad_pred = (2.0 * error).astype(BF16)
        gfin[...] += dot(grad_pred.T, final_in)
        grad_final = dot(grad_pred, w_fin[...])
        collect(6, grad_final)
        collect(7, grad_final * normed3)
        grad_out = norm_back(grad_final * (1.0 + scale3), normed3, inverse3)
        collect(5, grad_out * mlp_out)
        grad_mlp = (grad_out * gate2).astype(BF16)
        grad_mlp_t = grad_mlp.T
        mlp_in_t = mlp_in.T
        grad_mlp_in = jnp.zeros((TILE, width), F32)
        for j, wup, wdn, gup, gdn in parts:
            gdn[...] += dot(grad_mlp_t, active[:, j : j + half_hidden])
            grad_act = dot_nt(grad_mlp, wdn[...])
            grad_up = (grad_act * deriv[:TILE, j : j + half_hidden]).astype(BF16)
            gup[...] += dot(mlp_in_t, grad_up)
            grad_mlp_in = grad_mlp_in + dot_nt(grad_up, wup[...])
        collect(3, grad_mlp_in)
        collect(4, grad_mlp_in * normed2)
        grad_mid = grad_out + norm_back(grad_mlp_in * (1.0 + scale2), normed2, inverse2)
        gmid[r, :] = grad_mid
        collect(2, grad_mid * attended)
        grad_attended = (grad_mid * gate1).astype(BF16)
        gout[...] += dot(mixed_tile.T, grad_attended)
        gmixed[r, :] = dot_nt(grad_attended, wout[...]).astype(BF16)
        return carry

    lax.fori_loop(0, tiles, token_tile, 0)
    gqkv[...] = jnp.zeros(gqkv.shape, F32)
    out_kept[...] = gout[:group, :]
    at = 0
    for ref in (up_sent, down_sent):
        for j in range(0, half_hidden, 128):
            other[at : at + width, :] = ref[:, j : j + 128].astype(BF16)
            at += width
    for j in range(0, width, 128):
        other[at : at + group, :] = gout[group:, j : j + 128].astype(BF16)
        at += group
    every = jnp.ones((8, 2 * HEAD_DIM), BF16)

    def unattend_image(i, carry):
        dst = tab[2, i]

        def body(size, offset):
            r = rows_at(dst, size, 16)
            pairs = range(heads // 2)
            grads = [both_heads(gmixed[r, 128 * p : 128 * p + 128]) for p in pairs]
            queries = [both_heads(proj[r, 128 * p : 128 * p + 128]) for p in pairs]
            inners, probs, drops = [], [], []
            for p in pairs:
                out = mixed[r, 128 * p : 128 * p + 128].astype(F32)
                product = grads[p].astype(F32) * jnp.concatenate([out, out], 0)
                coarse = product.astype(BF16)
                fine = (product - coarse.astype(F32)).astype(BF16)
                inners.append((dot_nt(every, coarse) + dot_nt(every, fine))[0:1])
            for p in pairs:
                scores = dot_nt(proj[r, width + 128 * p : width + 128 * p + 128], queries[p])
                probs.append(jnp.exp(scores * HEAD_DIM ** (-0.5) - lse[tab[4, i], p : p + 1, : 2 * size]))
            for p in pairs:
                grad_probs = dot_nt(proj[r, 2 * width + 128 * p : 2 * width + 128 * p + 128], grads[p])
                drops.append((probs[p] * (grad_probs - inners[p])).astype(BF16))
            for p in pairs:
                key_t = proj[r, width + 128 * p : width + 128 * p + 128].T
                grad_value = dot(probs[p].astype(BF16), grads[p])
                grad_key = dot(drops[p], queries[p]) * HEAD_DIM ** (-0.5)
                grad_query = own_lanes(dot(key_t, drops[p]).T) * HEAD_DIM ** (-0.5)
                for part, value in enumerate((grad_query, grad_key, grad_value)):
                    at = part * width + 128 * p
                    proj[r, at : at + 128] = value.astype(BF16)

        for_sizes(tab[0, i], body)
        return carry

    lax.fori_loop(low, high, unattend_image, 0)

    def last_tile(t, carry):
        r = rows_at(t * TILE, TILE, TILE)
        hot = member[r, :]
        hot_t = member[r, :SLOT_LANES].astype(F32).T.astype(BF16)

        def collect(block, value):
            sg[block * SLOT_LANES : (block + 1) * SLOT_LANES, :] += dot(hot_t, value.astype(BF16))

        normed, inverse = normalize(stream[r, :])
        scale1 = spread(hot, 1)
        attn_in = (normed * (1.0 + scale1) + spread(hot, 0)).astype(BF16)
        grad_proj = proj[r, :]
        gqkv[...] += dot(attn_in.T, grad_proj)
        gshift[...] += dot(hot_t, grad_proj)
        grad_attn_in = dot(grad_proj, wqkv[...])
        collect(0, grad_attn_in)
        collect(1, grad_attn_in * normed)
        grad_in = gmid[r, :] + norm_back(grad_attn_in * (1.0 + scale1), normed, inverse)
        gemb[...] += dot(xtok[r, :].T, grad_in.astype(BF16))
        return carry

    lax.fori_loop(0, tiles, last_tile, 0)
    turned = gqkv[...].T
    kept = time_own.shape[0]
    for g, (main, shift) in enumerate(((main_own, time_own), (main_other, time_other))):
        pieces = []
        for h in range(heads // 2):
            for part in range(3):
                start = part * width + g * group + h * HEAD_DIM
                to = (3 * h + part) * HEAD_DIM
                main[to : to + HEAD_DIM, :] = turned[start : start + HEAD_DIM, :].astype(main.dtype)
                pieces.append(gshift[:kept, start : start + HEAD_DIM])
        shift[...] = jnp.concatenate(pieces, 1)
    for part in range(4):
        lower = sg[part * SLOT_LANES : part * SLOT_LANES + kept, :]
        upper = sg[(4 + part) * SLOT_LANES : (4 + part) * SLOT_LANES + kept, :]
        sg_own[part] = jnp.where(core == 0, lower, upper)
        sg_other[part] = jnp.where(core == 0, upper, lower)


def call_step(tab, x_own, x_got, mods, shifts, patch, weights):
    rows_kept, channels2, length = x_own.shape
    kept = mods[0].shape[0]
    width, half_hidden = weights[4].shape
    group = width // 2
    slots = SLOT_LANES
    longest = rows_kept * length + max(SIZES) // 2
    room = (longest + TILE + 15) // 16 * 16
    vmem = pl.BlockSpec(memory_space=pltpu.VMEM)
    shape = jax.ShapeDtypeStruct
    outs = (
        shape((width, half_hidden), F32),
        shape((width, half_hidden), F32),
        shape((group, width), F32),
        shape((width * (2 * half_hidden + group) // 128, 128), BF16),
        shape((channels2, width), F32),
        shape((1, channels2), F32),
        shape((3 * group, width), F32),
        shape((3 * group, width), BF16),
        shape((kept, 3 * group), F32),
        shape((kept, 3 * group), F32),
        shape((channels2, width), F32),
        shape((4, kept, width), F32),
        shape((4, kept, width), F32),
    )
    return pl.pallas_call(
        step_kernel,
        out_shape=outs,
        in_specs=[pl.BlockSpec(memory_space=pltpu.SMEM)] + [vmem] * 16,
        out_specs=[vmem] * len(outs),
        scratch_shapes=[
            pltpu.VMEM((room, 3 * width), BF16),
            pltpu.VMEM((room, width), BF16),
            pltpu.VMEM((room, width), BF16),
            pltpu.VMEM((room, width), F32),
            pltpu.VMEM((room, width), F32),
            pltpu.VMEM((room, channels2), BF16),
            pltpu.VMEM((room // min(SIZES), 8, 2 * max(SIZES)), F32),
            pltpu.VMEM((8 * slots, width), F32),
            pltpu.VMEM((2, 2 * slots, 4 * width), BF16),
            pltpu.VMEM((3 * width, width), BF16),
            pltpu.VMEM((2 * rows_kept * length, channels2), BF16),
            pltpu.VMEM((room, 2 * slots), BF16),
            pltpu.VMEM((max(TILE, width), max(2 * half_hidden, 3 * width)), F32),
            pltpu.VMEM((TILE, 2 * half_hidden), BF16),
            pltpu.VMEM((width, half_hidden), F32),
            pltpu.VMEM((width, half_hidden), F32),
            pltpu.VMEM((width, width), F32),
            pltpu.VMEM((2 * slots, 3 * width), BF16),
            pltpu.VMEM((width, width), BF16),
            pltpu.VMEM((channels2, width), BF16),
            pltpu.VMEM((channels2, width), BF16),
            pltpu.VMEM((slots, 3 * width), F32),
        ],
        compiler_params=pltpu.CompilerParams(vmem_limit_bytes=VMEM_LIMIT),
        name="step",
    )(tab, x_own, x_got, jnp.asarray(position_rows(width)), *mods, *shifts, patch, *weights)


def signal_levels(steps):
    index = jnp.arange(1000, dtype=jnp.int32)
    betas = 0.0001 + 0.0199 * index.astype(F32) / 999.0
    logs = jnp.log(1.0 - betas)
    return jnp.exp(jnp.sum(jnp.where(index <= steps[..., None], logs, 0.0), -1))


def time_features(steps, freqs):
    half = freqs // 2
    rates = jnp.exp(-math.log(10000.0) * jnp.arange(half, dtype=F32) / half)
    angle = steps.astype(F32)[..., None] * rates
    return jnp.concatenate([jnp.cos(angle), jnp.sin(angle)], -1)


def running_sum(values):
    size = values.shape[-1]
    before = np.arange(size)[:, None] > np.arange(size)[None, :]
    return jnp.sum(jnp.where(before, values[..., None, :], 0), -1)


def image_table(counts, core, length):
    rows_here, slots = counts.shape
    row_start = running_sum(counts) + length * jnp.arange(rows_here, dtype=jnp.int32)[:, None]
    flat = counts.reshape(-1)
    start = running_sum(flat)
    total = jnp.sum(flat)
    index = jnp.arange(flat.shape[0], dtype=jnp.int32)
    first_half = jnp.sum((2 * start + flat <= total).astype(jnp.int32))
    low = jnp.where(core == 0, 0, first_half)
    high = jnp.where(core == 0, first_half, flat.shape[0])
    base = jnp.sum(jnp.where(index < low, flat, 0))
    tokens = jnp.sum(jnp.where((index >= low) & (index < high), flat, 0))
    tiles = (tokens + TILE - 1) // TILE
    facts = jnp.stack([low, high, tokens, tiles, core]).astype(jnp.int32)
    pad = lambda v: jnp.pad(v.astype(jnp.int32), (0, 128 - v.shape[0]))
    return jnp.stack([pad(flat), pad(row_start.reshape(-1)), pad(start - base), pad(facts), pad((start - base) // min(SIZES))])


def swap(value):
    return lax.ppermute(value, "tensor", [(0, 1), (1, 0)])


def fine_dot(left, right, dims):
    left_a, right_a = left.astype(BF16), right.astype(BF16)
    left_b = (left - left_a.astype(F32)).astype(BF16)
    right_b = (right - right_a.astype(F32)).astype(BF16)
    product = partial(lax.dot_general, dimension_numbers=(dims, ((), ())), preferred_element_type=F32)
    return product(left_a, right_a) + (product(left_a, right_b) + product(left_b, right_a))


PLAIN, TURNED = ((1,), (0,)), ((1,), (1,))


def silu_slope(value):
    gate = 1.0 / (1.0 + jnp.exp(-value))
    return gate * (1.0 + value * (1.0 - gate))


def term_kernel(shift_own, shift_got, sg_own, sg_got, cond, w_mod, w_time, term):
    width = w_mod.shape[0]
    total = jnp.zeros(cond.shape, F32)
    for part in range(4):
        grad = sg_own[part] + sg_got[part]
        total = total + fine_dot(grad, w_mod[:, part * width : (part + 1) * width], TURNED)
    term[...] = total * silu_slope(cond[...]) + fine_dot(shift_own[...] + shift_got[...], w_time[...], PLAIN)


def pack_kernel(up, down, out, got, main_own, main_got, shift_own, shift_got, sg_own, sg_got, cond, rows):
    width = cond.shape[1]
    at = 0
    for ref in (up, down, out):
        for j in range(0, ref.shape[1], 128):
            to = slice(at, at + ref.shape[0])
            rows[to, :] = ref[:, j : j + 128] + got[to, :].astype(F32)
            at = to.stop
    values = cond[...]
    act_t = (values / (1.0 + jnp.exp(-values))).T
    shift_t = (shift_own[...] + shift_got[...]).T

    def put(block):
        nonlocal at
        for j in range(0, width, 128):
            rows[at : at + block.shape[0], :] = block[:, j : j + 128]
            at += block.shape[0]

    put(main_own[...] + main_got[...].astype(F32))
    put(fine_dot(shift_t, values, PLAIN))
    for part in range(4):
        put(fine_dot(act_t, sg_own[part] + sg_got[part], PLAIN))
    rows[at:, :] = jnp.zeros((rows.shape[0] - at, 128), F32)


def time_kernel(time_chunk, extra, tab, term, got, before, features, w_time, patch, patch_got, rows, flat):
    width = w_time.shape[1]
    freqs = features.shape[1]
    grad_cond = term[...] + got[...]
    values = before[...]
    hidden = values / (1.0 + jnp.exp(-values))
    second = fine_dot(hidden.T, grad_cond, PLAIN)
    inner = fine_dot(grad_cond, w_time[freqs:, :], TURNED) * silu_slope(values)
    first = fine_dot(features[...].T, inner, PLAIN)
    half = w_time.shape[0] // 2
    both = jnp.concatenate([first, second], 0)
    mine = jnp.where(tab[3, 4] == 0, both[:half], both[half:])
    shared = patch[...] + patch_got[...]
    n_dp = rows.shape[0]
    flat[...] = jnp.zeros(flat.shape, F32)
    patch_at = n_dp * time_chunk
    for t in range(width // 128):
        flat[t * half : (t + 1) * half, :] = mine[:, t * 128 : (t + 1) * 128]
        to = patch_at + t * shared.shape[0]
        flat[to : to + shared.shape[0], :] = shared[:, t * 128 : (t + 1) * 128]
    for d in range(n_dp):
        rows[d, :time_chunk, :] = flat[d * time_chunk : (d + 1) * time_chunk, :]
        rows[d, time_chunk:, :] = flat[patch_at + d * extra : patch_at + (d + 1) * extra, :]


def call_time(n_dp, time_chunk, extra, table, *args):
    vmem = pl.BlockSpec(memory_space=pltpu.VMEM)
    return pl.pallas_call(
        partial(time_kernel, time_chunk, extra),
        out_shape=jax.ShapeDtypeStruct((n_dp, time_chunk + extra, 128), F32),
        in_specs=[pl.BlockSpec(memory_space=pltpu.SMEM)] + [vmem] * len(args),
        out_specs=vmem,
        scratch_shapes=[pltpu.VMEM((n_dp * (time_chunk + extra), 128), F32)],
        compiler_params=pltpu.CompilerParams(vmem_limit_bytes=VMEM_LIMIT),
        name="time_grads",
    )(table, *args)


def call_small(kernel, shape, name, *args):
    vmem = pl.BlockSpec(memory_space=pltpu.VMEM)
    return pl.pallas_call(
        kernel,
        out_shape=jax.ShapeDtypeStruct(shape, F32),
        in_specs=[vmem] * len(args),
        out_specs=vmem,
        compiler_params=pltpu.CompilerParams(vmem_limit_bytes=VMEM_LIMIT),
        name=name,
    )(*args)


def adam_values(weight, first, second, grad, factor):
    clipped = grad * factor
    first = BETA_FIRST * first + (1.0 - BETA_FIRST) * clipped
    second = BETA_SECOND * second + (1.0 - BETA_SECOND) * clipped * clipped
    root = jnp.sqrt(second * (1.0 / (1.0 - BETA_SECOND**STEP))) + ADAM_EPS
    step = first * (1.0 / (1.0 - BETA_FIRST**STEP)) / root
    return (first, second, weight - LEARN_RATE * (step + WEIGHT_DECAY * weight))


def adam_kernel(n_dp, lists, chunks, time_chunk, extra, place, *refs):
    n_got = sum(len(pieces) for pieces, _ in lists)
    got, refs = refs[:n_got], refs[n_got:]
    ins, outs, stats, bufs = refs[:21], refs[21:42], refs[42], refs[43:64]
    rows, time_rows, extra_rows, sem_in, sem_out, sem_got = refs[64:]
    width = ins[3].shape[1]
    here = place[0]
    jobs = []
    for p in range(7):
        shape = ins[3 * p].shape
        if p == 0:
            jobs.append((p, None))
        elif p == 3:
            jobs.extend((p, (i,)) for i in range(2))
        else:
            step = shape[0] // 2 if p == 1 else min(width, shape[0])
            jobs.extend(
                (p, (pl.ds(r, step), pl.ds(j, width))) for r in range(0, shape[0], step) for j in range(0, shape[1], width)
            )

    def view(ref, where):
        return ref if where is None else ref.at[where]

    loads = []
    for i, (p, where) in enumerate(jobs):
        group = []
        for k in range(3):
            copy = pltpu.make_async_copy(
                view(ins[3 * p + k], where), view(bufs[3 * p + k], where), sem_in.at[3 * i + k]
            )
            copy.start()
            group.append(copy)
        loads.append(group)
    arrivals = []
    base = 0
    for stream, ((pieces, order), chunk) in enumerate(zip(lists, chunks)):
        for source, relatives in zip(pieces, order):
            for j, relative in enumerate(relatives):
                owner = here ^ relative
                parts = [(0, chunk, rows, base + owner * chunk)]
                if stream == len(chunks) - 1:
                    parts.append((chunk, time_chunk, time_rows, owner * time_chunk))
                    parts.append((chunk + time_chunk, time_chunk, time_rows, (n_dp + owner) * time_chunk))
                    parts.append((chunk + 2 * time_chunk, 6 * extra, extra_rows, owner * 6 * extra))
                for start, size, target, at in parts:
                    copy = pltpu.make_async_copy(
                        got[source].at[j, pl.ds(start, size), :],
                        target.at[pl.ds(pl.multiple_of(at, 16), size), :],
                        sem_got.at[len(arrivals)],
                    )
                    copy.start()
                    arrivals.append(copy)
        base += n_dp * chunk
    for copy in arrivals:
        copy.wait()
    shards = []
    squares = jnp.zeros((1, 128), F32)
    for owner in range(n_dp):
        at = owner * 6 * extra
        terms = [extra_rows[at + k * 2 * extra : at + (k + 1) * 2 * extra, :].astype(F32) for k in range(3)]
        whole = terms[0] + terms[1] + terms[2]
        shards.append(whole[:extra])
        squares = squares + whole[extra : extra + 1]
    shared = jnp.concatenate(shards, 0)
    each = 2 * ins[0].shape[1] + 8
    patch = jnp.concatenate([shared[t * each : t * each + each - 8] for t in range(width // 128)], 1)
    facts = shared[each - 8 : each - 7]
    loss, count = facts[:, 0:1], facts[:, 1:2]
    squares = jnp.sum(squares, 1, keepdims=True)
    squares = squares + jnp.sum(jnp.sum(patch * patch, 1, keepdims=True), 0, keepdims=True)
    grad_norm = jnp.sqrt(squares) / count
    scale = jnp.minimum(1.0, CLIP_LIMIT / grad_norm) / count
    lane = lax.broadcasted_iota(jnp.int32, stats.shape, 1)
    stats[...] = jnp.where(lane == 0, loss, jnp.where(lane == 1, count, grad_norm))
    patch = patch.reshape(ins[0].shape)

    def tiles(at, size, count):
        return jnp.concatenate([rows[at + i * size : at + (i + 1) * size, :] for i in range(count)], 1).astype(F32)

    per_tile = width // 128
    half_time = ins[3].shape[0] // 2
    offsets = {5: 0}
    offsets[6] = ins[15].shape[0] * ins[15].shape[1] // 128
    offsets[4] = offsets[6] + ins[18].shape[0] * ins[18].shape[1] // 128
    offsets[3] = offsets[4] + ins[12].shape[0] * ins[12].shape[1] // 128
    offsets[2] = offsets[3] + 2 * ins[9].shape[1] * ins[9].shape[2] // 128
    stores = []
    for i, (p, where) in enumerate(jobs):
        for copy in loads[i]:
            copy.wait()
        if p == 0:
            grad = patch
        elif p == 1:
            top = where[0].start // half_time * n_dp * time_chunk
            grad = jnp.concatenate(
                [time_rows[top + t * half_time : top + (t + 1) * half_time, :] for t in range(per_tile)], 1
            ).astype(F32)
        elif p == 3:
            size = ins[9].shape[1]
            grad = tiles(offsets[3] + where[0] * size * per_tile, size, per_tile)
        elif p == 6:
            grad = tiles(offsets[6] + where[0].start // 128 * width, width, per_tile).T
        else:
            size = ins[3 * p].shape[0]
            grad = tiles(offsets[p] + where[1].start // 128 * size, size, per_tile)
        b = bufs[3 * p : 3 * p + 3]
        index = ... if where is None else where
        values = adam_values(b[0][index], b[1][index], b[2][index], grad, scale)
        for k, value in enumerate(values):
            b[k][index] = value
            copy = pltpu.make_async_copy(view(b[k], where), view(outs[3 * p + k], where), sem_out.at[3 * i + k])
            copy.start()
            stores.append(copy)
    for copy in stores:
        copy.wait()


def call_adam(n_dp, lists, chunks, time_chunk, extra, place, got, params):
    smem = pl.BlockSpec(memory_space=pltpu.SMEM)
    vmem = pl.BlockSpec(memory_space=pltpu.VMEM)
    anywhere = pl.BlockSpec(memory_space=pl.ANY)
    n_jobs = 3 * 16
    return pl.pallas_call(
        partial(adam_kernel, n_dp, lists, chunks, time_chunk, extra),
        out_shape=[jax.ShapeDtypeStruct(w.shape, F32) for w in params] + [jax.ShapeDtypeStruct((8, 128), F32)],
        in_specs=[smem] + [anywhere] * (len(got) + len(params)),
        out_specs=[anywhere] * len(params) + [vmem],
        scratch_shapes=[pltpu.VMEM(w.shape, F32) for w in params]
        + [
            pltpu.VMEM((n_dp * sum(chunks), 128), BF16),
            pltpu.VMEM((2 * n_dp * time_chunk, 128), BF16),
            pltpu.VMEM((n_dp * 6 * extra, 128), BF16),
            pltpu.SemaphoreType.DMA((n_jobs,)),
            pltpu.SemaphoreType.DMA((n_jobs,)),
            pltpu.SemaphoreType.DMA((6 * n_dp,)),
        ],
        compiler_params=pltpu.CompilerParams(vmem_limit_bytes=VMEM_LIMIT),
        name="adam",
    )(place, *got, *params)


def stage(size, bit):
    return [(i, i ^ (1 << bit)) for i in range(size)]


def bit_order(size, turn):
    bits = list(range(size.bit_length() - 1))
    lead = bits[:3]
    turn %= max(len(lead), 1)
    return lead[turn:] + lead[:turn] + bits[3:]


def halve(streams, exact, size):
    place = lax.axis_index("dp")
    orders = [bit_order(size, turn) for turn in range(len(streams))]
    lefts = [sorted(order, reverse=True) for order in orders]
    last = len(streams) - 1

    def shaped(v):
        return v.reshape(*(2,) * len(orders[0]), *v.shape[1:])

    values = [shaped(v) for v in streams]
    exact = shaped(exact)
    for n in range(len(orders[0])):
        for k in range(len(streams)):
            bit = orders[k][n]
            mine = (place >> bit) & 1
            axis = lefts[k].index(bit)
            lefts[k].remove(bit)

            def halves(v):
                return (
                    lax.dynamic_index_in_dim(v, mine, axis, keepdims=False),
                    lax.dynamic_index_in_dim(v, 1 - mine, axis, keepdims=False),
                )

            keep, give = halves(values[k])
            give = give.astype(BF16)
            if k == last:
                exact, sent = halves(exact)
                coarse = lax.reduce_precision(sent, 8, 7)
                give = jnp.concatenate([give, coarse.astype(BF16), (sent - coarse).astype(BF16)], -2)
            got = lax.ppermute(give, "dp", stage(size, bit)).astype(F32)
            if k == last:
                m, e = keep.shape[-2], exact.shape[-2]
                exact = exact + (got[..., m : m + e, :] + got[..., m + e :, :])
                got = got[..., :m, :]
            values[k] = keep + got
    return values, exact


def gather(values, size, turn):
    held, relatives = values[None], [0]
    pieces = []
    order = bit_order(size, turn)[::-1]
    for n, bit in enumerate(order):
        got = lax.ppermute(held, "dp", stage(size, bit))
        moved = [r ^ (1 << bit) for r in relatives]
        if n == len(order) - 1:
            pieces = [(held, relatives), (got, moved)]
        else:
            held, relatives = jnp.concatenate([held, got], 0), relatives + moved
    return pieces


def shards(
    latents, noise_field, image_tokens, timesteps,
    w_patch, m_patch, v_patch, w_time, m_time, v_time, w_mod, m_mod, v_mod,
    w_qkv, m_qkv, v_qkv, w_out, m_out, v_out, w_up, m_up, v_up, w_down, m_down, v_down,
):
    rows_here, channels, length = latents.shape
    slots = image_tokens.shape[1]
    width = w_patch.shape[2]
    freqs = w_time.shape[0] - width
    core = lax.axis_index("tensor")
    n_dp = lax.axis_size("dp")
    chip_slots = rows_here * slots
    group = w_out.shape[0]
    kept = rows_here // 2
    mirror = [(i, n_dp - 1 - i) for i in range(n_dp)]

    numbers = jnp.concatenate([image_tokens, timesteps], 1)
    numbers = jnp.concatenate([numbers[:kept], lax.ppermute(numbers[kept:], "dp", mirror)], 0)
    level = signal_levels(timesteps)
    starts = running_sum(image_tokens)
    position = jnp.arange(length, dtype=jnp.int32)[None, :, None]
    member = (position >= starts[:, None, :]) & (position < (starts + image_tokens)[:, None, :])
    keep_tok = jnp.sum(jnp.where(member, jnp.sqrt(level)[:, None, :], 0.0), -1)
    fade_tok = jnp.sum(jnp.where(member, jnp.sqrt(1.0 - level)[:, None, :], 0.0), -1)
    noisy = keep_tok[:, None, :] * latents + fade_tok[:, None, :] * noise_field
    payload = jnp.concatenate([noisy.astype(BF16), noise_field.astype(BF16)], 1)
    x_got = lax.ppermute(payload[kept:], "dp", mirror)
    counts, steps = numbers[:, :slots], numbers[:, slots:].reshape(-1)
    tab = image_table(counts, core, length)

    qkv_t, qkv_m, qkv_v = (v.swapaxes(1, 2) for v in (w_qkv, m_qkv, v_qkv))
    halves = []
    for w in (qkv_t[0], w_out, w_up, w_down):
        w = w.astype(BF16)
        halves.extend((w, swap(w)))

    features = time_features(steps, freqs)
    before = precise(features, w_time[:freqs])
    cond = precise(jax.nn.silu(before), w_time[freqs:])
    mod_own = precise(jax.nn.silu(cond), w_mod)
    shift_own = precise(cond, qkv_t[1].T)

    up, down, out, other, gfin, loss, main_own, main_other, time_own, time_other, gemb, sg_own, sg_other = call_step(
        tab, payload[:kept], x_got, (mod_own, swap(mod_own)), (shift_own, swap(shift_own)), w_patch, halves
    )

    patch = jnp.concatenate([gemb[:channels], gfin[channels:]], 0)
    count_here = 0.5 * channels * jnp.sum(image_tokens).astype(F32)
    facts = jnp.stack([jnp.sum(loss), count_here])
    patch = jnp.concatenate([patch, jnp.pad(facts[None], ((0, 7), (0, width - 2)))], 0)
    slot_grads = (time_own, swap(time_other), sg_own, swap(sg_other))
    term = call_small(term_kernel, cond.shape, "cond_term", *slot_grads, cond, w_mod, qkv_t[1])

    def share(count, multiple):
        return (count + n_dp * multiple - 1) // (n_dp * multiple) * multiple

    time_chunk = share(w_time.shape[0] // 2 * width // 128, 16)
    extra = share(patch.size // 128, 8)
    wide = share(other.shape[0] + (2 * 3 * group + 4 * width) * width // 128, 1)
    most = (wide + 2 * (time_chunk + extra) + 47) // 48 * 16
    chunks = (most, most, max(wide - 2 * most + 15, 16) // 16 * 16)
    rows = call_small(
        pack_kernel, (n_dp * sum(chunks), 128), "pack_grads",
        up, down, out, swap(other), main_own, swap(main_other), *slot_grads, cond,
    )
    g_time = call_time(
        n_dp, time_chunk, extra, tab, term, swap(term), before, features, w_time, patch, swap(patch)
    )

    streams, at = [], 0
    for c in chunks:
        streams.append(rows[at : at + n_dp * c].reshape(n_dp, c, 128))
        at += n_dp * c
    parts, exact_part = halve(streams, g_time, n_dp)
    time_part, patch_part = exact_part[:time_chunk], exact_part[time_chunk:]
    squares = sum(jnp.sum(v * v) for v in (*parts, time_part))
    mine = jnp.concatenate([time_part, jnp.full((8, 128), squares, F32)], 0)
    theirs = swap(mine)
    first = core == 0
    both_time = [jnp.where(first, mine, theirs)[:time_chunk], jnp.where(first, theirs, mine)[:time_chunk]]
    lane = jnp.arange(128)[None]
    spot = (jnp.arange(extra)[:, None] == 0) & (lane == 0)
    total = jnp.where(spot, mine[time_chunk, 0] + theirs[time_chunk, 0], 0.0)
    terms, rest = [], jnp.concatenate([patch_part, total], 0)
    for _ in range(3):
        coarse = lax.reduce_precision(rest, 8, 7)
        terms.append(coarse.astype(BF16))
        rest = rest - coarse
    sent = [v.astype(BF16) for v in parts]
    sent[-1] = jnp.concatenate([sent[-1], *(v.astype(BF16) for v in both_time), *terms], 0)
    got, lists = [], []
    for k in range(3):
        pieces = gather(sent[k], n_dp, k)
        lists.append(([len(got) + i for i in range(len(pieces))], [r for _, r in pieces]))
        got.extend(v for v, _ in pieces)
    params = (
        w_patch, m_patch, v_patch, w_time, m_time, v_time, w_mod, m_mod, v_mod,
        qkv_t, qkv_m, qkv_v, w_out, m_out, v_out, w_up, m_up, v_up, w_down, m_down, v_down,
    )
    *updated, stats = call_adam(
        n_dp, lists, chunks, time_chunk, extra, lax.axis_index("dp").reshape(1), got, params
    )
    for k in range(9, 12):
        updated[k] = updated[k].swapaxes(1, 2)
    return (stats[0, 0], stats[0, 1], stats[0, 2], *updated)


def solution(mesh):
    rows, flat, cols = P("dp", None, None), P("dp", None), P(None, "tensor")
    whole, deep, split = P(), P(None, None, "tensor"), P("tensor", None)
    weights = [p for p in (whole, whole, cols, deep, split, cols, split) for _ in range(3)]
    return jax.shard_map(
        shards,
        mesh=mesh,
        in_specs=(rows, rows, flat, flat, *weights),
        out_specs=(whole, whole, whole, *weights),
        check_vma=False,
    )
```

```python
from functools import partial
import math

import jax
import jax.numpy as jnp
import numpy as np
from jax import lax
from jax.experimental import pallas as pl
from jax.experimental.pallas import tpu as pltpu
from jax.sharding import PartitionSpec as P

HEAD_DIM = 64
STEP = 10
PRECISE_MODE = lax.Precision.HIGHEST
NORM_EPS = 1e-06
CLIP_LIMIT = 0.001
LEARN_RATE = 0.03
BETA_FIRST = 0.9
BETA_SECOND = 0.95
ADAM_EPS = 1e-08
WEIGHT_DECAY = 0.1
SIZES = (64, 144, 256)
TILE = 256
SLOT_LANES = 128
GELU_A = math.sqrt(2.0 / math.pi)
GELU_B = 0.044715
VMEM_LIMIT = 60 * 1024 * 1024
F32 = jnp.float32
BF16 = jnp.bfloat16


def precise(left, right):
    return jnp.dot(left, right, precision=PRECISE_MODE)


def dot(left, right):
    return lax.dot_general(left, right, (((1,), (0,)), ((), ())), preferred_element_type=F32)


def dot_nt(left, right):
    return lax.dot_general(left, right, (((1,), (1,)), ((), ())), preferred_element_type=F32)


def normalize(values):
    centre = values - jnp.mean(values, -1, keepdims=True)
    inverse = lax.rsqrt(jnp.mean(centre * centre, -1, keepdims=True) + NORM_EPS)
    return (centre * inverse, inverse)


def norm_back(grad, normed, inverse):
    return inverse * (
        grad
        - jnp.mean(grad, -1, keepdims=True)
        - normed * jnp.mean(grad * normed, -1, keepdims=True)
    )


def position_rows(width):
    quarter = width // 4
    omega = np.exp(-math.log(10000.0) * np.arange(quarter) / quarter)
    parts = []
    for size in SIZES:
        side = math.isqrt(size)
        offset = np.arange(size)
        row_angle = (offset // side)[:, None] * omega
        col_angle = (offset % side)[:, None] * omega
        parts.append(
            np.concatenate(
                [np.sin(row_angle), np.cos(row_angle), np.sin(col_angle), np.cos(col_angle)], -1
            )
        )
    return np.concatenate(parts, 0).astype(np.float32)


def for_sizes(count, body):
    offset = 0
    for size in SIZES:
        pl.when(count == size)(partial(body, size, offset))
        offset += size


def rows_at(start, size, step):
    return pl.ds(pl.multiple_of(start, step), size)


def fill_member(member, dst, size, index):
    lane = lax.broadcasted_iota(jnp.int32, (size, 2 * SLOT_LANES), 1)
    hot = (lane == index) | (lane == index + SLOT_LANES)
    member[rows_at(dst, size, 16), :] = hot.astype(F32).astype(BF16)


def both_heads(pair):
    first = lax.broadcasted_iota(jnp.int32, pair.shape, 1) < HEAD_DIM
    nothing = jnp.zeros_like(pair)
    return jnp.concatenate([jnp.where(first, pair, nothing), jnp.where(first, nothing, pair)], 0)


def own_lanes(rows):
    size = rows.shape[0] // 2
    first = lax.broadcasted_iota(jnp.int32, (size, rows.shape[1]), 1) < HEAD_DIM
    return jnp.where(first, rows[:size], rows[size:])


def step_kernel(
    tab, x_own, x_got, places, mod_own, mod_got, shift_own, shift_got, patch,
    qkv_own, qkv_got, out_own, out_got, up_own, up_got, dn_own, dn_got,
    up_kept, down_kept, out_kept, other, gfin, loss, main_own, main_other, time_own, time_other, gemb, sg_own, sg_other,
    proj, mixed, gmixed, gmid, stream, xtok, lse, sg, modcat, wqkv,
    xrow, member, deriv, active, up_sent, down_sent, gout, shiftcat, wout, w_in, w_fin, gshift,
):
    width = stream.shape[1]
    gqkv = deriv.at[:, : 3 * width]
    low, high, tokens, tiles, core = (tab[3, j] for j in range(5))
    heads = width // HEAD_DIM
    group_heads = heads // 2
    group = width // 2
    half_hidden = up_own.shape[1]
    hidden = 2 * half_hidden
    channels = patch.shape[1]
    chip_slots = mod_own.shape[0]
    at = 0
    for x in (x_own, x_got):
        for r in range(x.shape[0]):
            turned = x[r].astype(F32).T
            xrow[at : at + turned.shape[0], :] = turned.astype(BF16)
            at += turned.shape[0]
    for g, source in enumerate((qkv_own, qkv_got)):
        for h in range(group_heads):
            for part in range(3):
                to = part * width + g * group + h * HEAD_DIM
                start = (3 * h + part) * HEAD_DIM
                wqkv[to : to + HEAD_DIM, :] = source[start : start + HEAD_DIM, :]
    wout[:group, :] = out_own[...]
    wout[group:, :] = out_got[...]
    nothing = jnp.zeros((channels, width), BF16)
    w_in[:channels, :] = patch[0].astype(BF16)
    w_in[channels:, :] = nothing
    w_fin[:channels, :] = nothing
    w_fin[channels:, :] = patch[1].astype(BF16)

    def two_terms(target, values):
        coarse = values.astype(BF16)
        rest = jnp.zeros((SLOT_LANES - chip_slots, values.shape[1]), BF16)
        for base, term in ((0, coarse), (SLOT_LANES, (values - coarse.astype(F32)).astype(BF16))):
            target[base : base + chip_slots, :] = term
            target[base + chip_slots : base + SLOT_LANES, :] = rest

    for half in range(2):
        two_terms(modcat.at[half], jnp.where(core == half, mod_own[...], mod_got[...]))
    two_terms(
        shiftcat,
        jnp.concatenate(
            [
                source[:, (3 * h + part) * HEAD_DIM : (3 * h + part + 1) * HEAD_DIM]
                for part in range(3)
                for source in (shift_own, shift_got)
                for h in range(group_heads)
            ],
            1,
        ),
    )
    parts = (
        (0, up_own, dn_own, up_kept, down_kept),
        (half_hidden, up_got, dn_got, up_sent, down_sent),
    )

    def place_image(i, carry):
        src, dst = tab[1, i], tab[2, i]

        def body(size, offset):
            xtok[rows_at(dst, size, 16), :] = xrow[rows_at(src, size, 16), :]
            stream[rows_at(dst, size, 16), :] = places[offset : offset + size, :]
            fill_member(member, dst, size, i)

        for_sizes(tab[0, i], body)
        return carry

    lax.fori_loop(low, high, place_image, 0)
    tail = rows_at(tokens, TILE, 16)
    for ref in (xtok, stream, member, mixed):
        ref[tail, :] = jnp.zeros((TILE, ref.shape[1]), ref.dtype)
    for ref in (up_kept, down_kept, up_sent, down_sent, gout, gfin, sg, loss, gshift, gemb):
        ref[...] = jnp.zeros(ref.shape, ref.dtype)

    def spread(hot, half, start, count):
        wide = dot(hot, modcat[half, :, start * width : (start + count) * width])
        return [wide[:, k * width : (k + 1) * width] for k in range(count)]

    def project_tile(t, carry):
        r = rows_at(t * TILE, TILE, TILE)
        entering = dot(xtok[r, :], w_in[...]) + stream[r, :]
        stream[r, :] = entering
        hot = member[r, :]
        normed, _ = normalize(entering)
        shift1, scale1 = spread(hot, 0, 0, 2)
        attn_in = (normed * (1.0 + scale1) + shift1).astype(BF16)
        proj[r, :] = (dot_nt(attn_in, wqkv[...]) + dot(hot, shiftcat[...])).astype(BF16)
        return carry

    lax.fori_loop(0, tiles, project_tile, 0)

    def attend_image(i, carry):
        dst = tab[2, i]

        def body(size, offset):
            r = rows_at(dst, size, 16)
            pairs = range(heads // 2)
            ones = jnp.ones((16, size), BF16)
            scores, weights = [], []
            for p in pairs:
                key = proj[r, width + 128 * p : width + 128 * p + 128]
                scores.append(dot_nt(key, both_heads(proj[r, 128 * p : 128 * p + 128])))
            tops = [jnp.max(v, 0, keepdims=True) for v in scores]
            weights = [jnp.exp((v - top) * HEAD_DIM ** (-0.5)) for v, top in zip(scores, tops)]
            for p in pairs:
                value_t = proj[r, 2 * width + 128 * p : 2 * width + 128 * p + 128].T
                out = dot(jnp.concatenate([value_t, ones], 0), weights[p].astype(BF16))
                total = out[128:129]
                lse[tab[4, i], p : p + 1, : 2 * size] = tops[p] * HEAD_DIM ** (-0.5) + jnp.log(total)
                mixed[r, 128 * p : 128 * p + 128] = own_lanes((out[:128] / total).T).astype(BF16)

        for_sizes(tab[0, i], body)
        return carry

    lax.fori_loop(low, high, attend_image, 0)

    def token_tile(t, carry):
        r = rows_at(t * TILE, TILE, TILE)
        hot = member[r, :]
        hot_t = member[r, :SLOT_LANES].astype(F32).T.astype(BF16)

        def collect(block, value):
            sg[block * SLOT_LANES : (block + 1) * SLOT_LANES, :] += dot(hot_t, value.astype(BF16))

        mixed_tile = mixed[r, :]
        attended = dot(mixed_tile, wout[...])
        gate1, shift2 = spread(hot, 0, 2, 2)
        scale2, gate2, shift3, scale3 = spread(hot, 1, 0, 4)
        mid = stream[r, :] + gate1 * attended
        normed2, inverse2 = normalize(mid)
        mlp_in = (normed2 * (1.0 + scale2) + shift2).astype(BF16)
        mlp_out = jnp.zeros((TILE, width), F32)
        for j, wup, wdn, _, _ in parts:
            up = dot(mlp_in, wup[...])
            square = up * up
            bent = jnp.tanh(up * (GELU_A + (GELU_A * GELU_B) * square))
            share = 0.5 + 0.5 * bent
            act = (up * share).astype(BF16)
            active[:, j : j + half_hidden] = act
            deriv[:TILE, j : j + half_hidden] = share + up * (share * (1.0 - share)) * (
                2.0 * GELU_A + (6.0 * GELU_A * GELU_B) * square
            )
            mlp_out = mlp_out + dot(act, wdn[...])
        leaving = mid + gate2 * mlp_out
        normed3, inverse3 = normalize(leaving)
        final_in = (normed3 * (1.0 + scale3) + shift3).astype(BF16)
        predicted = dot_nt(final_in, w_fin[...])
        lane = lax.broadcasted_iota(jnp.int32, predicted.shape, 1)
        row = lax.broadcasted_iota(jnp.int32, predicted.shape, 0) + t * TILE
        keep = (lane >= channels) & (row < tokens)
        error = jnp.where(keep, predicted - xtok[r, :].astype(F32), 0.0)
        loss[...] += jnp.sum(error * error, 0, keepdims=True)
        grad_pred = (2.0 * error).astype(BF16)
        gfin[...] += dot(grad_pred.T, final_in)
        grad_final = dot(grad_pred, w_fin[...])
        collect(6, grad_final)
        collect(7, grad_final * normed3)
        grad_out = norm_back(grad_final * (1.0 + scale3), normed3, inverse3)
        collect(5, grad_out * mlp_out)
        grad_mlp = (grad_out * gate2).astype(BF16)
        grad_mlp_t = grad_mlp.T
        mlp_in_t = mlp_in.T
        grad_mlp_in = jnp.zeros((TILE, width), F32)
        for j, wup, wdn, gup, gdn in parts:
            gdn[...] += dot(grad_mlp_t, active[:, j : j + half_hidden])
            grad_act = dot_nt(grad_mlp, wdn[...])
            grad_up = (grad_act * deriv[:TILE, j : j + half_hidden]).astype(BF16)
            gup[...] += dot(mlp_in_t, grad_up)
            grad_mlp_in = grad_mlp_in + dot_nt(grad_up, wup[...])
        collect(3, grad_mlp_in)
        collect(4, grad_mlp_in * normed2)
        grad_mid = grad_out + norm_back(grad_mlp_in * (1.0 + scale2), normed2, inverse2)
        gmid[r, :] = grad_mid
        collect(2, grad_mid * attended)
        grad_attended = (grad_mid * gate1).astype(BF16)
        gout[...] += dot(mixed_tile.T, grad_attended)
        gmixed[r, :] = dot_nt(grad_attended, wout[...]).astype(BF16)
        return carry

    lax.fori_loop(0, tiles, token_tile, 0)
    gqkv[...] = jnp.zeros(gqkv.shape, F32)
    out_kept[...] = gout[:group, :]
    at = 0
    for ref in (up_sent, down_sent):
        for j in range(0, half_hidden, 128):
            other[at : at + width, :] = ref[:, j : j + 128].astype(BF16)
            at += width
    for j in range(0, width, 128):
        other[at : at + group, :] = gout[group:, j : j + 128].astype(BF16)
        at += group
    every = jnp.ones((8, 2 * HEAD_DIM), BF16)

    def unattend_image(i, carry):
        dst = tab[2, i]

        def body(size, offset):
            r = rows_at(dst, size, 16)
            pairs = range(heads // 2)
            grads = [both_heads(gmixed[r, 128 * p : 128 * p + 128]) for p in pairs]
            queries = [both_heads(proj[r, 128 * p : 128 * p + 128]) for p in pairs]
            inners, probs, drops = [], [], []
            for p in pairs:
                out = mixed[r, 128 * p : 128 * p + 128].astype(F32)
                product = grads[p].astype(F32) * jnp.concatenate([out, out], 0)
                coarse = product.astype(BF16)
                fine = (product - coarse.astype(F32)).astype(BF16)
                inners.append((dot_nt(every, coarse) + dot_nt(every, fine))[0:1])
            for p in pairs:
                scores = dot_nt(proj[r, width + 128 * p : width + 128 * p + 128], queries[p])
                probs.append(jnp.exp(scores * HEAD_DIM ** (-0.5) - lse[tab[4, i], p : p + 1, : 2 * size]))
            for p in pairs:
                grad_probs = dot_nt(proj[r, 2 * width + 128 * p : 2 * width + 128 * p + 128], grads[p])
                drops.append((probs[p] * (grad_probs - inners[p])).astype(BF16))
            for p in pairs:
                key_t = proj[r, width + 128 * p : width + 128 * p + 128].T
                grad_value = dot(probs[p].astype(BF16), grads[p])
                grad_key = dot(drops[p], queries[p]) * HEAD_DIM ** (-0.5)
                grad_query = own_lanes(dot(key_t, drops[p]).T) * HEAD_DIM ** (-0.5)
                for part, value in enumerate((grad_query, grad_key, grad_value)):
                    at = part * width + 128 * p
                    proj[r, at : at + 128] = value.astype(BF16)

        for_sizes(tab[0, i], body)
        return carry

    lax.fori_loop(low, high, unattend_image, 0)

    def last_tile(t, carry):
        r = rows_at(t * TILE, TILE, TILE)
        hot = member[r, :]
        hot_t = member[r, :SLOT_LANES].astype(F32).T.astype(BF16)

        def collect(block, value):
            sg[block * SLOT_LANES : (block + 1) * SLOT_LANES, :] += dot(hot_t, value.astype(BF16))

        normed, inverse = normalize(stream[r, :])
        shift1, scale1 = spread(hot, 0, 0, 2)
        attn_in = (normed * (1.0 + scale1) + shift1).astype(BF16)
        grad_proj = proj[r, :]
        gqkv[...] += dot(attn_in.T, grad_proj)
        gshift[...] += dot(hot_t, grad_proj)
        grad_attn_in = dot(grad_proj, wqkv[...])
        collect(0, grad_attn_in)
        collect(1, grad_attn_in * normed)
        grad_in = gmid[r, :] + norm_back(grad_attn_in * (1.0 + scale1), normed, inverse)
        gemb[...] += dot(xtok[r, :].T, grad_in.astype(BF16))
        return carry

    lax.fori_loop(0, tiles, last_tile, 0)
    turned = gqkv[...].T
    kept = time_own.shape[0]
    for g, (main, shift) in enumerate(((main_own, time_own), (main_other, time_other))):
        pieces = []
        for h in range(heads // 2):
            for part in range(3):
                start = part * width + g * group + h * HEAD_DIM
                to = (3 * h + part) * HEAD_DIM
                main[to : to + HEAD_DIM, :] = turned[start : start + HEAD_DIM, :].astype(main.dtype)
                pieces.append(gshift[:kept, start : start + HEAD_DIM])
        shift[...] = jnp.concatenate(pieces, 1)
    for part in range(4):
        lower = sg[part * SLOT_LANES : part * SLOT_LANES + kept, :]
        upper = sg[(4 + part) * SLOT_LANES : (4 + part) * SLOT_LANES + kept, :]
        sg_own[part] = jnp.where(core == 0, lower, upper)
        sg_other[part] = jnp.where(core == 0, upper, lower)


def call_step(tab, x_own, x_got, mods, shifts, patch, weights):
    rows_kept, channels2, length = x_own.shape
    kept = mods[0].shape[0]
    width, half_hidden = weights[4].shape
    group = width // 2
    slots = SLOT_LANES
    longest = rows_kept * length + max(SIZES) // 2
    room = (longest + TILE + 15) // 16 * 16
    vmem = pl.BlockSpec(memory_space=pltpu.VMEM)
    shape = jax.ShapeDtypeStruct
    outs = (
        shape((width, half_hidden), F32),
        shape((width, half_hidden), F32),
        shape((group, width), F32),
        shape((width * (2 * half_hidden + group) // 128, 128), BF16),
        shape((channels2, width), F32),
        shape((1, channels2), F32),
        shape((3 * group, width), F32),
        shape((3 * group, width), BF16),
        shape((kept, 3 * group), F32),
        shape((kept, 3 * group), F32),
        shape((channels2, width), F32),
        shape((4, kept, width), F32),
        shape((4, kept, width), F32),
    )
    return pl.pallas_call(
        step_kernel,
        out_shape=outs,
        in_specs=[pl.BlockSpec(memory_space=pltpu.SMEM)] + [vmem] * 16,
        out_specs=[vmem] * len(outs),
        scratch_shapes=[
            pltpu.VMEM((room, 3 * width), BF16),
            pltpu.VMEM((room, width), BF16),
            pltpu.VMEM((room, width), BF16),
            pltpu.VMEM((room, width), F32),
            pltpu.VMEM((room, width), F32),
            pltpu.VMEM((room, channels2), BF16),
            pltpu.VMEM((room // min(SIZES), 8, 2 * max(SIZES)), F32),
            pltpu.VMEM((8 * slots, width), F32),
            pltpu.VMEM((2, 2 * slots, 4 * width), BF16),
            pltpu.VMEM((3 * width, width), BF16),
            pltpu.VMEM((2 * rows_kept * length, channels2), BF16),
            pltpu.VMEM((room, 2 * slots), BF16),
            pltpu.VMEM((max(TILE, width), max(2 * half_hidden, 3 * width)), F32),
            pltpu.VMEM((TILE, 2 * half_hidden), BF16),
            pltpu.VMEM((width, half_hidden), F32),
            pltpu.VMEM((width, half_hidden), F32),
            pltpu.VMEM((width, width), F32),
            pltpu.VMEM((2 * slots, 3 * width), BF16),
            pltpu.VMEM((width, width), BF16),
            pltpu.VMEM((channels2, width), BF16),
            pltpu.VMEM((channels2, width), BF16),
            pltpu.VMEM((slots, 3 * width), F32),
        ],
        compiler_params=pltpu.CompilerParams(vmem_limit_bytes=VMEM_LIMIT),
        name="step",
    )(tab, x_own, x_got, jnp.asarray(position_rows(width)), *mods, *shifts, patch, *weights)


def signal_tables():
    betas = 0.0001 + 0.0199 * np.arange(1000) / 999.0
    level = np.exp(np.cumsum(np.log(1.0 - betas)))
    return np.pad(np.stack([np.sqrt(level), np.sqrt(1.0 - level)]), ((0, 0), (0, 24))).astype(np.float32)


def noise_kernel(counts, steps, tables, latents, noise, own, sent):
    rows_here, channels, length = latents.shape
    kept = own.shape[0]
    position = lax.broadcasted_iota(jnp.int32, (1, length), 1)
    for r in range(rows_here):
        start = jnp.int32(0)
        keep = jnp.zeros((1, length), F32)
        fade = jnp.zeros((1, length), F32)
        for k in range(counts.shape[1]):
            end = start + counts[r, k]
            inside = (position >= start) & (position < end)
            keep = jnp.where(inside, tables[0, steps[r, k]], keep)
            fade = jnp.where(inside, tables[1, steps[r, k]], fade)
            start = end
        target = own.at[r] if r < kept else sent.at[r - kept]
        target[:channels, :] = (keep * latents[r] + fade * noise[r]).astype(BF16)
        target[channels:, :] = noise[r].astype(BF16)


def call_noise(counts, steps, latents, noise):
    rows_here, channels, length = latents.shape
    smem = pl.BlockSpec(memory_space=pltpu.SMEM)
    vmem = pl.BlockSpec(memory_space=pltpu.VMEM)
    kept = rows_here // 2
    return pl.pallas_call(
        noise_kernel,
        out_shape=[jax.ShapeDtypeStruct((n, 2 * channels, length), BF16) for n in (kept, rows_here - kept)],
        in_specs=[smem, smem, smem, vmem, vmem],
        out_specs=[vmem] * 2,
        compiler_params=pltpu.CompilerParams(vmem_limit_bytes=VMEM_LIMIT),
        name="add_noise",
    )(counts, steps, jnp.asarray(signal_tables()), latents, noise)


def time_features(steps, freqs):
    half = freqs // 2
    rates = jnp.exp(-math.log(10000.0) * jnp.arange(half, dtype=F32) / half)
    angle = steps.astype(F32)[..., None] * rates
    return jnp.concatenate([jnp.cos(angle), jnp.sin(angle)], -1)


def running_sum(values):
    size = values.shape[-1]
    before = np.arange(size)[:, None] > np.arange(size)[None, :]
    return jnp.sum(jnp.where(before, values[..., None, :], 0), -1)


def image_table(counts, core, place, length):
    rows_here, slots = counts.shape
    row_start = running_sum(counts) + length * jnp.arange(rows_here, dtype=jnp.int32)[:, None]
    flat = counts.reshape(-1)
    start = running_sum(flat)
    total = jnp.sum(flat)
    index = jnp.arange(flat.shape[0], dtype=jnp.int32)
    first_half = jnp.sum((2 * start + flat <= total).astype(jnp.int32))
    low = jnp.where(core == 0, 0, first_half)
    high = jnp.where(core == 0, first_half, flat.shape[0])
    base = jnp.sum(jnp.where(index < low, flat, 0))
    tokens = jnp.sum(jnp.where((index >= low) & (index < high), flat, 0))
    tiles = (tokens + TILE - 1) // TILE
    facts = jnp.stack([low, high, tokens, tiles, core, place]).astype(jnp.int32)
    pad = lambda v: jnp.pad(v.astype(jnp.int32), (0, 128 - v.shape[0]))
    return jnp.stack([pad(flat), pad(row_start.reshape(-1)), pad(start - base), pad(facts), pad((start - base) // min(SIZES))])


def swap(value):
    return lax.ppermute(value, "tensor", [(0, 1), (1, 0)])


def fine_dot(left, right, dims):
    left_a, right_a = left.astype(BF16), right.astype(BF16)
    left_b = (left - left_a.astype(F32)).astype(BF16)
    right_b = (right - right_a.astype(F32)).astype(BF16)
    product = partial(lax.dot_general, dimension_numbers=(dims, ((), ())), preferred_element_type=F32)
    return product(left_a, right_a) + (product(left_a, right_b) + product(left_b, right_a))


PLAIN, TURNED = ((1,), (0,)), ((1,), (1,))


def silu_slope(value):
    gate = 1.0 / (1.0 + jnp.exp(-value))
    return gate * (1.0 + value * (1.0 - gate))


def term_kernel(shift_own, shift_got, sg_own, sg_got, cond, w_mod, w_time, term):
    width = w_mod.shape[0]
    total = jnp.zeros(cond.shape, F32)
    for part in range(4):
        grad = sg_own[part] + sg_got[part]
        total = total + fine_dot(grad, w_mod[:, part * width : (part + 1) * width], TURNED)
    term[...] = total * silu_slope(cond[...]) + fine_dot(shift_own[...] + shift_got[...], w_time[...], PLAIN)


def pack_kernel(
    n_dp, chunks, tab, up, down, out, got, main_own, main_got, shift_own, shift_got, sg_own, sg_got, cond, *refs
):
    n = len(chunks)
    keeps, gives, done, rows = refs[:n], refs[n : 2 * n], refs[2 * n], refs[2 * n + 1]
    width = cond.shape[1]
    at = 0
    for ref in (up, down, out):
        for j in range(0, ref.shape[1], 128):
            to = slice(at, at + ref.shape[0])
            rows[to, :] = ref[:, j : j + 128] + got[to, :].astype(F32)
            at = to.stop
    values = cond[...]
    act_t = (values / (1.0 + jnp.exp(-values))).T
    shift_t = (shift_own[...] + shift_got[...]).T

    def put(block):
        nonlocal at
        for j in range(0, width, 128):
            rows[at : at + block.shape[0], :] = block[:, j : j + 128]
            at += block.shape[0]

    put(main_own[...] + main_got[...].astype(F32))
    put(fine_dot(shift_t, values, PLAIN))
    for part in range(4):
        put(fine_dot(act_t, sg_own[part] + sg_got[part], PLAIN))
    rows[at:, :] = jnp.zeros((rows.shape[0] - at, 128), F32)
    done[...] = jnp.zeros(done.shape, F32)
    base = 0
    for k, chunk in enumerate(chunks):
        bit = bit_order(n_dp, k)[0]
        mine = lax.shift_right_logical(tab[3, 5], bit) & 1
        for j in range(n_dp // 2):
            owner = (j >> bit << (bit + 1)) | (j & ((1 << bit) - 1))
            first = base + owner * chunk
            keep = first + mine * (chunk << bit)
            give = first + (1 - mine) * (chunk << bit)
            keeps[k][j] = rows[pl.ds(pl.multiple_of(keep, 16), chunk), :]
            gives[k][j] = rows[pl.ds(pl.multiple_of(give, 16), chunk), :].astype(BF16)
        base += n_dp * chunk


def call_pack(n_dp, chunks, table, *args):
    vmem = pl.BlockSpec(memory_space=pltpu.VMEM)
    shapes = [jax.ShapeDtypeStruct((n_dp // 2, c, 128), kind) for kind in (F32, BF16) for c in chunks]
    shapes.append(jax.ShapeDtypeStruct((8, 128), F32))
    return pl.pallas_call(
        partial(pack_kernel, n_dp, chunks),
        out_shape=shapes,
        in_specs=[pl.BlockSpec(memory_space=pltpu.SMEM)] + [vmem] * len(args),
        out_specs=[vmem] * len(shapes),
        scratch_shapes=[pltpu.VMEM((n_dp * sum(chunks), 128), F32)],
        compiler_params=pltpu.CompilerParams(vmem_limit_bytes=VMEM_LIMIT),
        name="pack_grads",
    )(table, *args)


def time_kernel(time_chunk, extra, tab, term, got, before, features, w_time, patch, patch_got, _, rows, flat):
    width = w_time.shape[1]
    freqs = features.shape[1]
    grad_cond = term[...] + got[...]
    values = before[...]
    hidden = values / (1.0 + jnp.exp(-values))
    second = fine_dot(hidden.T, grad_cond, PLAIN)
    inner = fine_dot(grad_cond, w_time[freqs:, :], TURNED) * silu_slope(values)
    first = fine_dot(features[...].T, inner, PLAIN)
    half = w_time.shape[0] // 2
    both = jnp.concatenate([first, second], 0)
    mine = jnp.where(tab[3, 4] == 0, both[:half], both[half:])
    shared = patch[...] + patch_got[...]
    n_dp = rows.shape[0]
    flat[...] = jnp.zeros(flat.shape, F32)
    patch_at = n_dp * time_chunk
    for t in range(width // 128):
        flat[t * half : (t + 1) * half, :] = mine[:, t * 128 : (t + 1) * 128]
        to = patch_at + t * shared.shape[0]
        flat[to : to + shared.shape[0], :] = shared[:, t * 128 : (t + 1) * 128]
    for d in range(n_dp):
        rows[d, :time_chunk, :] = flat[d * time_chunk : (d + 1) * time_chunk, :]
        rows[d, time_chunk:, :] = flat[patch_at + d * extra : patch_at + (d + 1) * extra, :]


def call_time(n_dp, time_chunk, extra, table, *args):
    vmem = pl.BlockSpec(memory_space=pltpu.VMEM)
    return pl.pallas_call(
        partial(time_kernel, time_chunk, extra),
        out_shape=jax.ShapeDtypeStruct((n_dp, time_chunk + extra, 128), F32),
        in_specs=[pl.BlockSpec(memory_space=pltpu.SMEM)] + [vmem] * len(args),
        out_specs=vmem,
        scratch_shapes=[pltpu.VMEM((n_dp * (time_chunk + extra), 128), F32)],
        compiler_params=pltpu.CompilerParams(vmem_limit_bytes=VMEM_LIMIT),
        name="time_grads",
    )(table, *args)


def call_small(kernel, shape, name, *args):
    vmem = pl.BlockSpec(memory_space=pltpu.VMEM)
    return pl.pallas_call(
        kernel,
        out_shape=jax.ShapeDtypeStruct(shape, F32),
        in_specs=[vmem] * len(args),
        out_specs=vmem,
        compiler_params=pltpu.CompilerParams(vmem_limit_bytes=VMEM_LIMIT),
        name=name,
    )(*args)


def adam_values(weight, first, second, grad, factor):
    clipped = grad * factor
    first = BETA_FIRST * first + (1.0 - BETA_FIRST) * clipped
    second = BETA_SECOND * second + (1.0 - BETA_SECOND) * clipped * clipped
    fixed = jnp.maximum(second * (1.0 / (1.0 - BETA_SECOND**STEP)), 1e-37)
    root = fixed * lax.rsqrt(fixed) + ADAM_EPS
    inverse = pl.reciprocal(root, approx=True)
    inverse = inverse * (2.0 - root * inverse)
    step = first * (1.0 / (1.0 - BETA_FIRST**STEP)) * inverse
    return (first, second, weight - LEARN_RATE * (step + WEIGHT_DECAY * weight))


def adam_kernel(n_dp, lists, chunks, time_chunk, extra, place, *refs):
    n_got = sum(len(pieces) for pieces, _ in lists)
    got, refs = refs[:n_got], refs[n_got:]
    ins, outs, stats, bufs = refs[:21], refs[21:42], refs[42], refs[43:64]
    rows, time_rows, extra_rows, sem_in, sem_out, sem_got = refs[64:]
    width = ins[3].shape[1]
    here = place[0]
    jobs = []
    for p in range(7):
        shape = ins[3 * p].shape
        if p == 0:
            jobs.append((p, None))
        elif p == 3:
            jobs.extend((p, (i,)) for i in range(2))
        else:
            step = shape[0] // 2 if p == 1 else min(width, shape[0])
            jobs.extend(
                (p, (pl.ds(r, step), pl.ds(j, width))) for r in range(0, shape[0], step) for j in range(0, shape[1], width)
            )

    def view(ref, where):
        return ref if where is None else ref.at[where]

    arrivals = []
    base = 0
    for stream, ((pieces, order), chunk) in enumerate(zip(lists, chunks)):
        for source, relatives in zip(pieces, order):
            for j, relative in enumerate(relatives):
                owner = here ^ relative
                parts = [(0, chunk, rows, base + owner * chunk)]
                if stream == len(chunks) - 1:
                    parts.append((chunk, time_chunk, time_rows, owner * time_chunk))
                    parts.append((chunk + time_chunk, time_chunk, time_rows, (n_dp + owner) * time_chunk))
                    parts.append((chunk + 2 * time_chunk, 6 * extra, extra_rows, owner * 6 * extra))
                for start, size, target, at in parts:
                    copy = pltpu.make_async_copy(
                        got[source].at[j, pl.ds(start, size), :],
                        target.at[pl.ds(pl.multiple_of(at, 16), size), :],
                        sem_got.at[len(arrivals)],
                    )
                    copy.start()
                    arrivals.append(copy)
        base += n_dp * chunk
    loads = []
    for i, (p, where) in enumerate(jobs):
        group = []
        for k in range(3):
            copy = pltpu.make_async_copy(
                view(ins[3 * p + k], where), view(bufs[3 * p + k], where), sem_in.at[3 * i + k]
            )
            copy.start()
            group.append(copy)
        loads.append(group)
    for copy in arrivals:
        copy.wait()
    shards = []
    squares = jnp.zeros((1, 128), F32)
    for owner in range(n_dp):
        at = owner * 6 * extra
        terms = [extra_rows[at + k * 2 * extra : at + (k + 1) * 2 * extra, :].astype(F32) for k in range(3)]
        whole = terms[0] + terms[1] + terms[2]
        shards.append(whole[:extra])
        squares = squares + whole[extra : extra + 1]
    shared = jnp.concatenate(shards, 0)
    each = 2 * ins[0].shape[1] + 8
    patch = jnp.concatenate([shared[t * each : t * each + each - 8] for t in range(width // 128)], 1)
    facts = shared[each - 8 : each - 7]
    loss, count = facts[:, 0:1], facts[:, 1:2]
    squares = jnp.sum(squares, 1, keepdims=True)
    squares = squares + jnp.sum(jnp.sum(patch * patch, 1, keepdims=True), 0, keepdims=True)
    grad_norm = jnp.sqrt(squares) / count
    scale = jnp.minimum(1.0, CLIP_LIMIT / grad_norm) / count
    lane = lax.broadcasted_iota(jnp.int32, stats.shape, 1)
    stats[...] = jnp.where(lane == 0, loss, jnp.where(lane == 1, count, grad_norm))
    patch = patch.reshape(ins[0].shape)

    def tiles(at, size, count):
        return jnp.concatenate([rows[at + i * size : at + (i + 1) * size, :] for i in range(count)], 1).astype(F32)

    per_tile = width // 128
    half_time = ins[3].shape[0] // 2
    offsets = {5: 0}
    offsets[6] = ins[15].shape[0] * ins[15].shape[1] // 128
    offsets[4] = offsets[6] + ins[18].shape[0] * ins[18].shape[1] // 128
    offsets[3] = offsets[4] + ins[12].shape[0] * ins[12].shape[1] // 128
    offsets[2] = offsets[3] + 2 * ins[9].shape[1] * ins[9].shape[2] // 128
    stores = []
    for i, (p, where) in enumerate(jobs):
        for copy in loads[i]:
            copy.wait()
        if p == 0:
            grad = patch
        elif p == 1:
            top = where[0].start // half_time * n_dp * time_chunk
            grad = jnp.concatenate(
                [time_rows[top + t * half_time : top + (t + 1) * half_time, :] for t in range(per_tile)], 1
            ).astype(F32)
        elif p == 3:
            size = ins[9].shape[1]
            grad = tiles(offsets[3] + where[0] * size * per_tile, size, per_tile)
        elif p == 6:
            grad = tiles(offsets[6] + where[0].start // 128 * width, width, per_tile).T
        else:
            size = ins[3 * p].shape[0]
            grad = tiles(offsets[p] + where[1].start // 128 * size, size, per_tile)
        b = bufs[3 * p : 3 * p + 3]
        index = ... if where is None else where
        values = adam_values(b[0][index], b[1][index], b[2][index], grad, scale)
        for k, value in enumerate(values):
            b[k][index] = value
            copy = pltpu.make_async_copy(view(b[k], where), view(outs[3 * p + k], where), sem_out.at[3 * i + k])
            copy.start()
            stores.append(copy)
    for copy in stores:
        copy.wait()


def call_adam(n_dp, lists, chunks, time_chunk, extra, place, got, params):
    smem = pl.BlockSpec(memory_space=pltpu.SMEM)
    vmem = pl.BlockSpec(memory_space=pltpu.VMEM)
    anywhere = pl.BlockSpec(memory_space=pl.ANY)
    n_jobs = 3 * 16
    return pl.pallas_call(
        partial(adam_kernel, n_dp, lists, chunks, time_chunk, extra),
        out_shape=[jax.ShapeDtypeStruct(w.shape, F32) for w in params] + [jax.ShapeDtypeStruct((8, 128), F32)],
        in_specs=[smem] + [anywhere] * (len(got) + len(params)),
        out_specs=[anywhere] * len(params) + [vmem],
        scratch_shapes=[pltpu.VMEM(w.shape, F32) for w in params]
        + [
            pltpu.VMEM((n_dp * sum(chunks), 128), BF16),
            pltpu.VMEM((2 * n_dp * time_chunk, 128), BF16),
            pltpu.VMEM((n_dp * 6 * extra, 128), BF16),
            pltpu.SemaphoreType.DMA((n_jobs,)),
            pltpu.SemaphoreType.DMA((n_jobs,)),
            pltpu.SemaphoreType.DMA((6 * n_dp,)),
        ],
        compiler_params=pltpu.CompilerParams(vmem_limit_bytes=VMEM_LIMIT),
        name="adam",
    )(place, *got, *params)


def stage(size, bit):
    return [(i, i ^ (1 << bit)) for i in range(size)]


def bit_order(size, turn):
    bits = list(range(size.bit_length() - 1))
    lead = bits[:3]
    turn %= max(len(lead), 1)
    return lead[turn:] + lead[:turn] + bits[3:]


def halve(keeps, gives, exact, size):
    place = lax.axis_index("dp")
    orders = [bit_order(size, turn) for turn in range(len(keeps))]
    lefts = [sorted(order, reverse=True) for order in orders]
    last = len(keeps) - 1
    values = [None for _ in keeps]
    exact = exact.reshape(*(2,) * len(orders[0]), *exact.shape[1:])
    for n in range(len(orders[0])):
        for k in range(len(keeps)):
            bit = orders[k][n]
            mine = (place >> bit) & 1
            axis = lefts[k].index(bit)
            lefts[k].remove(bit)

            def halves(v):
                return (
                    lax.dynamic_index_in_dim(v, mine, axis, keepdims=False),
                    lax.dynamic_index_in_dim(v, 1 - mine, axis, keepdims=False),
                )

            if n:
                keep, give = halves(values[k])
                give = give.astype(BF16)
            else:
                keep, give = (v[k].reshape(*(2,) * len(lefts[k]), *v[k].shape[1:]) for v in (keeps, gives))
            if k == last:
                exact, sent = halves(exact)
                coarse = lax.reduce_precision(sent, 8, 7)
                give = jnp.concatenate([give, coarse.astype(BF16), (sent - coarse).astype(BF16)], -2)
            got = lax.ppermute(give, "dp", stage(size, bit)).astype(F32)
            if k == last:
                m, e = keep.shape[-2], exact.shape[-2]
                exact = exact + (got[..., m : m + e, :] + got[..., m + e :, :])
                got = got[..., :m, :]
            values[k] = keep + got
    return values, exact


def gather(values, size, turn):
    held, relatives = values[None], [0]
    pieces = []
    order = bit_order(size, turn)[::-1]
    for n, bit in enumerate(order):
        got = lax.ppermute(held, "dp", stage(size, bit))
        moved = [r ^ (1 << bit) for r in relatives]
        if n == len(order) - 1:
            pieces = [(held, relatives), (got, moved)]
        else:
            held, relatives = jnp.concatenate([held, got], 0), relatives + moved
    return pieces


def shards(
    latents, noise_field, image_tokens, timesteps,
    w_patch, m_patch, v_patch, w_time, m_time, v_time, w_mod, m_mod, v_mod,
    w_qkv, m_qkv, v_qkv, w_out, m_out, v_out, w_up, m_up, v_up, w_down, m_down, v_down,
):
    rows_here, channels, length = latents.shape
    slots = image_tokens.shape[1]
    width = w_patch.shape[2]
    freqs = w_time.shape[0] - width
    core = lax.axis_index("tensor")
    n_dp = lax.axis_size("dp")
    chip_slots = rows_here * slots
    group = w_out.shape[0]
    kept = rows_here // 2
    mirror = [(i, n_dp - 1 - i) for i in range(n_dp)]

    numbers = jnp.concatenate([image_tokens, timesteps], 1)
    numbers = jnp.concatenate([numbers[:kept], lax.ppermute(numbers[kept:], "dp", mirror)], 0)
    x_own, sent = call_noise(image_tokens, timesteps, latents, noise_field)
    x_got = lax.ppermute(sent, "dp", mirror)
    counts, steps = numbers[:, :slots], numbers[:, slots:].reshape(-1)
    tab = image_table(counts, core, lax.axis_index("dp"), length)

    qkv_t, qkv_m, qkv_v = (v.swapaxes(1, 2) for v in (w_qkv, m_qkv, v_qkv))
    halves = []
    x_own, *mains = lax.optimization_barrier((x_own, qkv_t[0], w_out, w_up, w_down))
    for w in mains:
        w = w.astype(BF16)
        halves.extend((w, swap(w)))

    features = time_features(steps, freqs)
    before = precise(features, w_time[:freqs])
    cond = precise(jax.nn.silu(before), w_time[freqs:])
    mod_own = precise(jax.nn.silu(cond), w_mod)
    shift_own = precise(cond, qkv_t[1].T)

    up, down, out, other, gfin, loss, main_own, main_other, time_own, time_other, gemb, sg_own, sg_other = call_step(
        tab, x_own, x_got, (mod_own, swap(mod_own)), (shift_own, swap(shift_own)), w_patch, halves
    )

    patch = jnp.concatenate([gemb[:channels], gfin[channels:]], 0)
    count_here = 0.5 * channels * jnp.sum(image_tokens).astype(F32)
    facts = jnp.stack([jnp.sum(loss), count_here])
    patch = jnp.concatenate([patch, jnp.pad(facts[None], ((0, 7), (0, width - 2)))], 0)
    slot_grads = (time_own, swap(time_other), sg_own, swap(sg_other))
    term = call_small(term_kernel, cond.shape, "cond_term", *slot_grads, cond, w_mod, qkv_t[1])

    def share(count, multiple):
        return (count + n_dp * multiple - 1) // (n_dp * multiple) * multiple

    time_chunk = share(w_time.shape[0] // 2 * width // 128, 16)
    extra = share(patch.size // 128, 8)
    wide = share(other.shape[0] + (2 * 3 * group + 4 * width) * width // 128, 1)
    most = (wide + 2 * (time_chunk + extra) + 47) // 48 * 16
    chunks = (most, most, max(wide - 2 * most + 15, 16) // 16 * 16)
    packed = call_pack(
        n_dp, chunks, tab, up, down, out, swap(other), main_own, swap(main_other), *slot_grads, cond
    )
    g_time = call_time(
        n_dp, time_chunk, extra, tab, term, swap(term), before, features, w_time, patch, swap(patch), packed[-1]
    )

    parts, exact_part = halve(packed[:3], packed[3:6], g_time, n_dp)
    time_part, patch_part = exact_part[:time_chunk], exact_part[time_chunk:]
    squares = sum(jnp.sum(v * v) for v in (*parts, time_part))
    mine = jnp.concatenate([time_part, jnp.full((8, 128), squares, F32)], 0)
    theirs = swap(mine)
    first = core == 0
    both_time = [jnp.where(first, mine, theirs)[:time_chunk], jnp.where(first, theirs, mine)[:time_chunk]]
    lane = jnp.arange(128)[None]
    spot = (jnp.arange(extra)[:, None] == 0) & (lane == 0)
    total = jnp.where(spot, mine[time_chunk, 0] + theirs[time_chunk, 0], 0.0)
    terms, rest = [], jnp.concatenate([patch_part, total], 0)
    for _ in range(3):
        coarse = lax.reduce_precision(rest, 8, 7)
        terms.append(coarse.astype(BF16))
        rest = rest - coarse
    sent = [v.astype(BF16) for v in parts]
    sent[-1] = jnp.concatenate([sent[-1], *(v.astype(BF16) for v in both_time), *terms], 0)
    got, lists = [], []
    for k in range(3):
        pieces = gather(sent[k], n_dp, k)
        lists.append(([len(got) + i for i in range(len(pieces))], [r for _, r in pieces]))
        got.extend(v for v, _ in pieces)
    params = (
        w_patch, m_patch, v_patch, w_time, m_time, v_time, w_mod, m_mod, v_mod,
        qkv_t, qkv_m, qkv_v, w_out, m_out, v_out, w_up, m_up, v_up, w_down, m_down, v_down,
    )
    *updated, stats = call_adam(
        n_dp, lists, chunks, time_chunk, extra, lax.axis_index("dp").reshape(1), got, params
    )
    for k in range(9, 12):
        updated[k] = updated[k].swapaxes(1, 2)
    return (stats[0, 0], stats[0, 1], stats[0, 2], *updated)


def solution(mesh):
    rows, flat, cols = P("dp", None, None), P("dp", None), P(None, "tensor")
    whole, deep, split = P(), P(None, None, "tensor"), P("tensor", None)
    weights = [p for p in (whole, whole, cols, deep, split, cols, split) for _ in range(3)]
    return jax.shard_map(
        shards,
        mesh=mesh,
        in_specs=(rows, rows, flat, flat, *weights),
        out_specs=(whole, whole, whole, *weights),
        check_vma=False,
    )
```

```python
from functools import partial
import math

import jax
import jax.numpy as jnp
import numpy as np
from jax import lax
from jax.experimental import pallas as pl
from jax.experimental.pallas import tpu as pltpu
from jax.sharding import PartitionSpec as P

HEAD_DIM = 64
STEP = 10
PRECISE_MODE = lax.Precision.HIGHEST
NORM_EPS = 1e-06
CLIP_LIMIT = 0.001
LEARN_RATE = 0.03
BETA_FIRST = 0.9
BETA_SECOND = 0.95
ADAM_EPS = 1e-08
WEIGHT_DECAY = 0.1
SIZES = (64, 144, 256)
TILE = 256
SLOT_LANES = 128
GELU_A = math.sqrt(2.0 / math.pi)
GELU_B = 0.044715
VMEM_LIMIT = 60 * 1024 * 1024
F32 = jnp.float32
BF16 = jnp.bfloat16


def precise(left, right):
    return jnp.dot(left, right, precision=PRECISE_MODE)


def dot(left, right):
    return lax.dot_general(left, right, (((1,), (0,)), ((), ())), preferred_element_type=F32)


def dot_nt(left, right):
    return lax.dot_general(left, right, (((1,), (1,)), ((), ())), preferred_element_type=F32)


def normalize(values):
    centre = values - jnp.mean(values, -1, keepdims=True)
    inverse = lax.rsqrt(jnp.mean(centre * centre, -1, keepdims=True) + NORM_EPS)
    return (centre * inverse, inverse)


def norm_back(grad, normed, inverse):
    return inverse * (
        grad
        - jnp.mean(grad, -1, keepdims=True)
        - normed * jnp.mean(grad * normed, -1, keepdims=True)
    )


def position_rows(width):
    quarter = width // 4
    omega = np.exp(-math.log(10000.0) * np.arange(quarter) / quarter)
    parts = []
    for size in SIZES:
        side = math.isqrt(size)
        offset = np.arange(size)
        row_angle = (offset // side)[:, None] * omega
        col_angle = (offset % side)[:, None] * omega
        parts.append(
            np.concatenate(
                [np.sin(row_angle), np.cos(row_angle), np.sin(col_angle), np.cos(col_angle)], -1
            )
        )
    return np.concatenate(parts, 0).astype(np.float32)


def for_sizes(count, body):
    offset = 0
    for size in SIZES:
        pl.when(count == size)(partial(body, size, offset))
        offset += size


def rows_at(start, size, step):
    return pl.ds(pl.multiple_of(start, step), size)


def fill_member(member, dst, size, index):
    lane = lax.broadcasted_iota(jnp.int32, (size, 2 * SLOT_LANES), 1)
    hot = (lane == index) | (lane == index + SLOT_LANES)
    member[rows_at(dst, size, 16), :] = hot.astype(F32).astype(BF16)


def both_heads(pair):
    first = lax.broadcasted_iota(jnp.int32, pair.shape, 1) < HEAD_DIM
    nothing = jnp.zeros_like(pair)
    return jnp.concatenate([jnp.where(first, pair, nothing), jnp.where(first, nothing, pair)], 0)


def own_lanes(rows):
    size = rows.shape[0] // 2
    first = lax.broadcasted_iota(jnp.int32, (size, rows.shape[1]), 1) < HEAD_DIM
    return jnp.where(first, rows[:size], rows[size:])


def step_kernel(
    tab, x_own, x_got, places, mod_own, mod_got, shift_own, shift_got, patch,
    qkv_own, qkv_got, out_own, out_got, up_own, up_got, dn_own, dn_got,
    up_kept, down_kept, out_kept, other, gfin, loss, main_own, main_other, time_own, time_other, gemb, sg_own, sg_other,
    proj, mixed, gmixed, gmid, stream, xtok, lse, sg, modcat, wqkv,
    xrow, member, deriv, active, up_sent, down_sent, gout, shiftcat, wout, w_in, w_fin, gshift,
):
    width = stream.shape[1]
    gqkv = deriv.at[:, : 3 * width]
    images, tokens, full, rest, core = (tab[3, j] for j in range(5))
    heads = width // HEAD_DIM
    group_heads = heads // 2
    group = width // 2
    half_hidden = up_own.shape[1]
    hidden = 2 * half_hidden
    channels = patch.shape[1]
    chip_slots = mod_own.shape[0]
    at = 0
    for x in (x_own, x_got):
        for r in range(x.shape[0]):
            turned = x[r].astype(F32).T
            xrow[at : at + turned.shape[0], :] = turned.astype(BF16)
            at += turned.shape[0]
    for g, source in enumerate((qkv_own, qkv_got)):
        for h in range(group_heads):
            for part in range(3):
                to = part * width + g * group + h * HEAD_DIM
                start = (3 * h + part) * HEAD_DIM
                wqkv[to : to + HEAD_DIM, :] = source[start : start + HEAD_DIM, :]
    wout[:group, :] = out_own[...]
    wout[group:, :] = out_got[...]
    nothing = jnp.zeros((channels, width), BF16)
    w_in[:channels, :] = patch[0].astype(BF16)
    w_in[channels:, :] = nothing
    w_fin[:channels, :] = nothing
    w_fin[channels:, :] = patch[1].astype(BF16)

    def two_terms(target, values):
        coarse = values.astype(BF16)
        rest = jnp.zeros((SLOT_LANES - chip_slots, values.shape[1]), BF16)
        for base, term in ((0, coarse), (SLOT_LANES, (values - coarse.astype(F32)).astype(BF16))):
            target[base : base + chip_slots, :] = term
            target[base + chip_slots : base + SLOT_LANES, :] = rest

    for half in range(2):
        two_terms(modcat.at[half], jnp.where(core == half, mod_own[...], mod_got[...]))
    two_terms(
        shiftcat,
        jnp.concatenate(
            [
                source[:, (3 * h + part) * HEAD_DIM : (3 * h + part + 1) * HEAD_DIM]
                for part in range(3)
                for source in (shift_own, shift_got)
                for h in range(group_heads)
            ],
            1,
        ),
    )
    parts = (
        (0, up_own, dn_own, up_kept, down_kept),
        (half_hidden, up_got, dn_got, up_sent, down_sent),
    )

    def place_image(i, carry):
        src, dst = tab[1, i], tab[2, i]

        def body(size, offset):
            xtok[rows_at(dst, size, 16), :] = xrow[rows_at(src, size, 16), :]
            stream[rows_at(dst, size, 16), :] = places[offset : offset + size, :]
            fill_member(member, dst, size, tab[4, i])

        for_sizes(tab[0, i], body)
        return carry

    lax.fori_loop(0, images, place_image, 0)
    tail = rows_at(tokens, TILE, 16)
    for ref in (xtok, stream, member, mixed):
        ref[tail, :] = jnp.zeros((TILE, ref.shape[1]), ref.dtype)
    for ref in (up_kept, down_kept, up_sent, down_sent, gout, gfin, sg, loss, gshift, gemb):
        ref[...] = jnp.zeros(ref.shape, ref.dtype)

    def spread(hot, half, start, count):
        wide = dot(hot, modcat[half, :, start * width : (start + count) * width])
        return [wide[:, k * width : (k + 1) * width] for k in range(count)]

    def for_tiles(body):
        def whole(t, carry):
            body(t * TILE, TILE)
            return carry

        lax.fori_loop(0, full, whole, 0)
        pl.when(rest == 1)(partial(body, full * TILE, TILE // 2))

    def project_tile(start, size):
        r = rows_at(start, size, size)
        entering = dot(xtok[r, :], w_in[...]) + stream[r, :]
        stream[r, :] = entering
        hot = member[r, :]
        normed, _ = normalize(entering)
        shift1, scale1 = spread(hot, 0, 0, 2)
        attn_in = (normed * (1.0 + scale1) + shift1).astype(BF16)
        proj[r, :] = (dot_nt(attn_in, wqkv[...]) + dot(hot, shiftcat[...])).astype(BF16)

    for_tiles(project_tile)

    def attend_image(i, carry):
        dst = tab[2, i]

        def body(size, offset):
            r = rows_at(dst, size, 16)
            pairs = range(heads // 2)
            ones = jnp.ones((16, size), BF16)
            scores, weights = [], []
            for p in pairs:
                key = proj[r, width + 128 * p : width + 128 * p + 128]
                scores.append(dot_nt(key, both_heads(proj[r, 128 * p : 128 * p + 128])))
            tops = [jnp.max(v, 0, keepdims=True) for v in scores]
            weights = [jnp.exp((v - top) * HEAD_DIM ** (-0.5)) for v, top in zip(scores, tops)]
            for p in pairs:
                value_t = proj[r, 2 * width + 128 * p : 2 * width + 128 * p + 128].T
                out = dot(jnp.concatenate([value_t, ones], 0), weights[p].astype(BF16))
                total = out[128:129]
                lse[i, p : p + 1, : 2 * size] = tops[p] * HEAD_DIM ** (-0.5) + jnp.log(total)
                mixed[r, 128 * p : 128 * p + 128] = own_lanes((out[:128] / total).T).astype(BF16)

        for_sizes(tab[0, i], body)
        return carry

    lax.fori_loop(0, images, attend_image, 0)

    def token_tile(start, size):
        r = rows_at(start, size, size)
        hot = member[r, :]
        hot_t = member[r, :SLOT_LANES].astype(F32).T.astype(BF16)

        def collect(block, value):
            sg[block * SLOT_LANES : (block + 1) * SLOT_LANES, :] += dot(hot_t, value.astype(BF16))

        mixed_tile = mixed[r, :]
        attended = dot(mixed_tile, wout[...])
        gate1, shift2 = spread(hot, 0, 2, 2)
        scale2, gate2, shift3, scale3 = spread(hot, 1, 0, 4)
        mid = stream[r, :] + gate1 * attended
        normed2, inverse2 = normalize(mid)
        mlp_in = (normed2 * (1.0 + scale2) + shift2).astype(BF16)
        mlp_out = jnp.zeros((size, width), F32)
        for j, wup, wdn, _, _ in parts:
            up = dot(mlp_in, wup[...])
            square = up * up
            bent = jnp.tanh(up * (GELU_A + (GELU_A * GELU_B) * square))
            share = 0.5 + 0.5 * bent
            act = (up * share).astype(BF16)
            active[:size, j : j + half_hidden] = act
            deriv[:size, j : j + half_hidden] = share + up * (share * (1.0 - share)) * (
                2.0 * GELU_A + (6.0 * GELU_A * GELU_B) * square
            )
            mlp_out = mlp_out + dot(act, wdn[...])
        leaving = mid + gate2 * mlp_out
        normed3, inverse3 = normalize(leaving)
        final_in = (normed3 * (1.0 + scale3) + shift3).astype(BF16)
        predicted = dot_nt(final_in, w_fin[...])
        lane = lax.broadcasted_iota(jnp.int32, predicted.shape, 1)
        row = lax.broadcasted_iota(jnp.int32, predicted.shape, 0) + start
        keep = (lane >= channels) & (row < tokens)
        error = jnp.where(keep, predicted - xtok[r, :].astype(F32), 0.0)
        loss[...] += jnp.sum(error * error, 0, keepdims=True)
        grad_pred = (2.0 * error).astype(BF16)
        gfin[...] += dot(grad_pred.T, final_in)
        grad_final = dot(grad_pred, w_fin[...])
        collect(6, grad_final)
        collect(7, grad_final * normed3)
        grad_out = norm_back(grad_final * (1.0 + scale3), normed3, inverse3)
        collect(5, grad_out * mlp_out)
        grad_mlp = (grad_out * gate2).astype(BF16)
        grad_mlp_t = grad_mlp.T
        mlp_in_t = mlp_in.T
        grad_mlp_in = jnp.zeros((size, width), F32)
        for j, wup, wdn, gup, gdn in parts:
            gdn[...] += dot(grad_mlp_t, active[:size, j : j + half_hidden])
            grad_act = dot_nt(grad_mlp, wdn[...])
            grad_up = (grad_act * deriv[:size, j : j + half_hidden]).astype(BF16)
            gup[...] += dot(mlp_in_t, grad_up)
            grad_mlp_in = grad_mlp_in + dot_nt(grad_up, wup[...])
        collect(3, grad_mlp_in)
        collect(4, grad_mlp_in * normed2)
        grad_mid = grad_out + norm_back(grad_mlp_in * (1.0 + scale2), normed2, inverse2)
        gmid[r, :] = grad_mid
        collect(2, grad_mid * attended)
        grad_attended = (grad_mid * gate1).astype(BF16)
        gout[...] += dot(mixed_tile.T, grad_attended)
        gmixed[r, :] = dot_nt(grad_attended, wout[...]).astype(BF16)

    for_tiles(token_tile)
    gqkv[...] = jnp.zeros(gqkv.shape, F32)
    out_kept[...] = gout[:group, :]
    at = 0
    for ref in (up_sent, down_sent):
        for j in range(0, half_hidden, 128):
            other[at : at + width, :] = ref[:, j : j + 128].astype(BF16)
            at += width
    for j in range(0, width, 128):
        other[at : at + group, :] = gout[group:, j : j + 128].astype(BF16)
        at += group
    every = jnp.ones((8, 2 * HEAD_DIM), BF16)

    def unattend_image(i, carry):
        dst = tab[2, i]

        def body(size, offset):
            r = rows_at(dst, size, 16)
            pairs = range(heads // 2)
            grads = [both_heads(gmixed[r, 128 * p : 128 * p + 128]) for p in pairs]
            queries = [both_heads(proj[r, 128 * p : 128 * p + 128]) for p in pairs]
            inners, probs, drops = [], [], []
            for p in pairs:
                out = mixed[r, 128 * p : 128 * p + 128].astype(F32)
                product = grads[p].astype(F32) * jnp.concatenate([out, out], 0)
                coarse = product.astype(BF16)
                fine = (product - coarse.astype(F32)).astype(BF16)
                inners.append((dot_nt(every, coarse) + dot_nt(every, fine))[0:1])
            for p in pairs:
                scores = dot_nt(proj[r, width + 128 * p : width + 128 * p + 128], queries[p])
                probs.append(jnp.exp(scores * HEAD_DIM ** (-0.5) - lse[i, p : p + 1, : 2 * size]))
            for p in pairs:
                grad_probs = dot_nt(proj[r, 2 * width + 128 * p : 2 * width + 128 * p + 128], grads[p])
                drops.append((probs[p] * (grad_probs - inners[p])).astype(BF16))
            for p in pairs:
                key_t = proj[r, width + 128 * p : width + 128 * p + 128].T
                grad_value = dot(probs[p].astype(BF16), grads[p])
                grad_key = dot(drops[p], queries[p]) * HEAD_DIM ** (-0.5)
                grad_query = own_lanes(dot(key_t, drops[p]).T) * HEAD_DIM ** (-0.5)
                for part, value in enumerate((grad_query, grad_key, grad_value)):
                    at = part * width + 128 * p
                    proj[r, at : at + 128] = value.astype(BF16)

        for_sizes(tab[0, i], body)
        return carry

    lax.fori_loop(0, images, unattend_image, 0)

    def last_tile(start, size):
        r = rows_at(start, size, size)
        hot = member[r, :]
        hot_t = member[r, :SLOT_LANES].astype(F32).T.astype(BF16)

        def collect(block, value):
            sg[block * SLOT_LANES : (block + 1) * SLOT_LANES, :] += dot(hot_t, value.astype(BF16))

        normed, inverse = normalize(stream[r, :])
        shift1, scale1 = spread(hot, 0, 0, 2)
        attn_in = (normed * (1.0 + scale1) + shift1).astype(BF16)
        grad_proj = proj[r, :]
        gqkv[...] += dot(attn_in.T, grad_proj)
        gshift[...] += dot(hot_t, grad_proj)
        grad_attn_in = dot(grad_proj, wqkv[...])
        collect(0, grad_attn_in)
        collect(1, grad_attn_in * normed)
        grad_in = gmid[r, :] + norm_back(grad_attn_in * (1.0 + scale1), normed, inverse)
        gemb[...] += dot(xtok[r, :].T, grad_in.astype(BF16))

    for_tiles(last_tile)
    turned = gqkv[...].T
    kept = time_own.shape[0]
    for g, (main, shift) in enumerate(((main_own, time_own), (main_other, time_other))):
        pieces = []
        for h in range(heads // 2):
            for part in range(3):
                start = part * width + g * group + h * HEAD_DIM
                to = (3 * h + part) * HEAD_DIM
                main[to : to + HEAD_DIM, :] = turned[start : start + HEAD_DIM, :].astype(main.dtype)
                pieces.append(gshift[:kept, start : start + HEAD_DIM])
        shift[...] = jnp.concatenate(pieces, 1)
    for part in range(4):
        lower = sg[part * SLOT_LANES : part * SLOT_LANES + kept, :]
        upper = sg[(4 + part) * SLOT_LANES : (4 + part) * SLOT_LANES + kept, :]
        sg_own[part] = jnp.where(core == 0, lower, upper)
        sg_other[part] = jnp.where(core == 0, upper, lower)


def call_step(tab, x_own, x_got, mods, shifts, patch, weights):
    rows_kept, channels2, length = x_own.shape
    kept = mods[0].shape[0]
    width, half_hidden = weights[4].shape
    group = width // 2
    slots = SLOT_LANES
    longest = rows_kept * length + max(SIZES) // 2
    room = (longest + TILE + 15) // 16 * 16
    vmem = pl.BlockSpec(memory_space=pltpu.VMEM)
    shape = jax.ShapeDtypeStruct
    outs = (
        shape((width, half_hidden), F32),
        shape((width, half_hidden), F32),
        shape((group, width), F32),
        shape((width * (2 * half_hidden + group) // 128, 128), BF16),
        shape((channels2, width), F32),
        shape((1, channels2), F32),
        shape((3 * group, width), F32),
        shape((3 * group, width), BF16),
        shape((kept, 3 * group), F32),
        shape((kept, 3 * group), F32),
        shape((channels2, width), F32),
        shape((4, kept, width), F32),
        shape((4, kept, width), F32),
    )
    return pl.pallas_call(
        step_kernel,
        out_shape=outs,
        in_specs=[pl.BlockSpec(memory_space=pltpu.SMEM)] + [vmem] * 16,
        out_specs=[vmem] * len(outs),
        scratch_shapes=[
            pltpu.VMEM((room, 3 * width), BF16),
            pltpu.VMEM((room, width), BF16),
            pltpu.VMEM((room, width), BF16),
            pltpu.VMEM((room, width), F32),
            pltpu.VMEM((room, width), F32),
            pltpu.VMEM((room, channels2), BF16),
            pltpu.VMEM((room // min(SIZES), 8, 2 * max(SIZES)), F32),
            pltpu.VMEM((8 * slots, width), F32),
            pltpu.VMEM((2, 2 * slots, 4 * width), BF16),
            pltpu.VMEM((3 * width, width), BF16),
            pltpu.VMEM((2 * rows_kept * length, channels2), BF16),
            pltpu.VMEM((room, 2 * slots), BF16),
            pltpu.VMEM((max(TILE, width), max(2 * half_hidden, 3 * width)), F32),
            pltpu.VMEM((TILE, 2 * half_hidden), BF16),
            pltpu.VMEM((width, half_hidden), F32),
            pltpu.VMEM((width, half_hidden), F32),
            pltpu.VMEM((width, width), F32),
            pltpu.VMEM((2 * slots, 3 * width), BF16),
            pltpu.VMEM((width, width), BF16),
            pltpu.VMEM((channels2, width), BF16),
            pltpu.VMEM((channels2, width), BF16),
            pltpu.VMEM((slots, 3 * width), F32),
        ],
        compiler_params=pltpu.CompilerParams(vmem_limit_bytes=VMEM_LIMIT),
        name="step",
    )(tab, x_own, x_got, jnp.asarray(position_rows(width)), *mods, *shifts, patch, *weights)


def signal_tables():
    betas = 0.0001 + 0.0199 * np.arange(1000) / 999.0
    level = np.exp(np.cumsum(np.log(1.0 - betas)))
    return np.pad(np.stack([np.sqrt(level), np.sqrt(1.0 - level)]), ((0, 0), (0, 24))).astype(np.float32)


def noise_kernel(counts, steps, tables, latents, noise, own, sent):
    rows_here, channels, length = latents.shape
    kept = own.shape[0]
    position = lax.broadcasted_iota(jnp.int32, (1, length), 1)
    for r in range(rows_here):
        start = jnp.int32(0)
        keep = jnp.zeros((1, length), F32)
        fade = jnp.zeros((1, length), F32)
        for k in range(counts.shape[1]):
            end = start + counts[r, k]
            inside = (position >= start) & (position < end)
            keep = jnp.where(inside, tables[0, steps[r, k]], keep)
            fade = jnp.where(inside, tables[1, steps[r, k]], fade)
            start = end
        target = own.at[r] if r < kept else sent.at[r - kept]
        target[:channels, :] = (keep * latents[r] + fade * noise[r]).astype(BF16)
        target[channels:, :] = noise[r].astype(BF16)


def call_noise(counts, steps, latents, noise):
    rows_here, channels, length = latents.shape
    smem = pl.BlockSpec(memory_space=pltpu.SMEM)
    vmem = pl.BlockSpec(memory_space=pltpu.VMEM)
    kept = rows_here // 2
    return pl.pallas_call(
        noise_kernel,
        out_shape=[jax.ShapeDtypeStruct((n, 2 * channels, length), BF16) for n in (kept, rows_here - kept)],
        in_specs=[smem, smem, smem, vmem, vmem],
        out_specs=[vmem] * 2,
        compiler_params=pltpu.CompilerParams(vmem_limit_bytes=VMEM_LIMIT),
        name="add_noise",
    )(counts, steps, jnp.asarray(signal_tables()), latents, noise)


def time_features(steps, freqs):
    half = freqs // 2
    rates = jnp.exp(-math.log(10000.0) * jnp.arange(half, dtype=F32) / half)
    angle = steps.astype(F32)[..., None] * rates
    return jnp.concatenate([jnp.cos(angle), jnp.sin(angle)], -1)


def running_sum(values):
    size = values.shape[-1]
    before = np.arange(size)[:, None] > np.arange(size)[None, :]
    return jnp.sum(jnp.where(before, values[..., None, :], 0), -1)


def image_table(counts, core, place, length):
    rows_here, slots = counts.shape
    source = running_sum(counts) + length * jnp.arange(rows_here, dtype=jnp.int32)[:, None]
    flat, source = counts.reshape(-1), source.reshape(-1)
    kinds = jnp.stack([(flat == size).astype(jnp.int32) for size in SIZES])
    ranks = running_sum(kinds)
    small, middle, large = (jnp.sum(kind) for kind in kinds)
    odd = large & 1
    ahead = SIZES[2] * odd + SIZES[1] * (middle & 1) * (1 - 2 * odd)
    extra = (ahead + SIZES[0] // 2) // SIZES[0]
    lean = (ahead > SIZES[0] * extra).astype(jnp.int32)
    owners = jnp.stack(
        [
            jnp.where(ranks[0] < extra, 1, (ranks[0] - extra + lean) & 1),
            (ranks[1] + odd) & 1,
            ranks[2] & 1,
        ]
    )
    mine = jnp.sum(jnp.where(owners == core, kinds, 0), 0)
    flat = flat * mine
    spots = running_sum(jnp.stack([flat, mine]))
    index = jnp.arange(flat.shape[0], dtype=jnp.int32)
    chosen = (spots[1][None, :] == index[:, None]) & (mine[None, :] == 1)
    columns = jnp.stack([flat, source, spots[0], index])
    listed = jnp.sum(jnp.where(chosen[None], columns[:, None, :], 0), -1)
    tokens = jnp.sum(flat)
    full = (tokens + TILE // 2 - 1) // TILE
    rest = (tokens > full * TILE).astype(jnp.int32)
    facts = jnp.stack([jnp.sum(mine), tokens, full, rest, core, place]).astype(jnp.int32)
    pad = lambda v: jnp.pad(v.astype(jnp.int32), (0, 128 - v.shape[0]))
    return jnp.stack([pad(listed[0]), pad(listed[1]), pad(listed[2]), pad(facts), pad(listed[3])])


def swap(value):
    return lax.ppermute(value, "tensor", [(0, 1), (1, 0)])


def fine_dot(left, right, dims):
    left_a, right_a = left.astype(BF16), right.astype(BF16)
    left_b = (left - left_a.astype(F32)).astype(BF16)
    right_b = (right - right_a.astype(F32)).astype(BF16)
    product = partial(lax.dot_general, dimension_numbers=(dims, ((), ())), preferred_element_type=F32)
    return product(left_a, right_a) + (product(left_a, right_b) + product(left_b, right_a))


PLAIN, TURNED = ((1,), (0,)), ((1,), (1,))


def silu_slope(value):
    gate = 1.0 / (1.0 + jnp.exp(-value))
    return gate * (1.0 + value * (1.0 - gate))


def term_kernel(shift_own, shift_got, sg_own, sg_got, cond, w_mod, w_time, term):
    width = w_mod.shape[0]
    total = jnp.zeros(cond.shape, F32)
    for part in range(4):
        grad = sg_own[part] + sg_got[part]
        total = total + fine_dot(grad, w_mod[:, part * width : (part + 1) * width], TURNED)
    term[...] = total * silu_slope(cond[...]) + fine_dot(shift_own[...] + shift_got[...], w_time[...], PLAIN)


def pack_kernel(
    n_dp, chunks, tab, up, down, out, got, main_own, main_got, shift_own, shift_got, sg_own, sg_got, cond, *refs
):
    n = len(chunks)
    keeps, gives, done, rows = refs[:n], refs[n : 2 * n], refs[2 * n], refs[2 * n + 1]
    width = cond.shape[1]
    at = 0
    for ref in (up, down, out):
        for j in range(0, ref.shape[1], 128):
            to = slice(at, at + ref.shape[0])
            rows[to, :] = ref[:, j : j + 128] + got[to, :].astype(F32)
            at = to.stop
    values = cond[...]
    act_t = (values / (1.0 + jnp.exp(-values))).T
    shift_t = (shift_own[...] + shift_got[...]).T

    def put(block):
        nonlocal at
        for j in range(0, width, 128):
            rows[at : at + block.shape[0], :] = block[:, j : j + 128]
            at += block.shape[0]

    put(main_own[...] + main_got[...].astype(F32))
    put(fine_dot(shift_t, values, PLAIN))
    for part in range(4):
        put(fine_dot(act_t, sg_own[part] + sg_got[part], PLAIN))
    rows[at:, :] = jnp.zeros((rows.shape[0] - at, 128), F32)
    done[...] = jnp.zeros(done.shape, F32)
    base = 0
    for k, chunk in enumerate(chunks):
        bit = bit_order(n_dp, k)[0]
        mine = lax.shift_right_logical(tab[3, 5], bit) & 1
        for j in range(n_dp // 2):
            owner = (j >> bit << (bit + 1)) | (j & ((1 << bit) - 1))
            first = base + owner * chunk
            keep = first + mine * (chunk << bit)
            give = first + (1 - mine) * (chunk << bit)
            keeps[k][j] = rows[pl.ds(pl.multiple_of(keep, 16), chunk), :]
            gives[k][j] = rows[pl.ds(pl.multiple_of(give, 16), chunk), :].astype(BF16)
        base += n_dp * chunk


def call_pack(n_dp, chunks, table, *args):
    vmem = pl.BlockSpec(memory_space=pltpu.VMEM)
    shapes = [jax.ShapeDtypeStruct((n_dp // 2, c, 128), kind) for kind in (F32, BF16) for c in chunks]
    shapes.append(jax.ShapeDtypeStruct((8, 128), F32))
    return pl.pallas_call(
        partial(pack_kernel, n_dp, chunks),
        out_shape=shapes,
        in_specs=[pl.BlockSpec(memory_space=pltpu.SMEM)] + [vmem] * len(args),
        out_specs=[vmem] * len(shapes),
        scratch_shapes=[pltpu.VMEM((n_dp * sum(chunks), 128), F32)],
        compiler_params=pltpu.CompilerParams(vmem_limit_bytes=VMEM_LIMIT),
        name="pack_grads",
    )(table, *args)


def time_kernel(time_chunk, extra, tab, term, got, before, features, w_time, patch, patch_got, _, rows, flat):
    width = w_time.shape[1]
    freqs = features.shape[1]
    grad_cond = term[...] + got[...]
    values = before[...]
    hidden = values / (1.0 + jnp.exp(-values))
    second = fine_dot(hidden.T, grad_cond, PLAIN)
    inner = fine_dot(grad_cond, w_time[freqs:, :], TURNED) * silu_slope(values)
    first = fine_dot(features[...].T, inner, PLAIN)
    half = w_time.shape[0] // 2
    both = jnp.concatenate([first, second], 0)
    mine = jnp.where(tab[3, 4] == 0, both[:half], both[half:])
    shared = patch[...] + patch_got[...]
    n_dp = rows.shape[0]
    flat[...] = jnp.zeros(flat.shape, F32)
    patch_at = n_dp * time_chunk
    for t in range(width // 128):
        flat[t * half : (t + 1) * half, :] = mine[:, t * 128 : (t + 1) * 128]
        to = patch_at + t * shared.shape[0]
        flat[to : to + shared.shape[0], :] = shared[:, t * 128 : (t + 1) * 128]
    for d in range(n_dp):
        rows[d, :time_chunk, :] = flat[d * time_chunk : (d + 1) * time_chunk, :]
        rows[d, time_chunk:, :] = flat[patch_at + d * extra : patch_at + (d + 1) * extra, :]


def call_time(n_dp, time_chunk, extra, table, *args):
    vmem = pl.BlockSpec(memory_space=pltpu.VMEM)
    return pl.pallas_call(
        partial(time_kernel, time_chunk, extra),
        out_shape=jax.ShapeDtypeStruct((n_dp, time_chunk + extra, 128), F32),
        in_specs=[pl.BlockSpec(memory_space=pltpu.SMEM)] + [vmem] * len(args),
        out_specs=vmem,
        scratch_shapes=[pltpu.VMEM((n_dp * (time_chunk + extra), 128), F32)],
        compiler_params=pltpu.CompilerParams(vmem_limit_bytes=VMEM_LIMIT),
        name="time_grads",
    )(table, *args)


def call_small(kernel, shape, name, *args):
    vmem = pl.BlockSpec(memory_space=pltpu.VMEM)
    return pl.pallas_call(
        kernel,
        out_shape=jax.ShapeDtypeStruct(shape, F32),
        in_specs=[vmem] * len(args),
        out_specs=vmem,
        compiler_params=pltpu.CompilerParams(vmem_limit_bytes=VMEM_LIMIT),
        name=name,
    )(*args)


def adam_values(weight, first, second, grad, factor):
    clipped = grad * factor
    first = BETA_FIRST * first + (1.0 - BETA_FIRST) * clipped
    second = BETA_SECOND * second + (1.0 - BETA_SECOND) * clipped * clipped
    fixed = jnp.maximum(second * (1.0 / (1.0 - BETA_SECOND**STEP)), 1e-37)
    root = fixed * lax.rsqrt(fixed) + ADAM_EPS
    inverse = pl.reciprocal(root, approx=True)
    inverse = inverse * (2.0 - root * inverse)
    step = first * (1.0 / (1.0 - BETA_FIRST**STEP)) * inverse
    return (first, second, weight - LEARN_RATE * (step + WEIGHT_DECAY * weight))


def adam_kernel(n_dp, lists, chunks, time_chunk, extra, place, *refs):
    n_got = sum(len(pieces) for pieces, _ in lists)
    got, refs = refs[:n_got], refs[n_got:]
    ins, outs, stats, bufs = refs[:21], refs[21:42], refs[42:45], refs[45:66]
    rows, time_rows, extra_rows, sem_in, sem_out, sem_got = refs[66:]
    width = ins[3].shape[1]
    here = place[0]
    jobs = []
    for p in range(7):
        shape = ins[3 * p].shape
        if p == 0:
            jobs.append((p, None))
        elif p == 3:
            jobs.extend((p, (i,)) for i in range(2))
        else:
            step = shape[0] // 2 if p == 1 else min(width, shape[0])
            jobs.extend(
                (p, (pl.ds(r, step), pl.ds(j, width))) for r in range(0, shape[0], step) for j in range(0, shape[1], width)
            )

    def view(ref, where):
        return ref if where is None else ref.at[where]

    arrivals = []
    base = 0
    for stream, ((pieces, order), chunk) in enumerate(zip(lists, chunks)):
        for source, relatives in zip(pieces, order):
            for j, relative in enumerate(relatives):
                owner = here ^ relative
                parts = [(0, chunk, rows, base + owner * chunk)]
                if stream == len(chunks) - 1:
                    parts.append((chunk, time_chunk, time_rows, owner * time_chunk))
                    parts.append((chunk + time_chunk, time_chunk, time_rows, (n_dp + owner) * time_chunk))
                    parts.append((chunk + 2 * time_chunk, 6 * extra, extra_rows, owner * 6 * extra))
                for start, size, target, at in parts:
                    copy = pltpu.make_async_copy(
                        got[source].at[j, pl.ds(start, size), :],
                        target.at[pl.ds(pl.multiple_of(at, 16), size), :],
                        sem_got.at[len(arrivals)],
                    )
                    copy.start()
                    arrivals.append(copy)
        base += n_dp * chunk
    loads = []
    for i, (p, where) in enumerate(jobs):
        group = []
        for k in range(3):
            copy = pltpu.make_async_copy(
                view(ins[3 * p + k], where), view(bufs[3 * p + k], where), sem_in.at[3 * i + k]
            )
            copy.start()
            group.append(copy)
        loads.append(group)
    for copy in arrivals:
        copy.wait()
    shards = []
    squares = jnp.zeros((1, 128), F32)
    for owner in range(n_dp):
        at = owner * 6 * extra
        terms = [extra_rows[at + k * 2 * extra : at + (k + 1) * 2 * extra, :].astype(F32) for k in range(3)]
        whole = terms[0] + terms[1] + terms[2]
        shards.append(whole[:extra])
        squares = squares + whole[extra : extra + 1]
    shared = jnp.concatenate(shards, 0)
    each = 2 * ins[0].shape[1] + 8
    patch = jnp.concatenate([shared[t * each : t * each + each - 8] for t in range(width // 128)], 1)
    facts = shared[each - 8 : each - 7]
    loss, count = facts[:, 0:1], facts[:, 1:2]
    squares = jnp.sum(squares, 1, keepdims=True)
    squares = squares + jnp.sum(jnp.sum(patch * patch, 1, keepdims=True), 0, keepdims=True)
    grad_norm = jnp.sqrt(squares) / count
    scale = jnp.minimum(1.0, CLIP_LIMIT / grad_norm) / count
    for stat, value in zip(stats, (loss, count, grad_norm)):
        stat[0] = jnp.sum(value)
    patch = patch.reshape(ins[0].shape)

    def tiles(at, size, count):
        return jnp.concatenate([rows[at + i * size : at + (i + 1) * size, :] for i in range(count)], 1).astype(F32)

    per_tile = width // 128
    half_time = ins[3].shape[0] // 2
    offsets = {5: 0}
    offsets[6] = ins[15].shape[0] * ins[15].shape[1] // 128
    offsets[4] = offsets[6] + ins[18].shape[0] * ins[18].shape[1] // 128
    offsets[3] = offsets[4] + ins[12].shape[0] * ins[12].shape[1] // 128
    offsets[2] = offsets[3] + 2 * ins[9].shape[1] * ins[9].shape[2] // 128
    stores = []
    for i, (p, where) in enumerate(jobs):
        for copy in loads[i]:
            copy.wait()
        if p == 0:
            grad = patch
        elif p == 1:
            top = where[0].start // half_time * n_dp * time_chunk
            grad = jnp.concatenate(
                [time_rows[top + t * half_time : top + (t + 1) * half_time, :] for t in range(per_tile)], 1
            ).astype(F32)
        elif p == 3:
            size = ins[9].shape[1]
            grad = tiles(offsets[3] + where[0] * size * per_tile, size, per_tile)
        elif p == 6:
            grad = tiles(offsets[6] + where[0].start // 128 * width, width, per_tile).T
        else:
            size = ins[3 * p].shape[0]
            grad = tiles(offsets[p] + where[1].start // 128 * size, size, per_tile)
        b = bufs[3 * p : 3 * p + 3]
        index = ... if where is None else where
        values = adam_values(b[0][index], b[1][index], b[2][index], grad, scale)
        for k, value in enumerate(values):
            b[k][index] = value
            copy = pltpu.make_async_copy(view(b[k], where), view(outs[3 * p + k], where), sem_out.at[3 * i + k])
            copy.start()
            stores.append(copy)
    for copy in stores:
        copy.wait()


def call_adam(n_dp, lists, chunks, time_chunk, extra, place, got, params):
    smem = pl.BlockSpec(memory_space=pltpu.SMEM)
    anywhere = pl.BlockSpec(memory_space=pl.ANY)
    n_jobs = 3 * 16
    return pl.pallas_call(
        partial(adam_kernel, n_dp, lists, chunks, time_chunk, extra),
        out_shape=[jax.ShapeDtypeStruct(w.shape, F32) for w in params] + [jax.ShapeDtypeStruct((1,), F32)] * 3,
        in_specs=[smem] + [anywhere] * (len(got) + len(params)),
        out_specs=[anywhere] * len(params) + [smem] * 3,
        scratch_shapes=[pltpu.VMEM(w.shape, F32) for w in params]
        + [
            pltpu.VMEM((n_dp * sum(chunks), 128), BF16),
            pltpu.VMEM((2 * n_dp * time_chunk, 128), BF16),
            pltpu.VMEM((n_dp * 6 * extra, 128), BF16),
            pltpu.SemaphoreType.DMA((n_jobs,)),
            pltpu.SemaphoreType.DMA((n_jobs,)),
            pltpu.SemaphoreType.DMA((6 * n_dp,)),
        ],
        compiler_params=pltpu.CompilerParams(vmem_limit_bytes=VMEM_LIMIT),
        name="adam",
    )(place, *got, *params)


def stage(size, bit):
    return [(i, i ^ (1 << bit)) for i in range(size)]


def bit_order(size, turn):
    bits = list(range(size.bit_length() - 1))
    lead = bits[:3]
    turn %= max(len(lead), 1)
    return lead[turn:] + lead[:turn] + bits[3:]


def halve(keeps, gives, exact, size):
    place = lax.axis_index("dp")
    orders = [bit_order(size, turn) for turn in range(len(keeps))]
    lefts = [sorted(order, reverse=True) for order in orders]
    last = len(keeps) - 1
    values = [None for _ in keeps]
    exact = exact.reshape(*(2,) * len(orders[0]), *exact.shape[1:])
    for n in range(len(orders[0])):
        for k in range(len(keeps)):
            bit = orders[k][n]
            mine = (place >> bit) & 1
            axis = lefts[k].index(bit)
            lefts[k].remove(bit)

            def halves(v):
                return (
                    lax.dynamic_index_in_dim(v, mine, axis, keepdims=False),
                    lax.dynamic_index_in_dim(v, 1 - mine, axis, keepdims=False),
                )

            if n:
                keep, give = halves(values[k])
                give = give.astype(BF16)
            else:
                keep, give = (v[k].reshape(*(2,) * len(lefts[k]), *v[k].shape[1:]) for v in (keeps, gives))
            if k == last:
                exact, sent = halves(exact)
                coarse = lax.reduce_precision(sent, 8, 7)
                give = jnp.concatenate([give, coarse.astype(BF16), (sent - coarse).astype(BF16)], -2)
            got = lax.ppermute(give, "dp", stage(size, bit)).astype(F32)
            if k == last:
                m, e = keep.shape[-2], exact.shape[-2]
                exact = exact + (got[..., m : m + e, :] + got[..., m + e :, :])
                got = got[..., :m, :]
            values[k] = keep + got
    return values, exact


def gather(values, size, turn):
    held, relatives = values[None], [0]
    pieces = []
    order = bit_order(size, turn)[::-1]
    for n, bit in enumerate(order):
        got = lax.ppermute(held, "dp", stage(size, bit))
        moved = [r ^ (1 << bit) for r in relatives]
        if n == len(order) - 1:
            pieces = [(held, relatives), (got, moved)]
        else:
            held, relatives = jnp.concatenate([held, got], 0), relatives + moved
    return pieces


def shards(
    latents, noise_field, image_tokens, timesteps,
    w_patch, m_patch, v_patch, w_time, m_time, v_time, w_mod, m_mod, v_mod,
    w_qkv, m_qkv, v_qkv, w_out, m_out, v_out, w_up, m_up, v_up, w_down, m_down, v_down,
):
    rows_here, channels, length = latents.shape
    slots = image_tokens.shape[1]
    width = w_patch.shape[2]
    freqs = w_time.shape[0] - width
    core = lax.axis_index("tensor")
    n_dp = lax.axis_size("dp")
    chip_slots = rows_here * slots
    group = w_out.shape[0]
    kept = rows_here // 2
    mirror = [(i, n_dp - 1 - i) for i in range(n_dp)]

    numbers = jnp.concatenate([image_tokens, timesteps], 1)
    numbers = jnp.concatenate([numbers[:kept], lax.ppermute(numbers[kept:], "dp", mirror)], 0)
    x_own, sent = call_noise(image_tokens, timesteps, latents, noise_field)
    x_got = lax.ppermute(sent, "dp", mirror)
    counts, steps = numbers[:, :slots], numbers[:, slots:].reshape(-1)
    tab = image_table(counts, core, lax.axis_index("dp"), length)

    qkv_t, qkv_m, qkv_v = (v.swapaxes(1, 2) for v in (w_qkv, m_qkv, v_qkv))
    halves = []
    for w in (qkv_t[0], w_out, w_up, w_down):
        w = w.astype(BF16)
        halves.extend((w, swap(w)))

    features = time_features(steps, freqs)
    before = precise(features, w_time[:freqs])
    cond = precise(jax.nn.silu(before), w_time[freqs:])
    mod_own = precise(jax.nn.silu(cond), w_mod)
    shift_own = precise(cond, qkv_t[1].T)

    up, down, out, other, gfin, loss, main_own, main_other, time_own, time_other, gemb, sg_own, sg_other = call_step(
        tab, x_own, x_got, (mod_own, swap(mod_own)), (shift_own, swap(shift_own)), w_patch, halves
    )

    patch = jnp.concatenate([gemb[:channels], gfin[channels:]], 0)
    count_here = 0.5 * channels * jnp.sum(image_tokens).astype(F32)
    facts = jnp.stack([jnp.sum(loss), count_here])
    patch = jnp.concatenate([patch, jnp.pad(facts[None], ((0, 7), (0, width - 2)))], 0)
    slot_grads = (time_own, swap(time_other), sg_own, swap(sg_other))
    term = call_small(term_kernel, cond.shape, "cond_term", *slot_grads, cond, w_mod, qkv_t[1])

    def share(count, multiple):
        return (count + n_dp * multiple - 1) // (n_dp * multiple) * multiple

    time_chunk = share(w_time.shape[0] // 2 * width // 128, 16)
    extra = share(patch.size // 128, 8)
    wide = share(other.shape[0] + (2 * 3 * group + 4 * width) * width // 128, 1)
    most = (wide + 2 * (time_chunk + extra) + 47) // 48 * 16
    chunks = (most, most, max(wide - 2 * most + 15, 16) // 16 * 16)
    packed = call_pack(
        n_dp, chunks, tab, up, down, out, swap(other), main_own, swap(main_other), *slot_grads, cond
    )
    g_time = call_time(
        n_dp, time_chunk, extra, tab, term, swap(term), before, features, w_time, patch, swap(patch), packed[-1]
    )

    parts, exact_part = halve(packed[:3], packed[3:6], g_time, n_dp)
    time_part, patch_part = exact_part[:time_chunk], exact_part[time_chunk:]
    squares = sum(jnp.sum(v * v) for v in (*parts, time_part))
    mine = jnp.concatenate([time_part, jnp.full((8, 128), squares, F32)], 0)
    theirs = swap(mine)
    first = core == 0
    both_time = [jnp.where(first, mine, theirs)[:time_chunk], jnp.where(first, theirs, mine)[:time_chunk]]
    lane = jnp.arange(128)[None]
    spot = (jnp.arange(extra)[:, None] == 0) & (lane == 0)
    total = jnp.where(spot, mine[time_chunk, 0] + theirs[time_chunk, 0], 0.0)
    terms, rest = [], jnp.concatenate([patch_part, total], 0)
    for _ in range(3):
        coarse = lax.reduce_precision(rest, 8, 7)
        terms.append(coarse.astype(BF16))
        rest = rest - coarse
    sent = [v.astype(BF16) for v in parts]
    sent[-1] = jnp.concatenate([sent[-1], *(v.astype(BF16) for v in both_time), *terms], 0)
    got, lists = [], []
    for k in range(3):
        pieces = gather(sent[k], n_dp, k)
        lists.append(([len(got) + i for i in range(len(pieces))], [r for _, r in pieces]))
        got.extend(v for v, _ in pieces)
    params = (
        w_patch, m_patch, v_patch, w_time, m_time, v_time, w_mod, m_mod, v_mod,
        qkv_t, qkv_m, qkv_v, w_out, m_out, v_out, w_up, m_up, v_up, w_down, m_down, v_down,
    )
    *updated, loss_sum, count, grad_norm = call_adam(
        n_dp, lists, chunks, time_chunk, extra, lax.axis_index("dp").reshape(1), got, params
    )
    for k in range(9, 12):
        updated[k] = updated[k].swapaxes(1, 2)
    return (loss_sum.reshape(()), count.reshape(()), grad_norm.reshape(()), *updated)


def solution(mesh):
    rows, flat, cols = P("dp", None, None), P("dp", None), P(None, "tensor")
    whole, deep, split = P(), P(None, None, "tensor"), P("tensor", None)
    weights = [p for p in (whole, whole, cols, deep, split, cols, split) for _ in range(3)]
    return jax.shard_map(
        shards,
        mesh=mesh,
        in_specs=(rows, rows, flat, flat, *weights),
        out_specs=(whole, whole, whole, *weights),
        check_vma=False,
    )
```

```python
from functools import partial
import math

import jax
import jax.numpy as jnp
import numpy as np
from jax import lax
from jax.experimental import pallas as pl
from jax.experimental.pallas import tpu as pltpu
from jax.sharding import PartitionSpec as P

HEAD_DIM = 64
STEP = 10
PRECISE_MODE = lax.Precision.HIGHEST
NORM_EPS = 1e-06
CLIP_LIMIT = 0.001
LEARN_RATE = 0.03
BETA_FIRST = 0.9
BETA_SECOND = 0.95
ADAM_EPS = 1e-08
WEIGHT_DECAY = 0.1
SIZES = (64, 144, 256)
TILE = 256
SLOT_LANES = 128
GELU_A = math.sqrt(2.0 / math.pi)
GELU_B = 0.044715
VMEM_LIMIT = 60 * 1024 * 1024
F32 = jnp.float32
BF16 = jnp.bfloat16


def precise(left, right):
    return jnp.dot(left, right, precision=PRECISE_MODE)


def dot(left, right):
    return lax.dot_general(left, right, (((1,), (0,)), ((), ())), preferred_element_type=F32)


def dot_nt(left, right):
    return lax.dot_general(left, right, (((1,), (1,)), ((), ())), preferred_element_type=F32)


def normalize(values):
    centre = values - jnp.mean(values, -1, keepdims=True)
    inverse = lax.rsqrt(jnp.mean(centre * centre, -1, keepdims=True) + NORM_EPS)
    return (centre * inverse, inverse)


def norm_back(grad, normed, inverse):
    return inverse * (
        grad
        - jnp.mean(grad, -1, keepdims=True)
        - normed * jnp.mean(grad * normed, -1, keepdims=True)
    )


def position_rows(width):
    quarter = width // 4
    omega = np.exp(-math.log(10000.0) * np.arange(quarter) / quarter)
    parts = []
    for size in SIZES:
        side = math.isqrt(size)
        offset = np.arange(size)
        row_angle = (offset // side)[:, None] * omega
        col_angle = (offset % side)[:, None] * omega
        parts.append(
            np.concatenate(
                [np.sin(row_angle), np.cos(row_angle), np.sin(col_angle), np.cos(col_angle)], -1
            )
        )
    return np.concatenate(parts, 0).astype(np.float32)


def for_sizes(count, body):
    offset = 0
    for size in SIZES:
        pl.when(count == size)(partial(body, size, offset))
        offset += size


def rows_at(start, size, step):
    return pl.ds(pl.multiple_of(start, step), size)


def fill_member(member, dst, size, index):
    lane = lax.broadcasted_iota(jnp.int32, (size, 2 * SLOT_LANES), 1)
    hot = (lane == index) | (lane == index + SLOT_LANES)
    member[rows_at(dst, size, 16), :] = hot.astype(F32).astype(BF16)


def both_heads(pair):
    first = lax.broadcasted_iota(jnp.int32, pair.shape, 1) < HEAD_DIM
    nothing = jnp.zeros_like(pair)
    return jnp.concatenate([jnp.where(first, pair, nothing), jnp.where(first, nothing, pair)], 0)


def own_lanes(rows):
    size = rows.shape[0] // 2
    first = lax.broadcasted_iota(jnp.int32, (size, rows.shape[1]), 1) < HEAD_DIM
    return jnp.where(first, rows[:size], rows[size:])


def step_kernel(
    tab, x_own, x_got, places, mod_own, mod_got, shift_own, shift_got, patch,
    qkv_own, qkv_got, out_own, out_got, up_own, up_got, dn_own, dn_got,
    up_kept, down_kept, out_kept, other, gfin, loss, main_own, main_other, time_own, time_other, gemb, sg_own, sg_other,
    proj, mixed, gmixed, gmid, stream, xtok, lse, sg, modcat, wqkv,
    xrow, member, deriv, active, up_sent, down_sent, gout, shiftcat, wout, w_in, w_fin, gshift,
):
    width = stream.shape[1]
    gqkv = deriv.at[:, : 3 * width]
    images, tokens, full, rest, core = (tab[3, j] for j in range(5))
    heads = width // HEAD_DIM
    group_heads = heads // 2
    group = width // 2
    half_hidden = up_own.shape[1]
    hidden = 2 * half_hidden
    channels = patch.shape[1]
    chip_slots = mod_own.shape[0]
    at = 0
    for x in (x_own, x_got):
        for r in range(x.shape[0]):
            turned = x[r].astype(F32).T
            xrow[at : at + turned.shape[0], :] = turned.astype(BF16)
            at += turned.shape[0]
    for g, source in enumerate((qkv_own, qkv_got)):
        for h in range(group_heads):
            for part in range(3):
                to = part * width + g * group + h * HEAD_DIM
                start = (3 * h + part) * HEAD_DIM
                wqkv[to : to + HEAD_DIM, :] = source[start : start + HEAD_DIM, :]
    wout[:group, :] = out_own[...]
    wout[group:, :] = out_got[...]
    nothing = jnp.zeros((channels, width), BF16)
    w_in[:channels, :] = patch[0].astype(BF16)
    w_in[channels:, :] = nothing
    w_fin[:channels, :] = nothing
    w_fin[channels:, :] = patch[1].astype(BF16)

    def two_terms(target, values):
        coarse = values.astype(BF16)
        rest = jnp.zeros((SLOT_LANES - chip_slots, values.shape[1]), BF16)
        for base, term in ((0, coarse), (SLOT_LANES, (values - coarse.astype(F32)).astype(BF16))):
            target[base : base + chip_slots, :] = term
            target[base + chip_slots : base + SLOT_LANES, :] = rest

    for half in range(2):
        two_terms(modcat.at[half], jnp.where(core == half, mod_own[...], mod_got[...]))
    two_terms(
        shiftcat,
        jnp.concatenate(
            [
                source[:, (3 * h + part) * HEAD_DIM : (3 * h + part + 1) * HEAD_DIM]
                for part in range(3)
                for source in (shift_own, shift_got)
                for h in range(group_heads)
            ],
            1,
        ),
    )
    parts = (
        (0, up_own, dn_own, up_kept, down_kept),
        (half_hidden, up_got, dn_got, up_sent, down_sent),
    )

    def place_image(i, carry):
        src, dst = tab[1, i], tab[2, i]

        def body(size, offset):
            xtok[rows_at(dst, size, 16), :] = xrow[rows_at(src, size, 16), :]
            stream[rows_at(dst, size, 16), :] = places[offset : offset + size, :]
            fill_member(member, dst, size, tab[4, i])

        for_sizes(tab[0, i], body)
        return carry

    lax.fori_loop(0, images, place_image, 0)
    tail = rows_at(tokens, TILE, 16)
    for ref in (xtok, stream, member, mixed):
        ref[tail, :] = jnp.zeros((TILE, ref.shape[1]), ref.dtype)
    for ref in (up_kept, down_kept, up_sent, down_sent, gout, gfin, sg, loss, gshift, gemb):
        ref[...] = jnp.zeros(ref.shape, ref.dtype)

    def spread(hot, half, start, count):
        wide = dot(hot, modcat[half, :, start * width : (start + count) * width])
        return [wide[:, k * width : (k + 1) * width] for k in range(count)]

    def for_tiles(body):
        def whole(t, carry):
            body(t * TILE, TILE)
            return carry

        lax.fori_loop(0, full, whole, 0)
        pl.when(rest == 1)(partial(body, full * TILE, TILE // 2))

    def project_tile(start, size):
        r = rows_at(start, size, size)
        entering = dot(xtok[r, :], w_in[...]) + stream[r, :]
        stream[r, :] = entering
        hot = member[r, :]
        normed, _ = normalize(entering)
        shift1, scale1 = spread(hot, 0, 0, 2)
        attn_in = (normed * (1.0 + scale1) + shift1).astype(BF16)
        proj[r, :] = (dot_nt(attn_in, wqkv[...]) + dot(hot, shiftcat[...])).astype(BF16)

    for_tiles(project_tile)

    def attend_image(i, carry):
        dst = tab[2, i]

        def body(size, offset):
            r = rows_at(dst, size, 16)
            pairs = range(heads // 2)
            ones = jnp.ones((16, size), BF16)
            scores, weights = [], []
            for p in pairs:
                key = proj[r, width + 128 * p : width + 128 * p + 128]
                scores.append(dot_nt(key, both_heads(proj[r, 128 * p : 128 * p + 128])))
            tops = [jnp.max(v, 0, keepdims=True) for v in scores]
            weights = [jnp.exp((v - top) * HEAD_DIM ** (-0.5)) for v, top in zip(scores, tops)]
            for p in pairs:
                value_t = proj[r, 2 * width + 128 * p : 2 * width + 128 * p + 128].T
                out = dot(jnp.concatenate([value_t, ones], 0), weights[p].astype(BF16))
                total = out[128:129]
                lse[i, p : p + 1, : 2 * size] = tops[p] * HEAD_DIM ** (-0.5) + jnp.log(total)
                mixed[r, 128 * p : 128 * p + 128] = own_lanes((out[:128] / total).T).astype(BF16)

        for_sizes(tab[0, i], body)
        return carry

    lax.fori_loop(0, images, attend_image, 0)

    def token_tile(start, size):
        r = rows_at(start, size, size)
        hot = member[r, :]
        hot_t = member[r, :SLOT_LANES].astype(F32).T.astype(BF16)

        def collect(block, value):
            sg[block * SLOT_LANES : (block + 1) * SLOT_LANES, :] += dot(hot_t, value.astype(BF16))

        mixed_tile = mixed[r, :]
        attended = dot(mixed_tile, wout[...])
        gate1, shift2 = spread(hot, 0, 2, 2)
        scale2, gate2, shift3, scale3 = spread(hot, 1, 0, 4)
        mid = stream[r, :] + gate1 * attended
        normed2, inverse2 = normalize(mid)
        mlp_in = (normed2 * (1.0 + scale2) + shift2).astype(BF16)
        mlp_out = jnp.zeros((size, width), F32)
        for j, wup, wdn, _, _ in parts:
            up = dot(mlp_in, wup[...])
            square = up * up
            bent = jnp.tanh(up * (GELU_A + (GELU_A * GELU_B) * square))
            share = 0.5 + 0.5 * bent
            act = (up * share).astype(BF16)
            active[:size, j : j + half_hidden] = act
            deriv[:size, j : j + half_hidden] = share + up * (share * (1.0 - share)) * (
                2.0 * GELU_A + (6.0 * GELU_A * GELU_B) * square
            )
            mlp_out = mlp_out + dot(act, wdn[...])
        leaving = mid + gate2 * mlp_out
        normed3, inverse3 = normalize(leaving)
        final_in = (normed3 * (1.0 + scale3) + shift3).astype(BF16)
        predicted = dot_nt(final_in, w_fin[...])
        lane = lax.broadcasted_iota(jnp.int32, predicted.shape, 1)
        row = lax.broadcasted_iota(jnp.int32, predicted.shape, 0) + start
        keep = (lane >= channels) & (row < tokens)
        error = jnp.where(keep, predicted - xtok[r, :].astype(F32), 0.0)
        loss[...] += jnp.sum(error * error, 0, keepdims=True)
        grad_pred = (2.0 * error).astype(BF16)
        gfin[...] += dot(grad_pred.T, final_in)
        grad_final = dot(grad_pred, w_fin[...])
        collect(6, grad_final)
        collect(7, grad_final * normed3)
        grad_out = norm_back(grad_final * (1.0 + scale3), normed3, inverse3)
        collect(5, grad_out * mlp_out)
        grad_mlp = (grad_out * gate2).astype(BF16)
        grad_mlp_t = grad_mlp.T
        mlp_in_t = mlp_in.T
        grad_mlp_in = jnp.zeros((size, width), F32)
        for j, wup, wdn, gup, gdn in parts:
            gdn[...] += dot(grad_mlp_t, active[:size, j : j + half_hidden])
            grad_act = dot_nt(grad_mlp, wdn[...])
            grad_up = (grad_act * deriv[:size, j : j + half_hidden]).astype(BF16)
            gup[...] += dot(mlp_in_t, grad_up)
            grad_mlp_in = grad_mlp_in + dot_nt(grad_up, wup[...])
        collect(3, grad_mlp_in)
        collect(4, grad_mlp_in * normed2)
        grad_mid = grad_out + norm_back(grad_mlp_in * (1.0 + scale2), normed2, inverse2)
        gmid[r, :] = grad_mid
        collect(2, grad_mid * attended)
        grad_attended = (grad_mid * gate1).astype(BF16)
        gout[...] += dot(mixed_tile.T, grad_attended)
        gmixed[r, :] = dot_nt(grad_attended, wout[...]).astype(BF16)

    for_tiles(token_tile)
    gqkv[...] = jnp.zeros(gqkv.shape, F32)
    out_kept[...] = gout[:group, :]
    at = 0
    for ref in (up_sent, down_sent):
        for j in range(0, half_hidden, 128):
            other[at : at + width, :] = ref[:, j : j + 128].astype(BF16)
            at += width
    for j in range(0, width, 128):
        other[at : at + group, :] = gout[group:, j : j + 128].astype(BF16)
        at += group
    every = jnp.ones((8, 2 * HEAD_DIM), BF16)

    def unattend_image(i, carry):
        dst = tab[2, i]

        def body(size, offset):
            r = rows_at(dst, size, 16)
            pairs = range(heads // 2)
            grads = [both_heads(gmixed[r, 128 * p : 128 * p + 128]) for p in pairs]
            queries = [both_heads(proj[r, 128 * p : 128 * p + 128]) for p in pairs]
            inners, probs, drops = [], [], []
            for p in pairs:
                out = mixed[r, 128 * p : 128 * p + 128].astype(F32)
                product = grads[p].astype(F32) * jnp.concatenate([out, out], 0)
                coarse = product.astype(BF16)
                fine = (product - coarse.astype(F32)).astype(BF16)
                inners.append((dot_nt(every, coarse) + dot_nt(every, fine))[0:1])
            for p in pairs:
                scores = dot_nt(proj[r, width + 128 * p : width + 128 * p + 128], queries[p])
                probs.append(jnp.exp(scores * HEAD_DIM ** (-0.5) - lse[i, p : p + 1, : 2 * size]))
            for p in pairs:
                grad_probs = dot_nt(proj[r, 2 * width + 128 * p : 2 * width + 128 * p + 128], grads[p])
                drops.append((probs[p] * (grad_probs - inners[p])).astype(BF16))
            for p in pairs:
                key_t = proj[r, width + 128 * p : width + 128 * p + 128].T
                grad_value = dot(probs[p].astype(BF16), grads[p])
                grad_key = dot(drops[p], queries[p]) * HEAD_DIM ** (-0.5)
                grad_query = own_lanes(dot(key_t, drops[p]).T) * HEAD_DIM ** (-0.5)
                for part, value in enumerate((grad_query, grad_key, grad_value)):
                    at = part * width + 128 * p
                    proj[r, at : at + 128] = value.astype(BF16)

        for_sizes(tab[0, i], body)
        return carry

    lax.fori_loop(0, images, unattend_image, 0)

    def last_tile(start, size):
        r = rows_at(start, size, size)
        hot = member[r, :]
        hot_t = member[r, :SLOT_LANES].astype(F32).T.astype(BF16)

        def collect(block, value):
            sg[block * SLOT_LANES : (block + 1) * SLOT_LANES, :] += dot(hot_t, value.astype(BF16))

        normed, inverse = normalize(stream[r, :])
        shift1, scale1 = spread(hot, 0, 0, 2)
        attn_in = (normed * (1.0 + scale1) + shift1).astype(BF16)
        grad_proj = proj[r, :]
        gqkv[...] += dot(attn_in.T, grad_proj)
        gshift[...] += dot(hot_t, grad_proj)
        grad_attn_in = dot(grad_proj, wqkv[...])
        collect(0, grad_attn_in)
        collect(1, grad_attn_in * normed)
        grad_in = gmid[r, :] + norm_back(grad_attn_in * (1.0 + scale1), normed, inverse)
        gemb[...] += dot(xtok[r, :].T, grad_in.astype(BF16))

    for_tiles(last_tile)
    turned = gqkv[...].T
    kept = time_own.shape[0]
    for g, (main, shift) in enumerate(((main_own, time_own), (main_other, time_other))):
        pieces = []
        for h in range(heads // 2):
            for part in range(3):
                start = part * width + g * group + h * HEAD_DIM
                to = (3 * h + part) * HEAD_DIM
                main[to : to + HEAD_DIM, :] = turned[start : start + HEAD_DIM, :].astype(main.dtype)
                pieces.append(gshift[:kept, start : start + HEAD_DIM])
        shift[...] = jnp.concatenate(pieces, 1)
    for part in range(4):
        lower = sg[part * SLOT_LANES : part * SLOT_LANES + kept, :]
        upper = sg[(4 + part) * SLOT_LANES : (4 + part) * SLOT_LANES + kept, :]
        sg_own[part] = jnp.where(core == 0, lower, upper)
        sg_other[part] = jnp.where(core == 0, upper, lower)


def call_step(tab, x_own, x_got, mods, shifts, patch, weights):
    rows_kept, channels2, length = x_own.shape
    kept = mods[0].shape[0]
    width, half_hidden = weights[4].shape
    group = width // 2
    slots = SLOT_LANES
    longest = rows_kept * length + max(SIZES) // 2
    room = (longest + TILE + 15) // 16 * 16
    vmem = pl.BlockSpec(memory_space=pltpu.VMEM)
    shape = jax.ShapeDtypeStruct
    outs = (
        shape((width, half_hidden), F32),
        shape((width, half_hidden), F32),
        shape((group, width), F32),
        shape((width * (2 * half_hidden + group) // 128, 128), BF16),
        shape((channels2, width), F32),
        shape((1, channels2), F32),
        shape((3 * group, width), F32),
        shape((3 * group, width), BF16),
        shape((kept, 3 * group), F32),
        shape((kept, 3 * group), F32),
        shape((channels2, width), F32),
        shape((4, kept, width), F32),
        shape((4, kept, width), F32),
    )
    return pl.pallas_call(
        step_kernel,
        out_shape=outs,
        in_specs=[pl.BlockSpec(memory_space=pltpu.SMEM)] + [vmem] * 16,
        out_specs=[vmem] * len(outs),
        scratch_shapes=[
            pltpu.VMEM((room, 3 * width), BF16),
            pltpu.VMEM((room, width), BF16),
            pltpu.VMEM((room, width), BF16),
            pltpu.VMEM((room, width), F32),
            pltpu.VMEM((room, width), F32),
            pltpu.VMEM((room, channels2), BF16),
            pltpu.VMEM((room // min(SIZES), 8, 2 * max(SIZES)), F32),
            pltpu.VMEM((8 * slots, width), F32),
            pltpu.VMEM((2, 2 * slots, 4 * width), BF16),
            pltpu.VMEM((3 * width, width), BF16),
            pltpu.VMEM((2 * rows_kept * length, channels2), BF16),
            pltpu.VMEM((room, 2 * slots), BF16),
            pltpu.VMEM((max(TILE, width), max(2 * half_hidden, 3 * width)), F32),
            pltpu.VMEM((TILE, 2 * half_hidden), BF16),
            pltpu.VMEM((width, half_hidden), F32),
            pltpu.VMEM((width, half_hidden), F32),
            pltpu.VMEM((width, width), F32),
            pltpu.VMEM((2 * slots, 3 * width), BF16),
            pltpu.VMEM((width, width), BF16),
            pltpu.VMEM((channels2, width), BF16),
            pltpu.VMEM((channels2, width), BF16),
            pltpu.VMEM((slots, 3 * width), F32),
        ],
        compiler_params=pltpu.CompilerParams(vmem_limit_bytes=VMEM_LIMIT),
        name="step",
    )(tab, x_own, x_got, jnp.asarray(position_rows(width)), *mods, *shifts, patch, *weights)


def signal_tables():
    betas = 0.0001 + 0.0199 * np.arange(1000) / 999.0
    level = np.exp(np.cumsum(np.log(1.0 - betas)))
    return np.pad(np.stack([np.sqrt(level), np.sqrt(1.0 - level)]), ((0, 0), (0, 24))).astype(np.float32)


def start_kernel(counts, steps, tables, latents, noise, qkv, out, up, down, own, sent, qkv_b, out_b, up_b, down_b):
    qkv_b[...] = qkv[0].astype(BF16)
    for full, low in ((out, out_b), (up, up_b), (down, down_b)):
        low[...] = full[...].astype(BF16)
    rows_here, channels, length = latents.shape
    kept = own.shape[0]
    position = lax.broadcasted_iota(jnp.int32, (1, length), 1)
    for r in range(rows_here):
        start = jnp.int32(0)
        keep = jnp.zeros((1, length), F32)
        fade = jnp.zeros((1, length), F32)
        for k in range(counts.shape[1]):
            end = start + counts[r, k]
            inside = (position >= start) & (position < end)
            keep = jnp.where(inside, tables[0, steps[r, k]], keep)
            fade = jnp.where(inside, tables[1, steps[r, k]], fade)
            start = end
        target = own.at[r] if r < kept else sent.at[r - kept]
        target[:channels, :] = (keep * latents[r] + fade * noise[r]).astype(BF16)
        target[channels:, :] = noise[r].astype(BF16)


def call_start(counts, steps, latents, noise, *weights):
    rows_here, channels, length = latents.shape
    smem = pl.BlockSpec(memory_space=pltpu.SMEM)
    vmem = pl.BlockSpec(memory_space=pltpu.VMEM)
    kept = rows_here // 2
    shapes = [(n, 2 * channels, length) for n in (kept, rows_here - kept)]
    shapes += [weights[0].shape[1:]] + [w.shape for w in weights[1:]]
    return pl.pallas_call(
        start_kernel,
        out_shape=[jax.ShapeDtypeStruct(shape, BF16) for shape in shapes],
        in_specs=[smem] * 3 + [vmem] * 6,
        out_specs=[vmem] * len(shapes),
        compiler_params=pltpu.CompilerParams(vmem_limit_bytes=VMEM_LIMIT),
        name="start",
    )(counts, steps, jnp.asarray(signal_tables()), latents, noise, *weights)


def time_features(steps, freqs):
    half = freqs // 2
    rates = jnp.exp(-math.log(10000.0) * jnp.arange(half, dtype=F32) / half)
    angle = steps.astype(F32)[..., None] * rates
    return jnp.concatenate([jnp.cos(angle), jnp.sin(angle)], -1)


def running_sum(values):
    size = values.shape[-1]
    before = np.arange(size)[:, None] > np.arange(size)[None, :]
    return jnp.sum(jnp.where(before, values[..., None, :], 0), -1)


def image_table(counts, core, place, length):
    rows_here, slots = counts.shape
    source = running_sum(counts) + length * jnp.arange(rows_here, dtype=jnp.int32)[:, None]
    flat, source = counts.reshape(-1), source.reshape(-1)
    kinds = jnp.stack([(flat == size).astype(jnp.int32) for size in SIZES])
    ranks = running_sum(kinds)
    small, middle, large = (jnp.sum(kind) for kind in kinds)
    odd = large & 1
    ahead = SIZES[2] * odd + SIZES[1] * (middle & 1) * (1 - 2 * odd)
    extra = (ahead + SIZES[0] // 2) // SIZES[0]
    lean = (ahead > SIZES[0] * extra).astype(jnp.int32)
    owners = jnp.stack(
        [
            jnp.where(ranks[0] < extra, 1, (ranks[0] - extra + lean) & 1),
            (ranks[1] + odd) & 1,
            ranks[2] & 1,
        ]
    )
    mine = jnp.sum(jnp.where(owners == core, kinds, 0), 0)
    flat = flat * mine
    spots = running_sum(jnp.stack([flat, mine]))
    index = jnp.arange(flat.shape[0], dtype=jnp.int32)
    chosen = (spots[1][None, :] == index[:, None]) & (mine[None, :] == 1)
    columns = jnp.stack([flat, source, spots[0], index])
    listed = jnp.sum(jnp.where(chosen[None], columns[:, None, :], 0), -1)
    tokens = jnp.sum(flat)
    full = (tokens + TILE // 2 - 1) // TILE
    rest = (tokens > full * TILE).astype(jnp.int32)
    facts = jnp.stack([jnp.sum(mine), tokens, full, rest, core, place]).astype(jnp.int32)
    pad = lambda v: jnp.pad(v.astype(jnp.int32), (0, 128 - v.shape[0]))
    return jnp.stack([pad(listed[0]), pad(listed[1]), pad(listed[2]), pad(facts), pad(listed[3])])


def swap(value):
    return lax.ppermute(value, "tensor", [(0, 1), (1, 0)])


def fine_dot(left, right, dims):
    left_a, right_a = left.astype(BF16), right.astype(BF16)
    left_b = (left - left_a.astype(F32)).astype(BF16)
    right_b = (right - right_a.astype(F32)).astype(BF16)
    product = partial(lax.dot_general, dimension_numbers=(dims, ((), ())), preferred_element_type=F32)
    return product(left_a, right_a) + (product(left_a, right_b) + product(left_b, right_a))


PLAIN, TURNED = ((1,), (0,)), ((1,), (1,))


def silu_slope(value):
    gate = 1.0 / (1.0 + jnp.exp(-value))
    return gate * (1.0 + value * (1.0 - gate))


def term_kernel(shift_own, shift_got, sg_own, sg_got, cond, w_mod, w_time, term):
    width = w_mod.shape[0]
    total = jnp.zeros(cond.shape, F32)
    for part in range(4):
        grad = sg_own[part] + sg_got[part]
        total = total + fine_dot(grad, w_mod[:, part * width : (part + 1) * width], TURNED)
    term[...] = total * silu_slope(cond[...]) + fine_dot(shift_own[...] + shift_got[...], w_time[...], PLAIN)


def pack_kernel(
    n_dp, chunks, tab, up, down, out, got, main_own, main_got, shift_own, shift_got, sg_own, sg_got, cond, *refs
):
    n = len(chunks)
    keeps, gives, done, rows = refs[:n], refs[n : 2 * n], refs[2 * n], refs[2 * n + 1]
    width = cond.shape[1]
    at = 0
    for ref in (up, down, out):
        for j in range(0, ref.shape[1], 128):
            to = slice(at, at + ref.shape[0])
            rows[to, :] = ref[:, j : j + 128] + got[to, :].astype(F32)
            at = to.stop
    values = cond[...]
    act_t = (values / (1.0 + jnp.exp(-values))).T
    shift_t = (shift_own[...] + shift_got[...]).T

    def put(block):
        nonlocal at
        for j in range(0, width, 128):
            rows[at : at + block.shape[0], :] = block[:, j : j + 128]
            at += block.shape[0]

    put(main_own[...] + main_got[...].astype(F32))
    put(fine_dot(shift_t, values, PLAIN))
    for part in range(4):
        put(fine_dot(act_t, sg_own[part] + sg_got[part], PLAIN))
    rows[at:, :] = jnp.zeros((rows.shape[0] - at, 128), F32)
    done[...] = jnp.zeros(done.shape, F32)
    base = 0
    for k, chunk in enumerate(chunks):
        bit = bit_order(n_dp, k)[0]
        mine = lax.shift_right_logical(tab[3, 5], bit) & 1
        for j in range(n_dp // 2):
            owner = (j >> bit << (bit + 1)) | (j & ((1 << bit) - 1))
            first = base + owner * chunk
            keep = first + mine * (chunk << bit)
            give = first + (1 - mine) * (chunk << bit)
            keeps[k][j] = rows[pl.ds(pl.multiple_of(keep, 16), chunk), :]
            gives[k][j] = rows[pl.ds(pl.multiple_of(give, 16), chunk), :].astype(BF16)
        base += n_dp * chunk


def call_pack(n_dp, chunks, table, *args):
    vmem = pl.BlockSpec(memory_space=pltpu.VMEM)
    shapes = [jax.ShapeDtypeStruct((n_dp // 2, c, 128), kind) for kind in (F32, BF16) for c in chunks]
    shapes.append(jax.ShapeDtypeStruct((8, 128), F32))
    return pl.pallas_call(
        partial(pack_kernel, n_dp, chunks),
        out_shape=shapes,
        in_specs=[pl.BlockSpec(memory_space=pltpu.SMEM)] + [vmem] * len(args),
        out_specs=[vmem] * len(shapes),
        scratch_shapes=[pltpu.VMEM((n_dp * sum(chunks), 128), F32)],
        compiler_params=pltpu.CompilerParams(vmem_limit_bytes=VMEM_LIMIT),
        name="pack_grads",
    )(table, *args)


def time_kernel(time_chunk, extra, tab, term, got, before, features, w_time, patch, patch_got, _, rows, flat):
    width = w_time.shape[1]
    freqs = features.shape[1]
    grad_cond = term[...] + got[...]
    values = before[...]
    hidden = values / (1.0 + jnp.exp(-values))
    second = fine_dot(hidden.T, grad_cond, PLAIN)
    inner = fine_dot(grad_cond, w_time[freqs:, :], TURNED) * silu_slope(values)
    first = fine_dot(features[...].T, inner, PLAIN)
    half = w_time.shape[0] // 2
    both = jnp.concatenate([first, second], 0)
    mine = jnp.where(tab[3, 4] == 0, both[:half], both[half:])
    shared = patch[...] + patch_got[...]
    n_dp = rows.shape[0]
    flat[...] = jnp.zeros(flat.shape, F32)
    patch_at = n_dp * time_chunk
    for t in range(width // 128):
        flat[t * half : (t + 1) * half, :] = mine[:, t * 128 : (t + 1) * 128]
        to = patch_at + t * shared.shape[0]
        flat[to : to + shared.shape[0], :] = shared[:, t * 128 : (t + 1) * 128]
    for d in range(n_dp):
        rows[d, :time_chunk, :] = flat[d * time_chunk : (d + 1) * time_chunk, :]
        rows[d, time_chunk:, :] = flat[patch_at + d * extra : patch_at + (d + 1) * extra, :]


def call_time(n_dp, time_chunk, extra, table, *args):
    vmem = pl.BlockSpec(memory_space=pltpu.VMEM)
    return pl.pallas_call(
        partial(time_kernel, time_chunk, extra),
        out_shape=jax.ShapeDtypeStruct((n_dp, time_chunk + extra, 128), F32),
        in_specs=[pl.BlockSpec(memory_space=pltpu.SMEM)] + [vmem] * len(args),
        out_specs=vmem,
        scratch_shapes=[pltpu.VMEM((n_dp * (time_chunk + extra), 128), F32)],
        compiler_params=pltpu.CompilerParams(vmem_limit_bytes=VMEM_LIMIT),
        name="time_grads",
    )(table, *args)


def call_small(kernel, shape, name, *args):
    vmem = pl.BlockSpec(memory_space=pltpu.VMEM)
    return pl.pallas_call(
        kernel,
        out_shape=jax.ShapeDtypeStruct(shape, F32),
        in_specs=[vmem] * len(args),
        out_specs=vmem,
        compiler_params=pltpu.CompilerParams(vmem_limit_bytes=VMEM_LIMIT),
        name=name,
    )(*args)


def adam_values(weight, first, second, grad, factor):
    clipped = grad * factor
    first = BETA_FIRST * first + (1.0 - BETA_FIRST) * clipped
    second = BETA_SECOND * second + (1.0 - BETA_SECOND) * clipped * clipped
    fixed = jnp.maximum(second * (1.0 / (1.0 - BETA_SECOND**STEP)), 1e-37)
    root = fixed * lax.rsqrt(fixed) + ADAM_EPS
    inverse = pl.reciprocal(root, approx=True)
    inverse = inverse * (2.0 - root * inverse)
    step = first * (1.0 / (1.0 - BETA_FIRST**STEP)) * inverse
    return (first, second, weight - LEARN_RATE * (step + WEIGHT_DECAY * weight))


def adam_kernel(n_dp, lists, chunks, time_chunk, extra, place, *refs):
    n_got = sum(len(pieces) for pieces, _ in lists)
    got, refs = refs[:n_got], refs[n_got:]
    ins, outs, stats, bufs = refs[:21], refs[21:42], refs[42:45], refs[45:66]
    rows, time_rows, extra_rows, sem_in, sem_out, sem_got = refs[66:]
    width = ins[3].shape[1]
    here = place[0]
    jobs = []
    for p in range(7):
        shape = ins[3 * p].shape
        if p == 0:
            jobs.append((p, None))
        elif p == 3:
            jobs.extend((p, (i,)) for i in range(2))
        else:
            step = shape[0] // 2 if p == 1 else min(width, shape[0])
            jobs.extend(
                (p, (pl.ds(r, step), pl.ds(j, width))) for r in range(0, shape[0], step) for j in range(0, shape[1], width)
            )

    def view(ref, where):
        return ref if where is None else ref.at[where]

    arrivals = []
    base = 0
    for stream, ((pieces, order), chunk) in enumerate(zip(lists, chunks)):
        for source, relatives in zip(pieces, order):
            for j, relative in enumerate(relatives):
                owner = here ^ relative
                parts = [(0, chunk, rows, base + owner * chunk)]
                if stream == len(chunks) - 1:
                    parts.append((chunk, time_chunk, time_rows, owner * time_chunk))
                    parts.append((chunk + time_chunk, time_chunk, time_rows, (n_dp + owner) * time_chunk))
                    parts.append((chunk + 2 * time_chunk, 6 * extra, extra_rows, owner * 6 * extra))
                for start, size, target, at in parts:
                    copy = pltpu.make_async_copy(
                        got[source].at[j, pl.ds(start, size), :],
                        target.at[pl.ds(pl.multiple_of(at, 16), size), :],
                        sem_got.at[len(arrivals)],
                    )
                    copy.start()
                    arrivals.append(copy)
        base += n_dp * chunk
    loads = []
    for i, (p, where) in enumerate(jobs):
        group = []
        for k in range(3):
            copy = pltpu.make_async_copy(
                view(ins[3 * p + k], where), view(bufs[3 * p + k], where), sem_in.at[3 * i + k]
            )
            copy.start()
            group.append(copy)
        loads.append(group)
    for copy in arrivals:
        copy.wait()
    shards = []
    squares = jnp.zeros((1, 128), F32)
    for owner in range(n_dp):
        at = owner * 6 * extra
        terms = [extra_rows[at + k * 2 * extra : at + (k + 1) * 2 * extra, :].astype(F32) for k in range(3)]
        whole = terms[0] + terms[1] + terms[2]
        shards.append(whole[:extra])
        squares = squares + whole[extra : extra + 1]
    shared = jnp.concatenate(shards, 0)
    each = 2 * ins[0].shape[1] + 8
    patch = jnp.concatenate([shared[t * each : t * each + each - 8] for t in range(width // 128)], 1)
    facts = shared[each - 8 : each - 7]
    loss, count = facts[:, 0:1], facts[:, 1:2]
    squares = jnp.sum(squares, 1, keepdims=True)
    squares = squares + jnp.sum(jnp.sum(patch * patch, 1, keepdims=True), 0, keepdims=True)
    grad_norm = jnp.sqrt(squares) / count
    scale = jnp.minimum(1.0, CLIP_LIMIT / grad_norm) / count
    for stat, value in zip(stats, (loss, count, grad_norm)):
        stat[0] = jnp.sum(value)
    patch = patch.reshape(ins[0].shape)

    def tiles(at, size, count):
        return jnp.concatenate([rows[at + i * size : at + (i + 1) * size, :] for i in range(count)], 1).astype(F32)

    per_tile = width // 128
    half_time = ins[3].shape[0] // 2
    offsets = {5: 0}
    offsets[6] = ins[15].shape[0] * ins[15].shape[1] // 128
    offsets[4] = offsets[6] + ins[18].shape[0] * ins[18].shape[1] // 128
    offsets[3] = offsets[4] + ins[12].shape[0] * ins[12].shape[1] // 128
    offsets[2] = offsets[3] + 2 * ins[9].shape[1] * ins[9].shape[2] // 128
    stores = []
    for i, (p, where) in enumerate(jobs):
        for copy in loads[i]:
            copy.wait()
        if p == 0:
            grad = patch
        elif p == 1:
            top = where[0].start // half_time * n_dp * time_chunk
            grad = jnp.concatenate(
                [time_rows[top + t * half_time : top + (t + 1) * half_time, :] for t in range(per_tile)], 1
            ).astype(F32)
        elif p == 3:
            size = ins[9].shape[1]
            grad = tiles(offsets[3] + where[0] * size * per_tile, size, per_tile)
        elif p == 6:
            grad = tiles(offsets[6] + where[0].start // 128 * width, width, per_tile).T
        else:
            size = ins[3 * p].shape[0]
            grad = tiles(offsets[p] + where[1].start // 128 * size, size, per_tile)
        b = bufs[3 * p : 3 * p + 3]
        index = ... if where is None else where
        values = adam_values(b[0][index], b[1][index], b[2][index], grad, scale)
        for k, value in enumerate(values):
            b[k][index] = value
            copy = pltpu.make_async_copy(view(b[k], where), view(outs[3 * p + k], where), sem_out.at[3 * i + k])
            copy.start()
            stores.append(copy)
    for copy in stores:
        copy.wait()


def call_adam(n_dp, lists, chunks, time_chunk, extra, place, got, params):
    smem = pl.BlockSpec(memory_space=pltpu.SMEM)
    anywhere = pl.BlockSpec(memory_space=pl.ANY)
    n_jobs = 3 * 16
    return pl.pallas_call(
        partial(adam_kernel, n_dp, lists, chunks, time_chunk, extra),
        out_shape=[jax.ShapeDtypeStruct(w.shape, F32) for w in params] + [jax.ShapeDtypeStruct((1,), F32)] * 3,
        in_specs=[smem] + [anywhere] * (len(got) + len(params)),
        out_specs=[anywhere] * len(params) + [smem] * 3,
        scratch_shapes=[pltpu.VMEM(w.shape, F32) for w in params]
        + [
            pltpu.VMEM((n_dp * sum(chunks), 128), BF16),
            pltpu.VMEM((2 * n_dp * time_chunk, 128), BF16),
            pltpu.VMEM((n_dp * 6 * extra, 128), BF16),
            pltpu.SemaphoreType.DMA((n_jobs,)),
            pltpu.SemaphoreType.DMA((n_jobs,)),
            pltpu.SemaphoreType.DMA((6 * n_dp,)),
        ],
        compiler_params=pltpu.CompilerParams(vmem_limit_bytes=VMEM_LIMIT),
        name="adam",
    )(place, *got, *params)


def stage(size, bit):
    return [(i, i ^ (1 << bit)) for i in range(size)]


def bit_order(size, turn):
    bits = list(range(size.bit_length() - 1))
    lead = bits[:3]
    turn %= max(len(lead), 1)
    return lead[turn:] + lead[:turn] + bits[3:]


def halve(keeps, gives, exact, size):
    place = lax.axis_index("dp")
    orders = [bit_order(size, turn) for turn in range(len(keeps))]
    lefts = [sorted(order, reverse=True) for order in orders]
    last = len(keeps) - 1
    values = [None for _ in keeps]
    exact = exact.reshape(*(2,) * len(orders[0]), *exact.shape[1:])
    for n in range(len(orders[0])):
        for k in range(len(keeps)):
            bit = orders[k][n]
            mine = (place >> bit) & 1
            axis = lefts[k].index(bit)
            lefts[k].remove(bit)

            def halves(v):
                return (
                    lax.dynamic_index_in_dim(v, mine, axis, keepdims=False),
                    lax.dynamic_index_in_dim(v, 1 - mine, axis, keepdims=False),
                )

            if n:
                keep, give = halves(values[k])
                give = give.astype(BF16)
            else:
                keep, give = (v[k].reshape(*(2,) * len(lefts[k]), *v[k].shape[1:]) for v in (keeps, gives))
            if k == last:
                exact, sent = halves(exact)
                coarse = lax.reduce_precision(sent, 8, 7)
                give = jnp.concatenate([give, coarse.astype(BF16), (sent - coarse).astype(BF16)], -2)
            got = lax.ppermute(give, "dp", stage(size, bit)).astype(F32)
            if k == last:
                m, e = keep.shape[-2], exact.shape[-2]
                exact = exact + (got[..., m : m + e, :] + got[..., m + e :, :])
                got = got[..., :m, :]
            values[k] = keep + got
    return values, exact


def gather(values, size, turn):
    held, relatives = values[None], [0]
    pieces = []
    order = bit_order(size, turn)[::-1]
    for n, bit in enumerate(order):
        got = lax.ppermute(held, "dp", stage(size, bit))
        moved = [r ^ (1 << bit) for r in relatives]
        if n == len(order) - 1:
            pieces = [(held, relatives), (got, moved)]
        else:
            held, relatives = jnp.concatenate([held, got], 0), relatives + moved
    return pieces


def shards(
    latents, noise_field, image_tokens, timesteps,
    w_patch, m_patch, v_patch, w_time, m_time, v_time, w_mod, m_mod, v_mod,
    w_qkv, m_qkv, v_qkv, w_out, m_out, v_out, w_up, m_up, v_up, w_down, m_down, v_down,
):
    rows_here, channels, length = latents.shape
    slots = image_tokens.shape[1]
    width = w_patch.shape[2]
    freqs = w_time.shape[0] - width
    core = lax.axis_index("tensor")
    n_dp = lax.axis_size("dp")
    chip_slots = rows_here * slots
    group = w_out.shape[0]
    kept = rows_here // 2
    mirror = [(i, n_dp - 1 - i) for i in range(n_dp)]

    numbers = jnp.concatenate([image_tokens, timesteps], 1)
    numbers = jnp.concatenate([numbers[:kept], lax.ppermute(numbers[kept:], "dp", mirror)], 0)
    qkv_t, qkv_m, qkv_v = (v.swapaxes(1, 2) for v in (w_qkv, m_qkv, v_qkv))
    x_own, sent, *mains = call_start(image_tokens, timesteps, latents, noise_field, qkv_t, w_out, w_up, w_down)
    x_got = lax.ppermute(sent, "dp", mirror)
    counts, steps = numbers[:, :slots], numbers[:, slots:].reshape(-1)
    tab = image_table(counts, core, lax.axis_index("dp"), length)

    halves = []
    for w in mains:
        halves.extend((w, swap(w)))

    features = time_features(steps, freqs)
    before = precise(features, w_time[:freqs])
    cond = precise(jax.nn.silu(before), w_time[freqs:])
    mod_own = precise(jax.nn.silu(cond), w_mod)
    shift_own = precise(cond, qkv_t[1].T)

    up, down, out, other, gfin, loss, main_own, main_other, time_own, time_other, gemb, sg_own, sg_other = call_step(
        tab, x_own, x_got, (mod_own, swap(mod_own)), (shift_own, swap(shift_own)), w_patch, halves
    )

    patch = jnp.concatenate([gemb[:channels], gfin[channels:]], 0)
    count_here = 0.5 * channels * jnp.sum(image_tokens).astype(F32)
    facts = jnp.stack([jnp.sum(loss), count_here])
    patch = jnp.concatenate([patch, jnp.pad(facts[None], ((0, 7), (0, width - 2)))], 0)
    slot_grads = (time_own, swap(time_other), sg_own, swap(sg_other))
    term = call_small(term_kernel, cond.shape, "cond_term", *slot_grads, cond, w_mod, qkv_t[1])

    def share(count, multiple):
        return (count + n_dp * multiple - 1) // (n_dp * multiple) * multiple

    time_chunk = share(w_time.shape[0] // 2 * width // 128, 16)
    extra = share(patch.size // 128, 8)
    wide = share(other.shape[0] + (2 * 3 * group + 4 * width) * width // 128, 1)
    most = (wide + 2 * (time_chunk + extra) + 47) // 48 * 16
    chunks = (most, most, max(wide - 2 * most + 15, 16) // 16 * 16)
    packed = call_pack(
        n_dp, chunks, tab, up, down, out, swap(other), main_own, swap(main_other), *slot_grads, cond
    )
    g_time = call_time(
        n_dp, time_chunk, extra, tab, term, swap(term), before, features, w_time, patch, swap(patch), packed[-1]
    )

    parts, exact_part = halve(packed[:3], packed[3:6], g_time, n_dp)
    time_part, patch_part = exact_part[:time_chunk], exact_part[time_chunk:]
    squares = sum(jnp.sum(v * v) for v in (*parts, time_part))
    mine = jnp.concatenate([time_part, jnp.full((8, 128), squares, F32)], 0)
    theirs = swap(mine)
    first = core == 0
    both_time = [jnp.where(first, mine, theirs)[:time_chunk], jnp.where(first, theirs, mine)[:time_chunk]]
    lane = jnp.arange(128)[None]
    spot = (jnp.arange(extra)[:, None] == 0) & (lane == 0)
    total = jnp.where(spot, mine[time_chunk, 0] + theirs[time_chunk, 0], 0.0)
    terms, rest = [], jnp.concatenate([patch_part, total], 0)
    for _ in range(3):
        coarse = lax.reduce_precision(rest, 8, 7)
        terms.append(coarse.astype(BF16))
        rest = rest - coarse
    sent = [v.astype(BF16) for v in parts]
    sent[-1] = jnp.concatenate([sent[-1], *(v.astype(BF16) for v in both_time), *terms], 0)
    got, lists = [], []
    for k in range(3):
        pieces = gather(sent[k], n_dp, k)
        lists.append(([len(got) + i for i in range(len(pieces))], [r for _, r in pieces]))
        got.extend(v for v, _ in pieces)
    params = (
        w_patch, m_patch, v_patch, w_time, m_time, v_time, w_mod, m_mod, v_mod,
        qkv_t, qkv_m, qkv_v, w_out, m_out, v_out, w_up, m_up, v_up, w_down, m_down, v_down,
    )
    *updated, loss_sum, count, grad_norm = call_adam(
        n_dp, lists, chunks, time_chunk, extra, lax.axis_index("dp").reshape(1), got, params
    )
    for k in range(9, 12):
        updated[k] = updated[k].swapaxes(1, 2)
    return (loss_sum.reshape(()), count.reshape(()), grad_norm.reshape(()), *updated)


def solution(mesh):
    rows, flat, cols = P("dp", None, None), P("dp", None), P(None, "tensor")
    whole, deep, split = P(), P(None, None, "tensor"), P("tensor", None)
    weights = [p for p in (whole, whole, cols, deep, split, cols, split) for _ in range(3)]
    return jax.shard_map(
        shards,
        mesh=mesh,
        in_specs=(rows, rows, flat, flat, *weights),
        out_specs=(whole, whole, whole, *weights),
        check_vma=False,
    )
```
